32 devices in a mesh: section: 2 (over x), dp: 16 (over z, y, core).
Axes of the slice: x: 2, y: 2, z: 4, core: 2. Of those that a mesh axis runs over, the one named last changes fastest.
Arguments:
- embeds: bfloat16 [2, 32, 1024, 512], P('section', 'dp'), may hold values from -6 to 6
- cotangent: bfloat16 [2, 32, 1024, 512], P('section', 'dp'), may hold values from -6 to 6
- pair_ids: int32 [32], P('dp'), may hold values from 0 to 15
- seq_lengths: int32 [2, 32], P(None, 'dp'), may hold values from 512 to 1024, as said below
- alive_count: int32 [16], P('dp'), may hold values from 1 to 2, as said below
- self_proj: bfloat16 [2, 3, 512, 512], P('section'), may hold values from -0.25 to 0.25
- self_out: bfloat16 [2, 512, 512], P('section'), may hold values from -2 to 2
- self_bias: float32 [2, 3, 512], P('section'), may hold values from -1.75 to 1.75
- ffn_in: bfloat16 [2, 512, 2048], P('section'), may hold values from -0.25 to 0.25
- ffn_in_bias: float32 [2, 2048], P('section'), may hold values from -1.75 to 1.75
- ffn_out: bfloat16 [2, 2048, 512], P('section'), may hold values from -0.125 to 0.125
- ffn_out_bias: float32 [2, 512], P('section'), may hold values from -1.75 to 1.75
- norm_gain: float32 [2, 2, 512], P('section'), may hold values from 0.5 to 1.5
- norm_bias: float32 [2, 2, 512], P('section'), may hold values from -1.75 to 1.75
- cross_proj: bfloat16 [3, 512, 512], replicated, may hold values from -0.25 to 0.25
- cross_out: bfloat16 [512, 512], replicated, may hold values from -2 to 2
- cross_bias: float32 [3, 512], replicated, may hold values from -1.75 to 1.75
- cross_norm_gain: float32 [512], replicated, may hold values from 0.5 to 1.5
- cross_norm_bias: float32 [512], replicated, may hold values from -1.75 to 1.75
- pair_embed: float32 [16, 512], replicated, may hold values from -3 to 3
Outputs:
- layer_out: bfloat16 [2, 32, 1024, 512], P('section', 'dp')
- embeds_grad: float32 [2, 32, 1024, 512], P('section', 'dp')
- self_proj_grad: float32 [2, 3, 512, 512], P('section')
- self_out_grad: float32 [2, 512, 512], P('section')
- self_bias_grad: float32 [2, 3, 512], P('section')
- ffn_in_grad: float32 [2, 512, 2048], P('section')
- ffn_in_bias_grad: float32 [2, 2048], P('section')
- ffn_out_grad: float32 [2, 2048, 512], P('section')
- ffn_out_bias_grad: float32 [2, 512], P('section')
- norm_gain_grad: float32 [2, 2, 512], P('section')
- norm_bias_grad: float32 [2, 2, 512], P('section')
- cross_proj_grad: float32 [3, 512, 512], replicated
- cross_out_grad: float32 [512, 512], replicated
- cross_bias_grad: float32 [3, 512], replicated
- cross_norm_gain_grad: float32 [512], replicated
- cross_norm_bias_grad: float32 [512], replicated
- pair_embed_grad: float32 [16, 512], replicated
The draws below stay inside these ranges and needn't reach their ends.
Inputs may be any that keep to these rules, and one draw needn't show every extreme that they name: `seq_lengths`: in each row some sequence has exactly 1024 tokens. `alive_count`: sequence slots of a device at or past its count are padding; some device is full.
All inputs are finite; a program needn't handle non-finite values.
Results may differ from the reference program's by a relative error of at most 0.014.
Values may be sent and summed in bfloat16 or wider, within the bound.
A program may use at most 320 MiB of HBM per device.

```python
import jax
import jax.numpy as jnp
from jax import lax

D = 512
HEADS = 8
FF = 2048
L = 1024
SEQ_DEV = 2
SEQS = 32
PAIRS = 16


def draw_seq_lengths(key, part):
    key = jax.random.fold_in(key, 11)
    lengths = jax.random.randint(key, (2, SEQS), max(L // 2, 1), L + 1)
    chosen = jax.random.randint(jax.random.fold_in(key, 1), (2, 1), 0, SEQS)
    marked = jnp.arange(SEQS)[None, :] == chosen
    return jnp.where(marked, L, lengths).astype(jnp.int32)


def draw_alive_count(key, part):
    key = jax.random.fold_in(key, 12)
    devices = SEQS // SEQ_DEV
    counts = jax.random.randint(key, (devices,), 1, SEQ_DEV + 1)
    chosen = jax.random.randint(jax.random.fold_in(key, 1), (), 0, devices)
    return jnp.where(jnp.arange(devices) == chosen, SEQ_DEV, counts).astype(jnp.int32)


def set_ends(entries, own_key, least, largest):
    longest = entries.shape.index(max(entries.shape))
    spots = []
    for shift in (0, 1):
        where = [jax.random.randint(jax.random.fold_in(own_key, axis), (), 0, length) for axis, length in enumerate(entries.shape)]
        where[longest] = (where[longest] + shift) % entries.shape[longest]
        spots.append(tuple(where))
    return entries.at[spots[0]].set(least).at[spots[1]].set(largest)


def steps_of(own_key, dims, split, least, largest):
    level, own = 1.0, jax.random.fold_in(own_key, 6)
    for position, shards_of in split:
        draws = jnp.exp(jax.random.uniform(jax.random.fold_in(own, position), (shards_of,), jnp.float32, least / len(split), largest / len(split)))
        level = level * jnp.repeat(draws, dims[position] // shards_of).reshape([-1 if axis == position else 1 for axis in range(len(dims))])
    return level


def scatter_about(key, shape, deviation, limit, pieces=(), kind=jnp.bfloat16):
    values = deviation * jax.random.normal(key, shape, jnp.float32)
    if pieces:
        values = values * steps_of(key, shape, pieces, -0.22, 0.18)
    return jnp.clip(values, -limit, limit).astype(kind)


def setup_inputs(seed: int = 0) -> dict:
    seeds = jax.random.split(jax.random.key(seed), 21)
    return {
        "embeds": scatter_about(seeds[0], (2, SEQS, L, D), 1.0, 6.0, ((0, 2), (1, 16))),
        "cotangent": scatter_about(seeds[1], (2, SEQS, L, D), 1.0, 6.0, ((0, 2), (1, 16))),
        "pair_ids": set_ends(jax.random.randint(seeds[2], (SEQS,), 0, PAIRS), jax.random.fold_in(seeds[2], 1), 0, PAIRS - 1).astype(jnp.int32),
        "seq_lengths": draw_seq_lengths(jax.random.fold_in(seeds[20], 71), 0),
        "alive_count": draw_alive_count(jax.random.fold_in(seeds[20], 71), 0),
        "self_proj": scatter_about(seeds[5], (2, 3, D, D), D ** -0.5, 0.25, ((0, 2),)),
        "self_out": scatter_about(seeds[6], (2, D, D), (D * 16 // L) ** -0.5, 2.0, ((0, 2),)),
        "self_bias": scatter_about(seeds[7], (2, 3, D), 0.3, 1.75, ((0, 2),), jnp.float32),
        "ffn_in": scatter_about(seeds[8], (2, D, FF), D ** -0.5, 0.25, ((0, 2),)),
        "ffn_in_bias": scatter_about(seeds[9], (2, FF), 0.3, 1.75, ((0, 2),), jnp.float32),
        "ffn_out": scatter_about(seeds[10], (2, FF, D), FF ** -0.5, 0.125, ((0, 2),)),
        "ffn_out_bias": scatter_about(seeds[11], (2, D), 0.3, 1.75, ((0, 2),), jnp.float32),
        "norm_gain": jnp.clip(1.0 + 0.1 * jax.random.normal(seeds[12], (2, 2, D), jnp.float32), 0.5, 1.5),
        "norm_bias": scatter_about(seeds[13], (2, 2, D), 0.3, 1.75, ((0, 2),), jnp.float32),
        "cross_proj": scatter_about(seeds[14], (3, D, D), D ** -0.5, 0.25),
        "cross_out": scatter_about(seeds[15], (D, D), (D * 16 // L) ** -0.5, 2.0),
        "cross_bias": scatter_about(seeds[16], (3, D), 0.3, 1.75, (), jnp.float32),
        "cross_norm_gain": jnp.clip(1.0 + 0.1 * jax.random.normal(seeds[17], (D,), jnp.float32), 0.5, 1.5),
        "cross_norm_bias": scatter_about(seeds[18], (D,), 0.3, 1.75, (), jnp.float32),
        "pair_embed": scatter_about(seeds[19], (PAIRS, D), 0.5, 3.0, (), jnp.float32),
    }


EPSILON = 1e-05
MASKED = -1000000000.0

@jax.custom_vjp
def low(v):
    return lax.optimization_barrier(v.astype(jnp.bfloat16)).astype(jnp.float32)

@jax.custom_vjp
def low_back(v):
    return v

def low_keep(v):
    return (low(v), None)

def low_pass(kept, grad):
    return (grad,)

def back_keep(v):
    return (v, None)

def back_low(kept, grad):
    return (low(grad),)
low.defvjp(low_keep, low_pass)
low_back.defvjp(back_keep, back_low)

def matmul(left, right):
    return jnp.dot(left, right, precision=lax.Precision.HIGHEST)

def round_both(value):
    return low(low_back(value))

def layer_norm(value, gain, offset):
    centre = lax.optimization_barrier(jnp.mean(value, -1, keepdims=True))
    centred = value - centre
    spread = lax.optimization_barrier(jnp.mean(centred * centred, -1, keepdims=True))
    return centred * lax.rsqrt(spread + EPSILON) * gain + offset

def split_heads(value):
    return value.reshape(value.shape[0], HEADS, value.shape[1] // HEADS)

def attend(queries, key_rows, values, out_w, out_b, allowed):
    scaling = (queries.shape[1] // HEADS) ** (-0.5)
    scores = jnp.einsum('qhd,khd->hqk', split_heads(queries), split_heads(key_rows), precision=lax.Precision.HIGHEST)
    scores = low_back(scores * scaling)
    scores = jnp.where(allowed[None], scores, MASKED)
    attn_probs = low(jax.nn.softmax(scores, axis=-1))
    mixed_rows = jnp.einsum('hqk,khd->qhd', attn_probs, split_heads(values), precision=lax.Precision.HIGHEST)
    mixed_rows = mixed_rows.reshape(queries.shape[0], values.shape[1])
    return low_back(matmul(round_both(mixed_rows), out_w) + out_b)

def self_part(inputs, projection, bias_rows, out_w, allowed):
    inputs_low = low(inputs)
    queries = round_both(matmul(inputs_low, projection[0]) + bias_rows[0])
    key_rows = round_both(matmul(inputs_low, projection[1]))
    values = round_both(matmul(inputs_low, projection[2]) + bias_rows[1])
    return attend(queries, key_rows, values, out_w, bias_rows[2], allowed)

def feed_forward(inputs, w_in, b_in, w_out, b_out):
    hidden = low_back(matmul(low(inputs), w_in) + b_in)
    activated = low(jax.nn.gelu(hidden, approximate=False))
    return low_back(matmul(activated, w_out) + b_out)

def encode(embedded, length, layer):
    projection, out_w, bias_rows, w_in, b_in, w_out, b_out, gain_rows, offsets = layer
    row_count = embedded.shape[0]
    positions = jnp.arange(row_count)
    allowed = jnp.broadcast_to(positions[None, :] < length, (row_count, row_count))
    first_out = layer_norm(embedded + self_part(embedded, projection, bias_rows, out_w, allowed), gain_rows[0], offsets[0])
    return layer_norm(first_out + feed_forward(first_out, w_in, b_in, w_out, b_out) + embedded, gain_rows[1], offsets[1])

def decode(targets, memory_low, src_len, tgt_len, layer, cross_set):
    projection, out_w, bias_rows, w_in, b_in, w_out, b_out, gain_rows, offsets = layer
    c_proj, c_out, c_bias, c_gain, c_offset = cross_set
    row_count = targets.shape[0]
    positions = jnp.arange(row_count)
    self_ok = (positions[None, :] <= positions[:, None]) & (positions[None, :] < tgt_len)
    cross_ok = jnp.broadcast_to(positions[None, :] < src_len, (row_count, row_count))
    first_out = layer_norm(targets + self_part(targets, projection, bias_rows, out_w, self_ok), gain_rows[0], offsets[0])
    queries = round_both(matmul(low(first_out), c_proj[0]) + c_bias[0])
    key_rows = round_both(matmul(memory_low, c_proj[1]))
    values = round_both(matmul(memory_low, c_proj[2]) + c_bias[1])
    second = layer_norm(first_out + attend(queries, key_rows, values, c_out, c_bias[2], cross_ok), c_gain, c_offset)
    return layer_norm(second + feed_forward(second, w_in, b_in, w_out, b_out) + targets, gain_rows[1], offsets[1])

def forward(embeds, pair_embed, section_set, cross_set, pair_ids, seq_lengths, alive_count):
    encoder_layer = jax.tree.map(lambda weight: weight[0], section_set)
    decoder_layer = jax.tree.map(lambda weight: weight[1], section_set)

    def encode_one(packed):
        return encode(packed[0], packed[1], encoder_layer)

    def decode_one(packed):
        return decode(packed[0], packed[1], packed[2], packed[3], decoder_layer, cross_set)
    memory = lax.map(jax.checkpoint(encode_one), (embeds[0], seq_lengths[0]))
    memory_low = round_both(memory)
    targets = embeds[1] + pair_embed[pair_ids][:, None, :]
    decoded = lax.map(jax.checkpoint(decode_one), (targets, memory_low, seq_lengths[0], seq_lengths[1]))
    sequence = jnp.arange(SEQS)
    slot_live = sequence % SEQ_DEV < alive_count[sequence // SEQ_DEV]
    positions = jnp.arange(L)
    valid_src = ((positions[None, :] < seq_lengths[0][:, None]) & slot_live[:, None]).astype(jnp.float32)[:, :, None]
    valid_tgt = ((positions[None, :] < seq_lengths[1][:, None]) & slot_live[:, None]).astype(jnp.float32)[:, :, None]
    return jnp.stack([memory * valid_src, decoded * valid_tgt])

def widen(value):
    return value.astype(jnp.float32)

def reference(embeds, cotangent, pair_ids, seq_lengths, alive_count, self_proj, self_out, self_bias, ffn_in, ffn_in_bias, ffn_out, ffn_out_bias, norm_gain, norm_bias, cross_proj, cross_out, cross_bias, cross_norm_gain, cross_norm_bias, pair_embed):
    section_set = (widen(self_proj), widen(self_out), widen(self_bias), widen(ffn_in), widen(ffn_in_bias), widen(ffn_out), widen(ffn_out_bias), widen(norm_gain), widen(norm_bias))
    cross_set = (widen(cross_proj), widen(cross_out), widen(cross_bias), widen(cross_norm_gain), widen(cross_norm_bias))

    def run_layers(embedded, table, section_part, cross_part):
        return forward(embedded, table, section_part, cross_part, pair_ids, seq_lengths, alive_count)
    outputs, puller = jax.vjp(run_layers, widen(embeds), widen(pair_embed), section_set, cross_set)
    grad_embeds, grad_table, grad_section, grad_cross = puller(widen(cotangent))
    return (outputs.astype(jnp.bfloat16), grad_embeds, grad_section[0], grad_section[1], grad_section[2], grad_section[3], grad_section[4], grad_section[5], grad_section[6], grad_section[7], grad_section[8], grad_cross[0], grad_cross[1], grad_cross[2], grad_cross[3], grad_cross[4], grad_table)
```

```python
import jax
import jax.numpy as jnp
import numpy as np
from jax import lax
from jax.experimental import pallas as pl
from jax.experimental.pallas import tpu as pltpu
from jax.sharding import PartitionSpec as P

BF = jnp.bfloat16
F32 = jnp.float32
HEADS = 8
EPSILON = 1e-05
BLOCKED = -1e30
RB = 256
NN = (((1,), (0,)), ((), ()))
NT = (((1,), (1,)), ((), ()))
TN = (((0,), (0,)), ((), ()))


def dot(left, right, dims=NN):
    return lax.dot_general(left, right, dims, preferred_element_type=F32)


def row_block(index, size=RB):
    return pl.ds(pl.multiple_of(index * size, size), size)


def loop(count, body):
    def step(index, carry):
        body(index)
        return carry

    lax.fori_loop(0, count, step, 0)


def lanes_of(half):
    lane = lax.broadcasted_iota(jnp.int32, (1, 128), 1)
    inside = (lane // 64) == half
    spare = lane - 64 * (1 - half)
    ones = (~inside) & (spare < 32)
    block = (~inside) & (spare >= 32)
    flag = (~inside) & (spare == 32)
    return tuple(m.astype(F32) for m in (inside, ones, block, flag))


def norm_rows(value):
    centre = jnp.mean(value, -1, keepdims=True)
    centred = value - centre
    rstd = lax.rsqrt(jnp.mean(centred * centred, -1, keepdims=True) + EPSILON)
    return centred * rstd, rstd


def norm_rows_back(normed, rstd, gain, grad):
    scaled = grad * gain
    return rstd * (
        scaled
        - jnp.mean(scaled, -1, keepdims=True)
        - normed * jnp.mean(scaled * normed, -1, keepdims=True)
    )


def gelu_both(hidden):
    size = jnp.abs(hidden)
    t = pl.reciprocal(1.0 + (0.3275911 * 0.7071067811865476) * size)
    bell = jnp.exp(-0.5 * hidden * hidden)
    half = t * (
        0.127414796
        + t * (-0.142248368 + t * (0.7107068705 + t * (-0.7265760135 + t * 0.5307027145)))
    )
    half = half * bell
    phi = jnp.where(hidden < 0, half, 1.0 - half)
    return hidden * phi, phi + hidden * (bell * 0.3989422804014327)


def key_fill(count, length, ones, block):
    position = lax.broadcasted_iota(jnp.int32, (count, 128), 0)
    return ones + jnp.where(position < length, 0.0, BLOCKED) * block


def causal_cut(scores, query_axis):
    query = lax.broadcasted_iota(jnp.int32, scores.shape, query_axis)
    key = lax.broadcasted_iota(jnp.int32, scores.shape, 1 - query_axis)
    return jnp.where(key <= query, scores, BLOCKED)


def mix_forward(queries, keys, values_t, length, causal, mixed_t, lse):
    count = queries.shape[0]
    span = keys.shape[0]
    size = 256 if causal else min(512, count)

    def pair(index):
        cols = row_block(index, 128)
        q = queries[:, cols].astype(F32) * 0.125
        k = keys[:, cols].astype(F32)
        vt = values_t[cols, :]
        lane = lax.broadcasted_iota(jnp.int32, (128, 1), 0)
        qa, ka, va = [], [], []
        for half in range(2):
            inside, ones, block, flag = lanes_of(half)
            qa.append((q * inside + flag).astype(BF))
            ka.append((k * inside + key_fill(span, length, ones, block)).astype(BF))
            va.append(jnp.where((lane // 64) == half, vt.astype(F32), 1.0).astype(BF))
        for part in range(count // size):
            here = slice(part * size, (part + 1) * size)
            for half in range(2):
                if causal:
                    pieces = [(0, part * size, False), (part * size, size, True)]
                else:
                    pieces = [(0, span, False)]
                pieces = [piece for piece in pieces if piece[1]]
                scores = []
                for start, length_k, cut in pieces:
                    s = dot(ka[half][start : start + length_k], qa[half][here], NT)
                    scores.append(causal_cut(s, 1) if cut else s)
                top = jnp.max(scores[0], axis=0, keepdims=True)
                for s in scores[1:]:
                    top = jnp.maximum(top, jnp.max(s, axis=0, keepdims=True))
                total = None
                for (start, length_k, _), s in zip(pieces, scores):
                    probs = jnp.exp(s - top).astype(BF)
                    o = dot(va[half][:, start : start + length_k], probs)
                    total = o if total is None else total + o
                other = 64 * (1 - half)
                mass = total[other : other + 1]
                own = total[64 * half : 64 * half + 64] / mass
                mixed_t[pl.ds(pl.multiple_of(index * 128 + 64 * half, 64), 64), here] = own.astype(BF)
                lse[index * 2 + half, :, here] = top + jnp.log(mass)

    loop(4, pair)


def split3(value):
    high = value.astype(BF).astype(F32)
    middle = (value - high).astype(BF).astype(F32)
    low = (value - high - middle).astype(BF).astype(F32)
    return high, middle, low


def place_matrix():
    out = np.zeros((16, 512), np.float32)
    for half in range(2):
        other = 64 * (1 - half)
        for piece in range(3):
            out[half * 4 + piece, half * 128 + other + piece] = 1
            out[8 + half * 4 + piece, 256 + half * 128 + other + piece] = 1
        out[half * 4 + 3, half * 128 + other + 32] = 1
    return out


def mix_back(queries, keys, values, mixed_t, lse, grad_mixed, place, length, causal, d_q, d_k, d_v):
    count = queries.shape[0]
    span = keys.shape[0]
    size = 256 if causal else min(512, count)

    def pair(index):
        cols = row_block(index, 128)
        q = queries[:, cols].astype(F32) * 0.125
        k_low = keys[:, cols]
        k = k_low.astype(F32)
        v = values[:, cols].astype(F32)
        g_low = grad_mixed[:, cols]
        g = g_low.astype(F32)
        q_t = q.astype(BF).T
        g_t = g_low.T
        product = g_t.astype(F32) * mixed_t[cols, :].astype(F32)
        row = lax.broadcasted_iota(jnp.int32, (16, count), 0)
        spread = jnp.where((row == 3) | (row == 7), 1.0, 0.0)
        for half in range(2):
            shift = -lse[index * 2 + half]
            delta = -jnp.sum(product[64 * half : 64 * half + 64], axis=0, keepdims=True)
            for base, value in ((0, shift), (8, delta)):
                for piece, part in enumerate(split3(value)):
                    spread = jnp.where(row == base + 4 * half + piece, part, spread)
        extra = dot(spread.astype(BF), place[...], TN)
        qa, ka, va, ga = [], [], [], []
        for half in range(2):
            inside, ones, block, flag = lanes_of(half)
            qa.append((q * inside + extra[:, half * 128 : half * 128 + 128]).astype(BF))
            ga.append((g * inside + extra[:, 256 + half * 128 : 384 + half * 128]).astype(BF))
            ka.append((k * inside + key_fill(span, length, ones, block)).astype(BF))
            va.append((v * inside + (1.0 - inside)).astype(BF))
        lane = lax.broadcasted_iota(jnp.int32, (size, 128), 1)
        total_k = [None, None]
        total_v = [None, None]

        def grow(total, value):
            if total is None:
                return value
            if total.shape == value.shape:
                return total + value
            known = total.shape[1]
            return jnp.concatenate([total + value[:, :known], value[:, known:]], axis=1)

        for part in range(count // size):
            here = slice(part * size, (part + 1) * size)
            reach = (part + 1) * size if causal else span
            out_q = []
            for half in range(2):
                s = dot(qa[half][here], ka[half][:reach], NT)
                if causal:
                    if part:
                        s = jnp.concatenate([s[:, : part * size], causal_cut(s[:, part * size :], 0)], axis=1)
                    else:
                        s = causal_cut(s, 0)
                probs = jnp.exp(s)
                grads = dot(ga[half][here], va[half][:reach], NT)
                probs_low = probs.astype(BF)
                d_s = (probs * grads).astype(BF)
                total_v[half] = grow(total_v[half], dot(g_t[:, here], probs_low))
                total_k[half] = grow(total_k[half], dot(q_t[:, here], d_s))
                out_q.append(dot(d_s, k_low[:reach]))
            d_q[here, cols] = (jnp.where(lane < 64, out_q[0], out_q[1]) * 0.125).astype(BF)
        for target, total in ((d_k, total_k), (d_v, total_v)):
            joined = jnp.concatenate([total[0][:64], total[1][64:]], axis=0).astype(BF)
            target[:, cols] = joined.T

    loop(4, pair)


def project(x_low, proj, bias, q_ref, k_ref, v_ref, v_t, low_ref=None):
    def body(index):
        r = row_block(index)
        x = x_low(r)
        q_ref[r] = (dot(x, proj[0]) + bias[0:1]).astype(BF)
        k_ref[r] = dot(x, proj[1]).astype(BF)
        v_ref[r] = (dot(x, proj[2]) + bias[1:2]).astype(BF)

    loop(q_ref.shape[0] // RB, body)
    v_t[...] = v_ref[...].T


def valid_rows(index, limit):
    return (lax.broadcasted_iota(jnp.int32, (RB, 1), 0) + index * RB < limit).astype(F32)


def ffn_rows(z_low, w_in, c_in, w_out, c_out, act_ref, slope_ref, r):
    total = None
    for c in range(w_in.shape[1] // 512):
        cols = slice(c * 512, c * 512 + 512)
        act, slope = gelu_both(dot(z_low, w_in[:, cols]) + c_in[:, cols])
        act = act.astype(BF)
        act_ref[r, cols] = act
        slope_ref[r, cols] = slope.astype(BF)
        part = dot(act, w_out[cols])
        total = part if total is None else total + part
    return total + c_out[...]


def enc_forward_kernel(
    length, x, proj, out_w, bias, w_in, c_in, w_out, c_out, gain, offset,
    memory, shown, q_ref, k_ref, v_ref, mixed_t, lse, normed1, rstd1, act, slope, normed2, rstd2, v_t,
):
    project(lambda r: x[r], proj, bias, q_ref, k_ref, v_ref, v_t)
    mix_forward(q_ref, k_ref, v_t, length[0], False, mixed_t, lse)
    rows_after(x, mixed_t, out_w, bias, w_in, c_in, w_out, c_out, gain, offset, length[1], memory, shown, normed1, rstd1, act, slope, normed2, rstd2)


def rows_after(x, mixed_t, out_w, bias, w_in, c_in, w_out, c_out, gain, offset, limit, memory, shown, normed1, rstd1, act, slope, normed2, rstd2):
    def body(index):
        r = row_block(index)
        xf = x[r].astype(F32)
        n1, s1 = norm_rows(xf + dot(mixed_t[:, r], out_w[...], TN) + bias[2:3])
        normed1[r] = n1.astype(BF)
        rstd1[r] = s1
        y = n1 * gain[0:1] + offset[0:1]
        f = ffn_rows(y.astype(BF), w_in, c_in, w_out, c_out, act, slope, r)
        n2, s2 = norm_rows(y + f + xf)
        normed2[r] = n2.astype(BF)
        rstd2[r] = s2
        result = n2 * gain[1:2] + offset[1:2]
        memory[r] = result.astype(BF)
        shown[r] = (result * valid_rows(index, limit)).astype(BF)

    loop(x.shape[0] // RB, body)


def ffn_back(grad_low, act, slope, z_low, w_in, w_out, d_hidden, d_w1, d_w2, small, first_row, on_rows):
    small[first_row : first_row + 5] = jnp.zeros((5, 512), F32)

    def body(index):
        r = row_block(index)
        g = grad_low[r]
        total = None
        for c in range(4):
            cols = slice(c * 512, c * 512 + 512)
            dh = (dot(g, w_out[cols], NT) * slope[r, cols].astype(F32)).astype(BF)
            d_hidden[r, cols] = dh
            small[first_row + c : first_row + c + 1] += jnp.sum(dh.astype(F32), axis=0, keepdims=True)
            part = dot(dh, w_in[:, cols], NT)
            total = part if total is None else total + part
        small[first_row + 4 : first_row + 5] += jnp.sum(g.astype(F32), axis=0, keepdims=True)
        on_rows(r, total)

    loop(grad_low.shape[0] // RB, body)
    z = z_low[...]
    g = grad_low[...]
    for c in range(4):
        cols = slice(c * 512, c * 512 + 512)
        d_w1[cols] = dot(z, d_hidden[:, cols], TN).astype(BF)
        d_w2[cols] = dot(act[:, cols], g, TN).astype(BF)


def self_back(x_low, proj, out_w, q_ref, k_ref, v_ref, mixed_t, lse, place, length, causal, grad_low, grad_mixed, d_q, d_k, d_v, d_proj, d_out, small, rest):
    grad_mixed[...] = dot(grad_low[...], out_w[...], NT).astype(BF)
    d_out[...] = dot(mixed_t[...], grad_low[...]).astype(BF)
    mix_back(q_ref, k_ref, v_ref, mixed_t, lse, grad_mixed, place, length, causal, d_q, d_k, d_v)
    small[0:1] = jnp.sum(d_q[...].astype(F32), axis=0, keepdims=True)
    small[1:2] = jnp.sum(d_v[...].astype(F32), axis=0, keepdims=True)
    small[2:3] = jnp.sum(grad_low[...].astype(F32), axis=0, keepdims=True)
    x = x_low[...]
    d_proj[0:512] = dot(x, d_q[...], TN).astype(BF)
    d_proj[512:1024] = dot(x, d_k[...], TN).astype(BF)
    d_proj[1024:1536] = dot(x, d_v[...], TN).astype(BF)

    def body(index):
        r = row_block(index)
        rest(r, dot(d_q[r], proj[0], NT) + dot(d_k[r], proj[1], NT) + dot(d_v[r], proj[2], NT))

    loop(x_low.shape[0] // RB, body)


def enc_back_kernel(
    length, x, d_memory, cot, proj, out_w, w_in, w_out, gain, offset, place,
    q_ref, k_ref, v_ref, mixed_t, lse, normed1, rstd1, act, slope, normed2, rstd2,
    d_x, d_proj, d_out, d_w1, d_w2, small,
    last, grad_low, z_low, d_hidden, grad_mixed, d_q, d_k, d_v,
):
    small[...] = jnp.zeros(small.shape, F32)

    def top(index):
        r = row_block(index)
        n2 = normed2[r].astype(F32)
        g = cot[r].astype(F32) * valid_rows(index, length[1]) + d_memory[r].astype(F32)
        small[9:10] += jnp.sum(g * n2, axis=0, keepdims=True)
        small[11:12] += jnp.sum(g, axis=0, keepdims=True)
        g = norm_rows_back(n2, rstd2[r], gain[1:2], g)
        last[r] = g
        grad_low[r] = g.astype(BF)
        z_low[r] = (normed1[r].astype(F32) * gain[0:1] + offset[0:1]).astype(BF)

    loop(x.shape[0] // RB, top)

    def middle(r, grad):
        n1 = normed1[r].astype(F32)
        g = last[r] + grad
        small[8:9] += jnp.sum(g * n1, axis=0, keepdims=True)
        small[10:11] += jnp.sum(g, axis=0, keepdims=True)
        g = norm_rows_back(n1, rstd1[r], gain[0:1], g)
        last[r] = last[r] + g
        grad_mixed[r] = g.astype(BF)

    ffn_back(grad_low, act, slope, z_low, w_in, w_out, d_hidden, d_w1, d_w2, small, 3, middle)
    grad_low[...] = grad_mixed[...]

    def rest(r, grad):
        d_x[r] = last[r] + grad

    self_back(x, proj, out_w, q_ref, k_ref, v_ref, mixed_t, lse, place, length[0], False, grad_low, grad_mixed, d_q, d_k, d_v, d_proj, d_out, small, rest)


def dec_self_kernel(
    length, x, pair_row, proj, out_w, bias, gain, offset,
    x_low, q_ref, k_ref, v_ref, mixed_t, lse, normed1, rstd1, v_t,
):
    def low(r):
        value = (x[r].astype(F32) + pair_row[...]).astype(BF)
        x_low[r] = value
        return value

    project(low, proj, bias, q_ref, k_ref, v_ref, v_t)
    mix_forward(q_ref, k_ref, v_t, length[0], True, mixed_t, lse)

    def body(index):
        r = row_block(index)
        n1, s1 = norm_rows(x[r].astype(F32) + pair_row[...] + dot(mixed_t[:, r], out_w[...], TN) + bias[2:3])
        normed1[r] = n1
        rstd1[r] = s1

    loop(x.shape[0] // RB, body)


def dec_mid_kernel(
    length, x, pair_row, normed1, memory, cot, c_proj, c_out, c_bias, c_gain, c_offset,
    w_in, c_in, w_out, c_out_b, gain, offset, place,
    shown, grad_last, grad_first, d_memory, d_cproj, d_cout, d_w1, d_w2, small,
    y_low, z_low, q_ref, k_ref, v_ref, v_t, mixed_t, lse, normed2, rstd2, act, slope, normed3, rstd3, grad_low, d_hidden, grad_mixed, d_q, d_k, d_v,
):
    count = x.shape[0]
    span = memory.shape[0]
    small[...] = jnp.zeros(small.shape, F32)

    def queries(index):
        r = row_block(index)
        y = (normed1[r] * gain[0:1] + offset[0:1]).astype(BF)
        y_low[r] = y
        q_ref[r] = (dot(y, c_proj[0]) + c_bias[0:1]).astype(BF)

    loop(count // RB, queries)

    def keys(index):
        r = row_block(index)
        m = memory[r]
        k_ref[r] = dot(m, c_proj[1]).astype(BF)
        v_ref[r] = (dot(m, c_proj[2]) + c_bias[1:2]).astype(BF)

    loop(span // RB, keys)
    v_t[...] = v_ref[...].T
    mix_forward(q_ref, k_ref, v_t, length[0], False, mixed_t, lse)

    def forward(index):
        r = row_block(index)
        y = normed1[r] * gain[0:1] + offset[0:1]
        n2, s2 = norm_rows(y + dot(mixed_t[:, r], c_out[...], TN) + c_bias[2:3])
        normed2[r] = n2.astype(BF)
        rstd2[r] = s2
        z = n2 * c_gain[...] + c_offset[...]
        zl = z.astype(BF)
        z_low[r] = zl
        f = ffn_rows(zl, w_in, c_in, w_out, c_out_b, act, slope, r)
        n3, s3 = norm_rows(z + f + x[r].astype(F32) + pair_row[...])
        shown[r] = ((n3 * gain[1:2] + offset[1:2]) * valid_rows(index, length[1])).astype(BF)
        g = cot[r].astype(F32) * valid_rows(index, length[1])
        small[9:10] += jnp.sum(g * n3, axis=0, keepdims=True)
        small[11:12] += jnp.sum(g, axis=0, keepdims=True)
        g = norm_rows_back(n3, s3, gain[1:2], g)
        grad_last[r] = g
        grad_low[r] = g.astype(BF)

    loop(count // RB, forward)

    def middle(r, grad):
        n2 = normed2[r].astype(F32)
        g = grad_last[r] + grad
        small[8:9] += jnp.sum(g * n2, axis=0, keepdims=True)
        small[10:11] += jnp.sum(g, axis=0, keepdims=True)
        g = norm_rows_back(n2, rstd2[r], c_gain[...], g)
        grad_first[r] = g
        grad_mixed[r] = g.astype(BF)

    ffn_back(grad_low, act, slope, z_low, w_in, w_out, d_hidden, d_w1, d_w2, small, 3, middle)
    grad_low[...] = grad_mixed[...]
    grad_mixed[...] = dot(grad_low[...], c_out[...], NT).astype(BF)
    d_cout[...] = dot(mixed_t[...], grad_low[...]).astype(BF)
    mix_back(q_ref, k_ref, v_ref, mixed_t, lse, grad_mixed, place, length[0], False, d_q, d_k, d_v)
    small[0:1] = jnp.sum(d_q[...].astype(F32), axis=0, keepdims=True)
    small[1:2] = jnp.sum(d_v[...].astype(F32), axis=0, keepdims=True)
    small[2:3] = jnp.sum(grad_low[...].astype(F32), axis=0, keepdims=True)
    m = memory[...]
    d_cproj[0:512] = dot(y_low[...], d_q[...], TN).astype(BF)
    d_cproj[512:1024] = dot(m, d_k[...], TN).astype(BF)
    d_cproj[1024:1536] = dot(m, d_v[...], TN).astype(BF)

    def first(index):
        r = row_block(index)
        grad_first[r] += dot(d_q[r], c_proj[0], NT)

    loop(count // RB, first)

    def back(index):
        r = row_block(index)
        d_memory[r] = (dot(d_k[r], c_proj[1], NT) + dot(d_v[r], c_proj[2], NT)).astype(BF)

    loop(span // RB, back)


def dec_self_back_kernel(
    length, x_low, grad_last, grad_first, proj, out_w, gain, place, q_ref, k_ref, v_ref, mixed_t, lse, normed1, rstd1,
    d_x, d_proj, d_out, small,
    last, grad_low, grad_mixed, d_q, d_k, d_v,
):
    small[...] = jnp.zeros(small.shape, F32)

    def top(index):
        r = row_block(index)
        n1 = normed1[r]
        g = grad_first[r]
        small[3:4] += jnp.sum(g * n1, axis=0, keepdims=True)
        small[4:5] += jnp.sum(g, axis=0, keepdims=True)
        g = norm_rows_back(n1, rstd1[r], gain[0:1], g)
        last[r] = grad_last[r] + g
        grad_low[r] = g.astype(BF)

    loop(x_low.shape[0] // RB, top)

    def rest(r, grad):
        g = last[r] + grad
        d_x[r] = g
        small[5:6] += jnp.sum(g, axis=0, keepdims=True)

    self_back(x_low, proj, out_w, q_ref, k_ref, v_ref, mixed_t, lse, place, length[0], True, grad_low, grad_mixed, d_q, d_k, d_v, d_proj, d_out, small, rest)


def vm(shape, dtype):
    return pltpu.VMEM(shape, dtype)


def sds(shape, dtype):
    return jax.ShapeDtypeStruct(shape, dtype)


def call(kernel, name, outs, scratch, length, args, flops=0):
    spec = pl.BlockSpec(memory_space=pltpu.VMEM)
    return pl.pallas_call(
        kernel,
        name=name,
        out_shape=[sds(*o) for o in outs],
        in_specs=[pl.BlockSpec(memory_space=pltpu.SMEM)] + [spec] * len(args),
        out_specs=[spec] * len(outs),
        scratch_shapes=[vm(*s) for s in scratch],
        compiler_params=pltpu.CompilerParams(vmem_limit_bytes=62 * 2**20),
        cost_estimate=pl.CostEstimate(flops=flops, bytes_accessed=20 * 2**20, transcendentals=0),
    )(length, *args)


def enc_forward(length, x, layer):
    proj, out_w, bias, w_in, c_in, w_out, c_out, gain, offset = layer
    n, d = x.shape
    f = w_in.shape[1]
    outs = [((n, d), BF), ((n, d), BF), ((n, d), BF), ((n, d), BF), ((n, d), BF), ((d, n), BF), ((8, 1, n), F32),
            ((n, d), BF), ((n, 1), F32), ((n, f), BF), ((n, f), BF), ((n, d), BF), ((n, 1), F32)]
    res = call(enc_forward_kernel, "encoder_forward", outs, [((d, n), BF)], length,
               [x, proj, out_w, bias, w_in, c_in, w_out, c_out, gain, offset], int(15e9))
    return res[0], res[1], tuple(res[2:])


def enc_back(length, x, d_memory, cot, layer, place, saved):
    proj, out_w, bias, w_in, c_in, w_out, c_out, gain, offset = layer
    n, d = x.shape
    f = w_in.shape[1]
    outs = [((n, d), F32), ((3 * d, d), BF), ((d, d), BF), ((f, d), BF), ((f, d), BF), ((16, d), F32)]
    scratch = [((n, d), F32), ((n, d), BF), ((n, d), BF), ((n, f), BF), ((n, d), BF), ((n, d), BF), ((n, d), BF), ((n, d), BF)]
    return call(enc_back_kernel, "encoder_back", outs, scratch, length,
                [x, d_memory, cot, proj, out_w, w_in, w_out, gain, offset, place, *saved], int(35e9))


def dec_self(length, x, pair_row, layer):
    proj, out_w, bias, w_in, c_in, w_out, c_out, gain, offset = layer
    n, d = x.shape
    outs = [((n, d), BF), ((n, d), BF), ((n, d), BF), ((n, d), BF), ((d, n), BF), ((8, 1, n), F32), ((n, d), F32), ((n, 1), F32)]
    return call(dec_self_kernel, "decoder_self", outs, [((d, n), BF)], length,
                [x, pair_row, proj, out_w, bias, gain, offset], int(8e9))


def dec_mid(length, x, pair_row, normed1, memory, cot, layer, cross, place):
    proj, out_w, bias, w_in, c_in, w_out, c_out, gain, offset = layer
    n, d = x.shape
    m = memory.shape[0]
    f = w_in.shape[1]
    outs = [((n, d), BF), ((n, d), F32), ((n, d), F32), ((m, d), BF), ((3 * d, d), BF), ((d, d), BF), ((f, d), BF), ((f, d), BF), ((16, d), F32)]
    scratch = [((n, d), BF), ((n, d), BF), ((n, d), BF), ((m, d), BF), ((m, d), BF), ((d, m), BF), ((d, n), BF), ((8, 1, n), F32),
               ((n, d), BF), ((n, 1), F32), ((n, f), BF), ((n, f), BF), ((8, 128), F32), ((8, 128), F32), ((n, d), BF), ((n, f), BF), ((n, d), BF),
               ((n, d), BF), ((m, d), BF), ((m, d), BF)]
    return call(dec_mid_kernel, "decoder_middle", outs, scratch, length,
                [x, pair_row, normed1, memory, cot, *cross, w_in, c_in, w_out, c_out, gain, offset, place], int(55e9))


def dec_self_back(length, x_low, grad_last, grad_first, layer, place, saved):
    proj, out_w, bias, w_in, c_in, w_out, c_out, gain, offset = layer
    n, d = x_low.shape
    outs = [((n, d), F32), ((3 * d, d), BF), ((d, d), BF), ((8, d), F32)]
    scratch = [((n, d), F32), ((n, d), BF), ((n, d), BF), ((n, d), BF), ((n, d), BF), ((n, d), BF)]
    return call(dec_self_back_kernel, "decoder_self_back", outs, scratch, length,
                [x_low, grad_last, grad_first, proj, out_w, gain, place, *saved], int(20e9))


def nothing(*refs):
    pass


def blank(*shapes):
    spec = pl.BlockSpec(memory_space=pl.ANY)
    return pl.pallas_call(nothing, name="blank", out_shape=[sds(*s) for s in shapes], out_specs=[spec] * len(shapes))()


def per_device(
    embeds, cotangent, pair_ids, seq_lengths, alive_count,
    self_proj, self_out, self_bias, ffn_in, ffn_in_bias, ffn_out, ffn_out_bias, norm_gain, norm_bias,
    cross_proj, cross_out, cross_bias, cross_norm_gain, cross_norm_bias, pair_embed,
):
    layer = (self_proj[0], self_out[0], self_bias[0], ffn_in[0], ffn_in_bias, ffn_out[0], ffn_out_bias, norm_gain[0], norm_bias[0])
    cross = (cross_proj, cross_out, cross_bias, cross_norm_gain[None], cross_norm_bias[None])
    place = jnp.asarray(place_matrix(), BF)
    section_zero = lax.axis_index("section") == 0
    x, cot = embeds[0], cotangent[0]
    count, n, d = x.shape
    f = ffn_in.shape[2]
    live = (jnp.arange(count) < alive_count[0])[None, :]
    valid = jnp.where(live, seq_lengths, 0)
    pairs = pair_embed.shape[0]
    onehot = (pair_ids[:, None] == jnp.arange(pairs)[None, :]).astype(F32)
    pair_rows = jnp.dot(onehot, pair_embed, precision=lax.Precision.HIGHEST)
    src = [jnp.stack([seq_lengths[0, s], valid[0, s]]) for s in range(count)]
    tgt = [jnp.stack([seq_lengths[1, s], valid[1, s]]) for s in range(count)]
    mid = [jnp.stack([seq_lengths[0, s], valid[1, s]]) for s in range(count)]
    nd, nf, n1 = (n, d), (n, f), (n, 1)

    def first(s):
        def enc():
            memory, shown, (q, k, v, mt, lse, na, ra, act, slope, nb, rb) = enc_forward(src[s], x[s], layer)
            (wide,) = blank((nd, F32))
            return memory, shown, q, k, v, mt, lse, ra, na, wide, act, slope, nb, rb

        def dec():
            low, q, k, v, mt, lse, na, ra = dec_self(tgt[s], x[s], pair_rows[s : s + 1], layer)
            memory, shown, act, slope, nb, rb = blank((nd, BF), (nd, BF), (nf, BF), (nf, BF), (nd, BF), (n1, F32))
            return memory, shown, q, k, v, mt, lse, ra, low, na, act, slope, nb, rb

        return lax.cond(section_zero, enc, dec)

    def middle(s, saved, memory):
        def enc():
            return (saved[1], *blank((nd, F32), (nd, F32), (nd, BF), ((3 * d, d), BF), ((d, d), BF), ((f, d), BF), ((f, d), BF), ((16, d), F32)))

        def dec():
            return tuple(dec_mid(mid[s], x[s], pair_rows[s : s + 1], saved[9], memory, cot[s], layer, cross, place))

        return lax.cond(section_zero, enc, dec)

    def last(s, saved, done, d_memory):
        _, _, q, k, v, mt, lse, ra, na, wide, act, slope, nb, rb = saved

        def enc():
            d_x, dp, do, d1, d2, small = enc_back(src[s], x[s], d_memory, cot[s], layer, place, (q, k, v, mt, lse, na, ra, act, slope, nb, rb))
            return d_x, dp, do, d1, d2, small

        def dec():
            d_x, dp, do, small = dec_self_back(tgt[s], na, done[1], done[2], layer, place, (q, k, v, mt, lse, wide, ra))
            m = done[8]
            own = jnp.concatenate([small[0:3], m[3:8], small[3:4], m[9:10], small[4:5], m[11:12], small[5:6], jnp.zeros((3, d), F32)])
            return d_x, dp, do, done[6], done[7], own

        return lax.cond(section_zero, enc, dec)

    ahead = [(0, 1)]
    behind = [(1, 0)]
    saved, memory, done, grads, d_memory = [], [], [], [], []
    for s in range(count):
        saved.append(first(s))
        memory.append(lax.ppermute(saved[s][0], "section", ahead))
    for s in range(count):
        done.append(middle(s, saved[s], memory[s]))
        d_memory.append(lax.ppermute(done[s][3], "section", behind))
    for s in range(count):
        grads.append(last(s, saved[s], done[s], d_memory[s]))
    shown = jnp.stack([done[s][0] for s in range(count)])
    d_x = jnp.stack([grads[s][0] for s in range(count)])

    def total(parts):
        return sum(p.astype(F32) for p in parts)

    own = total([g[5] for g in grads])
    pack = jnp.concatenate([total([g[i] for g in grads]) for i in (1, 2, 3, 4)] + [own]).astype(BF)
    pair_grad = sum(onehot[s][:, None] * grads[s][5][12:13] for s in range(count))
    mid_small = total([m[8] for m in done])
    pack_cross = jnp.concatenate([total([m[4] for m in done]), total([m[5] for m in done]), mid_small, pair_grad]).astype(BF)
    pack = lax.psum(pack, "dp").astype(F32)
    pack_cross = lax.psum(jnp.where(section_zero, 0, pack_cross), ("section", "dp")).astype(F32)
    a, b, c, e = 3 * d, 4 * d, 4 * d + f, 4 * d + 2 * f
    small = pack[e:]
    w1 = pack[b:c].reshape(f // d, d, d).transpose(1, 0, 2).reshape(d, f)
    cs = pack_cross[4 * d :]
    return (
        shown[None], d_x[None],
        pack[:a].reshape(1, 3, d, d), pack[a:b][None], small[None, 0:3], w1[None], small[3:7].reshape(1, f), pack[c:e][None], small[7:8],
        small[None, 8:10], small[None, 10:12],
        pack_cross[:a].reshape(3, d, d), pack_cross[a:b], cs[0:3], cs[8], cs[10], cs[16 : 16 + pairs],
    )


def solution(mesh):
    s, r = "section", P()
    in_specs = (
        P(s, "dp"), P(s, "dp"), P("dp"), P(None, "dp"), P("dp"),
        P(s), P(s), P(s), P(s), P(s), P(s), P(s), P(s), P(s), r, r, r, r, r, r,
    )
    out_specs = (P(s, "dp"), P(s, "dp"), P(s), P(s), P(s), P(s), P(s), P(s), P(s), P(s), P(s), r, r, r, r, r, r)
    return jax.shard_map(per_device, mesh=mesh, in_specs=in_specs, out_specs=out_specs, check_vma=False)
```

```python
import functools

import jax
import jax.numpy as jnp
import numpy as np
from jax import lax
from jax.experimental import pallas as pl
from jax.experimental.pallas import tpu as pltpu
from jax.sharding import PartitionSpec as P

BF = jnp.bfloat16
F32 = jnp.float32
HEADS = 8
PAIRS = 16
MESH = pl.DeviceIdType.MESH
EPSILON = 1e-05
BLOCKED = -1e30
RB = 256
NN = (((1,), (0,)), ((), ()))
NT = (((1,), (1,)), ((), ()))
TN = (((0,), (0,)), ((), ()))


def dot(left, right, dims=NN):
    return lax.dot_general(left, right, dims, preferred_element_type=F32)


def row_block(index, size=RB):
    return pl.ds(pl.multiple_of(index * size, size), size)


def loop(count, body):
    def step(index, carry):
        body(index)
        return carry

    lax.fori_loop(0, count, step, 0)


def lanes_of(half):
    lane = lax.broadcasted_iota(jnp.int32, (1, 128), 1)
    inside = (lane // 64) == half
    spare = lane - 64 * (1 - half)
    ones = (~inside) & (spare < 32)
    block = (~inside) & (spare >= 32)
    flag = (~inside) & (spare == 32)
    return tuple(m.astype(F32) for m in (inside, ones, block, flag))


def norm_rows(value):
    centre = jnp.mean(value, -1, keepdims=True)
    centred = value - centre
    rstd = lax.rsqrt(jnp.mean(centred * centred, -1, keepdims=True) + EPSILON)
    return centred * rstd, rstd


def norm_rows_back(normed, rstd, gain, grad):
    scaled = grad * gain
    return rstd * (
        scaled
        - jnp.mean(scaled, -1, keepdims=True)
        - normed * jnp.mean(scaled * normed, -1, keepdims=True)
    )


def gelu_both(hidden):
    size = jnp.abs(hidden)
    t = pl.reciprocal(1.0 + (0.3275911 * 0.7071067811865476) * size)
    bell = jnp.exp(-0.5 * hidden * hidden)
    half = t * (
        0.127414796
        + t * (-0.142248368 + t * (0.7107068705 + t * (-0.7265760135 + t * 0.5307027145)))
    )
    half = half * bell
    phi = jnp.where(hidden < 0, half, 1.0 - half)
    return hidden * phi, phi + hidden * (bell * 0.3989422804014327)


def key_fill(count, length, ones, block):
    position = lax.broadcasted_iota(jnp.int32, (count, 128), 0)
    return ones + jnp.where(position < length, 0.0, BLOCKED) * block


def causal_cut(scores, query_axis):
    query = lax.broadcasted_iota(jnp.int32, scores.shape, query_axis)
    key = lax.broadcasted_iota(jnp.int32, scores.shape, 1 - query_axis)
    return jnp.where(key <= query, scores, BLOCKED)


def mix_forward(queries, keys, values_t, length, causal, mixed_t, lse):
    count = queries.shape[0]
    span = keys.shape[0]
    size = 256 if causal else min(512, count)

    def pair(index):
        cols = row_block(index, 128)
        q = queries[:, cols].astype(F32) * 0.125
        k = keys[:, cols].astype(F32)
        vt = values_t[cols, :]
        lane = lax.broadcasted_iota(jnp.int32, (128, 1), 0)
        qa, ka, va = [], [], []
        for half in range(2):
            inside, ones, block, flag = lanes_of(half)
            qa.append((q * inside + flag).astype(BF))
            ka.append((k * inside + key_fill(span, length, ones, block)).astype(BF))
            va.append(jnp.where((lane // 64) == half, vt.astype(F32), 1.0).astype(BF))
        for part in range(count // size):
            here = slice(part * size, (part + 1) * size)
            for half in range(2):
                if causal:
                    pieces = [(0, part * size, False), (part * size, size, True)]
                else:
                    pieces = [(0, span, False)]
                pieces = [piece for piece in pieces if piece[1]]
                scores = []
                for start, length_k, cut in pieces:
                    s = dot(ka[half][start : start + length_k], qa[half][here], NT)
                    scores.append(causal_cut(s, 1) if cut else s)
                top = jnp.max(scores[0], axis=0, keepdims=True)
                for s in scores[1:]:
                    top = jnp.maximum(top, jnp.max(s, axis=0, keepdims=True))
                total = None
                for (start, length_k, _), s in zip(pieces, scores):
                    probs = jnp.exp(s - top).astype(BF)
                    o = dot(va[half][:, start : start + length_k], probs)
                    total = o if total is None else total + o
                other = 64 * (1 - half)
                mass = total[other : other + 1]
                own = total[64 * half : 64 * half + 64] / mass
                mixed_t[pl.ds(pl.multiple_of(index * 128 + 64 * half, 64), 64), here] = own.astype(BF)
                lse[index * 2 + half, :, here] = top + jnp.log(mass)

    loop(4, pair)


def split3(value):
    high = value.astype(BF).astype(F32)
    middle = (value - high).astype(BF).astype(F32)
    low = (value - high - middle).astype(BF).astype(F32)
    return high, middle, low


def place_matrix():
    out = np.zeros((16, 512), np.float32)
    for half in range(2):
        other = 64 * (1 - half)
        for piece in range(3):
            out[half * 4 + piece, half * 128 + other + piece] = 1
            out[8 + half * 4 + piece, 256 + half * 128 + other + piece] = 1
        out[half * 4 + 3, half * 128 + other + 32] = 1
    return out


def mix_back(queries, keys, values, mixed_t, lse, grad_mixed, place, length, causal, d_q, d_k, d_v):
    count = queries.shape[0]
    span = keys.shape[0]
    size = 256 if causal else min(512, count)

    def pair(index):
        cols = row_block(index, 128)
        q = queries[:, cols].astype(F32) * 0.125
        k_low = keys[:, cols]
        k = k_low.astype(F32)
        v = values[:, cols].astype(F32)
        g_low = grad_mixed[:, cols]
        g = g_low.astype(F32)
        q_t = q.astype(BF).T
        g_t = g_low.T
        product = g_t.astype(F32) * mixed_t[cols, :].astype(F32)
        row = lax.broadcasted_iota(jnp.int32, (16, count), 0)
        spread = jnp.where((row == 3) | (row == 7), 1.0, 0.0)
        for half in range(2):
            shift = -lse[index * 2 + half]
            delta = -jnp.sum(product[64 * half : 64 * half + 64], axis=0, keepdims=True)
            for base, value in ((0, shift), (8, delta)):
                for piece, part in enumerate(split3(value)):
                    spread = jnp.where(row == base + 4 * half + piece, part, spread)
        extra = dot(spread.astype(BF), place[...], TN)
        qa, ka, va, ga = [], [], [], []
        for half in range(2):
            inside, ones, block, flag = lanes_of(half)
            qa.append((q * inside + extra[:, half * 128 : half * 128 + 128]).astype(BF))
            ga.append((g * inside + extra[:, 256 + half * 128 : 384 + half * 128]).astype(BF))
            ka.append((k * inside + key_fill(span, length, ones, block)).astype(BF))
            va.append((v * inside + (1.0 - inside)).astype(BF))
        lane = lax.broadcasted_iota(jnp.int32, (size, 128), 1)
        total_k = [None, None]
        total_v = [None, None]

        def grow(total, value):
            if total is None:
                return value
            if total.shape == value.shape:
                return total + value
            known = total.shape[1]
            return jnp.concatenate([total + value[:, :known], value[:, known:]], axis=1)

        for part in range(count // size):
            here = slice(part * size, (part + 1) * size)
            reach = (part + 1) * size if causal else span
            out_q = []
            for half in range(2):
                s = dot(qa[half][here], ka[half][:reach], NT)
                if causal:
                    if part:
                        s = jnp.concatenate([s[:, : part * size], causal_cut(s[:, part * size :], 0)], axis=1)
                    else:
                        s = causal_cut(s, 0)
                probs = jnp.exp(s)
                grads = dot(ga[half][here], va[half][:reach], NT)
                probs_low = probs.astype(BF)
                d_s = (probs * grads).astype(BF)
                total_v[half] = grow(total_v[half], dot(g_t[:, here], probs_low))
                total_k[half] = grow(total_k[half], dot(q_t[:, here], d_s))
                out_q.append(dot(d_s, k_low[:reach]))
            d_q[here, cols] = (jnp.where(lane < 64, out_q[0], out_q[1]) * 0.125).astype(BF)
        for target, total in ((d_k, total_k), (d_v, total_v)):
            joined = jnp.concatenate([total[0][:64], total[1][64:]], axis=0).astype(BF)
            target[:, cols] = joined.T

    loop(4, pair)


def project(x_low, proj, bias, q_ref, k_ref, v_ref, v_t, low_ref=None):
    def body(index):
        r = row_block(index)
        x = x_low(r)
        q_ref[r] = (dot(x, proj[0]) + bias[0:1]).astype(BF)
        k_ref[r] = dot(x, proj[1]).astype(BF)
        v_ref[r] = (dot(x, proj[2]) + bias[1:2]).astype(BF)

    loop(q_ref.shape[0] // RB, body)
    v_t[...] = v_ref[...].T


def valid_rows(index, limit):
    return (lax.broadcasted_iota(jnp.int32, (RB, 1), 0) + index * RB < limit).astype(F32)


def ffn_rows(z_low, w_in, c_in, w_out, c_out, act_ref, slope_ref, r):
    total = None
    for c in range(w_in.shape[1] // 512):
        cols = slice(c * 512, c * 512 + 512)
        act, slope = gelu_both(dot(z_low, w_in[:, cols]) + c_in[:, cols])
        act = act.astype(BF)
        act_ref[r, cols] = act
        slope_ref[r, cols] = slope.astype(BF)
        part = dot(act, w_out[cols])
        total = part if total is None else total + part
    return total + c_out[...]


def enc_forward_kernel(
    length, x, proj, out_w, bias, w_in, c_in, w_out, c_out, gain, offset,
    memory, shown, q_ref, k_ref, v_ref, mixed_t, lse, normed1, rstd1, act, slope, normed2, rstd2, v_t,
):
    project(lambda r: x[r], proj, bias, q_ref, k_ref, v_ref, v_t)
    mix_forward(q_ref, k_ref, v_t, length[0], False, mixed_t, lse)
    rows_after(x, mixed_t, out_w, bias, w_in, c_in, w_out, c_out, gain, offset, length[1], memory, shown, normed1, rstd1, act, slope, normed2, rstd2)


def rows_after(x, mixed_t, out_w, bias, w_in, c_in, w_out, c_out, gain, offset, limit, memory, shown, normed1, rstd1, act, slope, normed2, rstd2):
    def body(index):
        r = row_block(index)
        xf = x[r].astype(F32)
        n1, s1 = norm_rows(xf + dot(mixed_t[:, r], out_w[...], TN) + bias[2:3])
        normed1[r] = n1.astype(BF)
        rstd1[r] = s1
        y = n1 * gain[0:1] + offset[0:1]
        f = ffn_rows(y.astype(BF), w_in, c_in, w_out, c_out, act, slope, r)
        n2, s2 = norm_rows(y + f + xf)
        normed2[r] = n2.astype(BF)
        rstd2[r] = s2
        result = n2 * gain[1:2] + offset[1:2]
        memory[r] = result.astype(BF)
        shown[r] = (result * valid_rows(index, limit)).astype(BF)

    loop(x.shape[0] // RB, body)


def put(target, rows, value, later):
    target[rows] = (value + target[rows].astype(F32) if later else value).astype(BF)


def carry_on(later, before, targets, sems):
    copies = [pltpu.make_async_copy(b, t, sems.at[i]) for i, (b, t) in enumerate(zip(before, targets))] if later else []
    for copy in copies:
        copy.start()
    return copies


def ffn_back(grad_low, act, slope, z_low, w_in, w_out, d_hidden, pack, copies, small, first_row, on_rows):
    def body(index):
        r = row_block(index)
        g = grad_low[r]
        total = None
        for c in range(4):
            cols = slice(c * 512, c * 512 + 512)
            dh = (dot(g, w_out[cols], NT) * slope[r, cols].astype(F32)).astype(BF)
            d_hidden[r, cols] = dh
            small[first_row + c : first_row + c + 1] += jnp.sum(dh.astype(F32), axis=0, keepdims=True)
            part = dot(dh, w_in[:, cols], NT)
            total = part if total is None else total + part
        small[first_row + 4 : first_row + 5] += jnp.sum(g.astype(F32), axis=0, keepdims=True)
        on_rows(r, total)

    loop(grad_low.shape[0] // RB, body)
    z = z_low[...]
    g = grad_low[...]
    for copy in copies:
        copy.wait()
    prev = bool(copies)
    for c in range(4):
        cols = slice(c * 512, c * 512 + 512)
        put(pack, cols, dot(z, d_hidden[:, cols], TN), prev)
        put(pack, slice(2048 + c * 512, 2560 + c * 512), dot(act[:, cols], g, TN), prev)


def self_back(x_low, proj, out_w, q_ref, k_ref, v_ref, mixed_t, lse, place, length, causal, grad_low, grad_mixed, d_q, d_k, d_v, pack, copies, small, rest):
    for copy in copies:
        copy.wait()
    prev = bool(copies)
    grad_mixed[...] = dot(grad_low[...], out_w[...], NT).astype(BF)
    put(pack, slice(1536, 2048), dot(mixed_t[...], grad_low[...]), prev)
    mix_back(q_ref, k_ref, v_ref, mixed_t, lse, grad_mixed, place, length, causal, d_q, d_k, d_v)
    small[0:1] += jnp.sum(d_q[...].astype(F32), axis=0, keepdims=True)
    small[1:2] += jnp.sum(d_v[...].astype(F32), axis=0, keepdims=True)
    small[2:3] += jnp.sum(grad_low[...].astype(F32), axis=0, keepdims=True)
    x = x_low[...]
    put(pack, slice(0, 512), dot(x, d_q[...], TN), prev)
    put(pack, slice(512, 1024), dot(x, d_k[...], TN), prev)
    put(pack, slice(1024, 1536), dot(x, d_v[...], TN), prev)

    def body(index):
        r = row_block(index)
        rest(r, dot(d_q[r], proj[0], NT) + dot(d_k[r], proj[1], NT) + dot(d_v[r], proj[2], NT))

    loop(x_low.shape[0] // RB, body)


def enc_back_kernel(
    later, length, x, d_memory, cot, proj, out_w, w_in, w_out, gain, offset, place,
    q_ref, k_ref, v_ref, mixed_t, lse, normed1, rstd1, act, slope, normed2, rstd2, *refs,
):
    d_x, pack_a, pack_b, small, last, grad_low, z_low, d_hidden, grad_mixed, d_q, d_k, d_v, sems = refs[3 * later :]
    copies = carry_on(later, refs[:3], (small, pack_b, pack_a), sems)
    if later:
        copies[0].wait()
    else:
        small[...] = jnp.zeros(small.shape, F32)

    def top(index):
        r = row_block(index)
        n2 = normed2[r].astype(F32)
        g = cot[r].astype(F32) * valid_rows(index, length[1]) + d_memory[r].astype(F32)
        small[9:10] += jnp.sum(g * n2, axis=0, keepdims=True)
        small[11:12] += jnp.sum(g, axis=0, keepdims=True)
        g = norm_rows_back(n2, rstd2[r], gain[1:2], g)
        last[r] = g
        grad_low[r] = g.astype(BF)
        z_low[r] = (normed1[r].astype(F32) * gain[0:1] + offset[0:1]).astype(BF)

    loop(x.shape[0] // RB, top)

    def middle(r, grad):
        n1 = normed1[r].astype(F32)
        g = last[r] + grad
        small[8:9] += jnp.sum(g * n1, axis=0, keepdims=True)
        small[10:11] += jnp.sum(g, axis=0, keepdims=True)
        g = norm_rows_back(n1, rstd1[r], gain[0:1], g)
        last[r] = last[r] + g
        grad_mixed[r] = g.astype(BF)

    ffn_back(grad_low, act, slope, z_low, w_in, w_out, d_hidden, pack_b, copies[1:2], small, 3, middle)
    grad_low[...] = grad_mixed[...]

    def rest(r, grad):
        d_x[r] = last[r] + grad

    self_back(x, proj, out_w, q_ref, k_ref, v_ref, mixed_t, lse, place, length[0], False, grad_low, grad_mixed, d_q, d_k, d_v, pack_a, copies[-1:], small, rest)


def dec_self_kernel(
    length, x, pair_row, proj, out_w, bias, gain, offset,
    x_low, q_ref, k_ref, v_ref, mixed_t, lse, normed1, rstd1, v_t,
):
    def low(r):
        value = (x[r].astype(F32) + pair_row[...]).astype(BF)
        x_low[r] = value
        return value

    project(low, proj, bias, q_ref, k_ref, v_ref, v_t)
    mix_forward(q_ref, k_ref, v_t, length[0], True, mixed_t, lse)

    def body(index):
        r = row_block(index)
        n1, s1 = norm_rows(x[r].astype(F32) + pair_row[...] + dot(mixed_t[:, r], out_w[...], TN) + bias[2:3])
        normed1[r] = n1
        rstd1[r] = s1

    loop(x.shape[0] // RB, body)


def dec_mid_kernel(
    later, length, x, pair_row, normed1, memory, cot, c_proj, c_out, c_bias, c_gain, c_offset,
    w_in, c_in, w_out, c_out_b, gain, offset, place, *refs,
):
    shown, grad_last, grad_first, d_memory, pack_b, pack_c, small = refs[3 * later : 3 * later + 7]
    (
        y_low, z_low, q_ref, k_ref, v_ref, v_t, mixed_t, lse, normed2, rstd2, act, slope, grad_low, d_hidden, grad_mixed, d_q, d_k, d_v, sems,
    ) = refs[3 * later + 7 :]
    copies = carry_on(later, refs[:3], (small, pack_b, pack_c), sems)
    count = x.shape[0]
    span = memory.shape[0]
    if later:
        copies[0].wait()
    else:
        small[...] = jnp.zeros(small.shape, F32)

    def queries(index):
        r = row_block(index)
        y = (normed1[r] * gain[0:1] + offset[0:1]).astype(BF)
        y_low[r] = y
        q_ref[r] = (dot(y, c_proj[0]) + c_bias[0:1]).astype(BF)

    loop(count // RB, queries)

    def keys(index):
        r = row_block(index)
        m = memory[r]
        k_ref[r] = dot(m, c_proj[1]).astype(BF)
        v_ref[r] = (dot(m, c_proj[2]) + c_bias[1:2]).astype(BF)

    loop(span // RB, keys)
    v_t[...] = v_ref[...].T
    mix_forward(q_ref, k_ref, v_t, length[0], False, mixed_t, lse)

    def forward(index):
        r = row_block(index)
        y = normed1[r] * gain[0:1] + offset[0:1]
        n2, s2 = norm_rows(y + dot(mixed_t[:, r], c_out[...], TN) + c_bias[2:3])
        normed2[r] = n2.astype(BF)
        rstd2[r] = s2
        z = n2 * c_gain[...] + c_offset[...]
        zl = z.astype(BF)
        z_low[r] = zl
        f = ffn_rows(zl, w_in, c_in, w_out, c_out_b, act, slope, r)
        n3, s3 = norm_rows(z + f + x[r].astype(F32) + pair_row[...])
        shown[r] = ((n3 * gain[1:2] + offset[1:2]) * valid_rows(index, length[1])).astype(BF)
        g = cot[r].astype(F32) * valid_rows(index, length[1])
        small[9:10] += jnp.sum(g * n3, axis=0, keepdims=True)
        small[11:12] += jnp.sum(g, axis=0, keepdims=True)
        g = norm_rows_back(n3, s3, gain[1:2], g)
        grad_last[r] = g
        grad_low[r] = g.astype(BF)

    loop(count // RB, forward)

    def middle(r, grad):
        n2 = normed2[r].astype(F32)
        g = grad_last[r] + grad
        small[8:9] += jnp.sum(g * n2, axis=0, keepdims=True)
        small[10:11] += jnp.sum(g, axis=0, keepdims=True)
        g = norm_rows_back(n2, rstd2[r], c_gain[...], g)
        grad_first[r] = g
        grad_mixed[r] = g.astype(BF)

    ffn_back(grad_low, act, slope, z_low, w_in, w_out, d_hidden, pack_b, copies[1:2], small, 3, middle)
    grad_low[...] = grad_mixed[...]
    grad_mixed[...] = dot(grad_low[...], c_out[...], NT).astype(BF)
    for copy in copies[2:]:
        copy.wait()
    put(pack_c, slice(1536, 2048), dot(mixed_t[...], grad_low[...]), later)
    mix_back(q_ref, k_ref, v_ref, mixed_t, lse, grad_mixed, place, length[0], False, d_q, d_k, d_v)
    small[0:1] += jnp.sum(d_q[...].astype(F32), axis=0, keepdims=True)
    small[1:2] += jnp.sum(d_v[...].astype(F32), axis=0, keepdims=True)
    small[2:3] += jnp.sum(grad_low[...].astype(F32), axis=0, keepdims=True)
    m = memory[...]
    put(pack_c, slice(0, 512), dot(y_low[...], d_q[...], TN), later)
    put(pack_c, slice(512, 1024), dot(m, d_k[...], TN), later)
    put(pack_c, slice(1024, 1536), dot(m, d_v[...], TN), later)

    def first(index):
        r = row_block(index)
        grad_first[r] += dot(d_q[r], c_proj[0], NT)

    loop(count // RB, first)

    def back(index):
        r = row_block(index)
        d_memory[r] = (dot(d_k[r], c_proj[1], NT) + dot(d_v[r], c_proj[2], NT)).astype(BF)

    loop(span // RB, back)


def dec_self_back_kernel(
    later, length, x_low, grad_last, grad_first, proj, out_w, gain, place, q_ref, k_ref, v_ref, mixed_t, lse, normed1, rstd1,
    middle_small, pair_mark, *refs,
):
    d_x, pack_a, small, last, grad_low, grad_mixed, d_q, d_k, d_v, column, sems = refs[2 * later :]
    copies = carry_on(later, refs[:2], (small, pack_a), sems)
    if later:
        copies[0].wait()
    else:
        small[...] = jnp.zeros(small.shape, F32)
    for here in (3, 4, 5, 6, 7, 9, 11):
        small[here : here + 1] = middle_small[here : here + 1]
    column[...] = jnp.zeros(column.shape, F32)

    def top(index):
        r = row_block(index)
        n1 = normed1[r]
        g = grad_first[r]
        small[8:9] += jnp.sum(g * n1, axis=0, keepdims=True)
        small[10:11] += jnp.sum(g, axis=0, keepdims=True)
        g = norm_rows_back(n1, rstd1[r], gain[0:1], g)
        last[r] = grad_last[r] + g
        grad_low[r] = g.astype(BF)

    loop(x_low.shape[0] // RB, top)

    def rest(r, grad):
        g = last[r] + grad
        d_x[r] = g
        column[0:1] += jnp.sum(g, axis=0, keepdims=True)

    self_back(x_low, proj, out_w, q_ref, k_ref, v_ref, mixed_t, lse, place, length[0], True, grad_low, grad_mixed, d_q, d_k, d_v, pack_a, copies[-1:], small, rest)
    small[16:] += pair_mark[...] * column[0:1]


def vm(shape, dtype):
    return pltpu.VMEM(shape, dtype)


def sds(shape, dtype):
    return jax.ShapeDtypeStruct(shape, dtype)


def call(kernel, name, outs, scratch, length, args, flops=0, before=()):
    spec = pl.BlockSpec(memory_space=pltpu.VMEM)
    anywhere = pl.BlockSpec(memory_space=pl.ANY)
    return pl.pallas_call(
        kernel,
        name=name,
        out_shape=[sds(*o) for o in outs],
        in_specs=[pl.BlockSpec(memory_space=pltpu.SMEM)] + [spec] * len(args) + [anywhere] * len(before),
        out_specs=[spec] * len(outs),
        scratch_shapes=[vm(*s) if isinstance(s, tuple) else s for s in scratch],
        compiler_params=pltpu.CompilerParams(vmem_limit_bytes=62 * 2**20),
        cost_estimate=pl.CostEstimate(flops=flops, bytes_accessed=20 * 2**20, transcendentals=0),
    )(length, *args, *before)


def enc_forward(length, x, layer):
    proj, out_w, bias, w_in, c_in, w_out, c_out, gain, offset = layer
    n, d = x.shape
    f = w_in.shape[1]
    outs = [((n, d), BF), ((n, d), BF), ((n, d), BF), ((n, d), BF), ((n, d), BF), ((d, n), BF), ((8, 1, n), F32),
            ((n, d), BF), ((n, 1), F32), ((n, f), BF), ((n, f), BF), ((n, d), BF), ((n, 1), F32)]
    res = call(enc_forward_kernel, "encoder_forward", outs, [((d, n), BF)], length,
               [x, proj, out_w, bias, w_in, c_in, w_out, c_out, gain, offset], int(15e9))
    return res[0], res[1], tuple(res[2:])


def enc_back(length, x, d_memory, cot, layer, place, saved, prev):
    proj, out_w, bias, w_in, c_in, w_out, c_out, gain, offset = layer
    n, d = x.shape
    f = w_in.shape[1]
    outs = [((n, d), F32), ((4 * d, d), BF), ((2 * f, d), BF), ((16 + PAIRS, d), F32)]
    scratch = [((n, d), F32), ((n, d), BF), ((n, d), BF), ((n, f), BF), ((n, d), BF), ((n, d), BF), ((n, d), BF), ((n, d), BF), pltpu.SemaphoreType.DMA((3,))]
    return call(functools.partial(enc_back_kernel, bool(prev)), "encoder_back", outs, scratch, length,
                [x, d_memory, cot, proj, out_w, w_in, w_out, gain, offset, place, *saved], int(35e9), prev)


def dec_self(length, x, pair_row, layer):
    proj, out_w, bias, w_in, c_in, w_out, c_out, gain, offset = layer
    n, d = x.shape
    outs = [((n, d), BF), ((n, d), BF), ((n, d), BF), ((n, d), BF), ((d, n), BF), ((8, 1, n), F32), ((n, d), F32), ((n, 1), F32)]
    return call(dec_self_kernel, "decoder_self", outs, [((d, n), BF)], length,
                [x, pair_row, proj, out_w, bias, gain, offset], int(8e9))


def dec_mid(length, x, pair_row, normed1, memory, cot, layer, cross, place, prev):
    proj, out_w, bias, w_in, c_in, w_out, c_out, gain, offset = layer
    n, d = x.shape
    m = memory.shape[0]
    f = w_in.shape[1]
    outs = [((n, d), BF), ((n, d), F32), ((n, d), F32), ((m, d), BF), ((2 * f, d), BF), ((4 * d, d), BF), ((16, d), F32)]
    scratch = [((n, d), BF), ((n, d), BF), ((n, d), BF), ((m, d), BF), ((m, d), BF), ((d, m), BF), ((d, n), BF), ((8, 1, n), F32),
               ((n, d), BF), ((n, 1), F32), ((n, f), BF), ((n, f), BF), ((n, d), BF), ((n, f), BF), ((n, d), BF),
               ((n, d), BF), ((m, d), BF), ((m, d), BF), pltpu.SemaphoreType.DMA((3,))]
    return call(functools.partial(dec_mid_kernel, bool(prev)), "decoder_middle", outs, scratch, length,
                [x, pair_row, normed1, memory, cot, *cross, w_in, c_in, w_out, c_out, gain, offset, place], int(55e9), prev)


def dec_self_back(length, x_low, grad_last, grad_first, layer, place, saved, middle_small, pair_mark, prev):
    proj, out_w, bias, w_in, c_in, w_out, c_out, gain, offset = layer
    n, d = x_low.shape
    outs = [((n, d), F32), ((4 * d, d), BF), ((16 + pair_mark.shape[0], d), F32)]
    scratch = [((n, d), F32), ((n, d), BF), ((n, d), BF), ((n, d), BF), ((n, d), BF), ((n, d), BF), ((8, d), F32), pltpu.SemaphoreType.DMA((2,))]
    return call(functools.partial(dec_self_back_kernel, bool(prev)), "decoder_self_back", outs, scratch, length,
                [x_low, grad_last, grad_first, proj, out_w, gain, place, *saved, middle_small, pair_mark], int(20e9), prev)


def add_rows(target, start, size, sources):
    block = max(b for b in range(16, min(size, 96) + 1, 16) if size % b == 0)

    def body(index):
        here = pl.ds(pl.multiple_of(start + index * block, 16), block)
        value = 0.0
        for ref, begin in sources:
            value = value + ref[pl.ds(pl.multiple_of(begin + index * block, 16), block)].astype(F32)
        target[here] = value.astype(BF)

    loop(size // block, body)


def grad_sum_kernel(count, rows1, rows2, a, b, c, own, mids, out, work, final, inbox, pairbox, load_sem, send_sem, recv_sem):
    m = count // 2
    me = lax.axis_index("dp")
    section = lax.axis_index("section")
    core = me % 2
    chip = me // 2
    decoder = section == 1
    na, nb, nc = a.shape[0], b.shape[0], c.shape[0]
    ns, nm = own.shape[0], mids.shape[0]
    loads = [
        pltpu.make_async_copy(a, work.at[pl.ds(0, na)], load_sem.at[0]),
        pltpu.make_async_copy(b, work.at[pl.ds(na, nb)], load_sem.at[1]),
        pltpu.make_async_copy(c, work.at[pl.ds(rows1, nc)], load_sem.at[2]),
    ]
    for copy in loads:
        copy.start()

    def device_at(place, core):
        place = place % m
        turn = place * (1 - core) + ((m - place) % m) * core
        odd = turn // (m // 2)
        return 2 * (2 * (turn * (1 - odd) + (m - 1 - turn) * odd) + odd) + core

    turn = (chip // 2) * (1 - chip % 2) + (m - 1 - chip // 2) * (chip % 2)
    back = (m - turn) % m
    place = turn * (1 - core) + back * core
    place_other = turn * core + back * (1 - core)
    other = me + 1 - 2 * core
    after = device_at(place + 1, core)
    before = device_at(place + m - 1, core)
    barrier = pltpu.get_barrier_semaphore()
    for device in (after, before, other):
        pl.semaphore_signal(barrier, inc=1, device_id={"dp": device}, device_id_type=MESH)
    pl.semaphore_signal(barrier, inc=1, device_id={"section": 1 - section}, device_id_type=MESH)
    pad1 = rows1 - na - nb
    work[na + nb : rows1] = jnp.concatenate([own[0:16], jnp.zeros((pad1 - 16, own.shape[1]), F32)]).astype(BF)
    pad2 = rows2 - nc
    work[rows1 + nc : rows1 + rows2] = jnp.concatenate(
        [mids[...], own[16:], jnp.zeros((pad2 - nm - ns + 16, own.shape[1]), F32)]
    ).astype(BF)
    for copy in loads:
        copy.wait()
    pl.semaphore_wait(barrier, 4)

    starts, chunks = (0, rows1), (rows1 // count, rows2 // count)
    units = []
    for region in range(2):
        first = chunks[region] // 32 * 16
        units += [(region, 0, first), (region, first, chunks[region] - first)]
    boxes, width = [], 0
    for _, _, size in units:
        boxes.append(width)
        width += size

    def low(region, half, chunk):
        return starts[region] + half * (m * chunks[region]) + (chunk % m) * chunks[region]

    slot = iter(range(10**6))

    def remote(src, dst, device):
        index = next(slot)
        return pltpu.make_async_remote_copy(
            src, dst, send_sem.at[index], recv_sem.at[index], device_id=device, device_id_type=MESH
        )

    def rows(ref, start, size):
        return ref.at[pl.ds(pl.multiple_of(start, 16), size)]

    def on_decoder(region, action):
        if region == 0:
            action()
        else:
            pl.when(decoder)(action)

    def pair_copy(region, t):
        size = chunks[region]
        start = low(region, 1 - core, place_other + 2 * m - 1 - t)
        return remote(rows(work, start, size), rows(pairbox, start - (1 - core) * m * size - starts[region] + (region * m * chunks[0]), size), {"dp": other})

    def pair_low(region, chunk):
        return region * m * chunks[0] + (chunk % m) * chunks[region]

    pairs = [[pair_copy(region, t) for region in range(2)] for t in range(m)]
    for t in range(m):
        for region in range(2):
            on_decoder(region, pairs[t][region].start)
    sends = [[None] * len(units) for _ in range(m - 1)]
    for s in range(m - 1):
        for u, (region, offset, size) in enumerate(units):
            start = low(region, core, place + 2 * m - 1 - s) + offset
            sends[s][u] = remote(rows(work, start, size), inbox.at[pl.ds(s * width + boxes[u], size)], {"dp": after})
    for t in range(m):
        for region in range(2):
            on_decoder(region, pairs[t][region].wait_recv)
        for u, (region, offset, size) in enumerate(units):
            chunk = place + 2 * m - 1 - t

            def step(t=t, u=u, region=region, offset=offset, size=size, chunk=chunk):
                start = low(region, core, chunk) + offset
                sources = [(work, start), (pairbox, pair_low(region, chunk) + offset)]
                if t:
                    sends[t - 1][u].wait_recv()
                    sources.append((inbox, (t - 1) * width + boxes[u]))
                add_rows(work if t < m - 1 else final, start, size, sources)
                if t < m - 1:
                    sends[t][u].start()

            on_decoder(region, step)

    mine = rows(final, low(1, core, place), chunks[1])
    across = remote(mine, mine, {"section": 1 - section})
    pl.when(decoder)(across.start)
    passes = [[None] * len(units) for _ in range(m - 1)]
    for s in range(m - 1):
        for u, (region, offset, size) in enumerate(units):
            here = rows(final, low(region, core, place + 2 * m - s) + offset, size)
            passes[s][u] = remote(here, here, {"dp": after})
    shares = []
    for s in range(m):
        for region in range(2):
            here = rows(final, low(region, core, place + 2 * m - s), chunks[region])
            shares.append(remote(here, here, {"dp": other}))
    for s in range(m):
        for u, (region, offset, size) in enumerate(units):
            if s:
                passes[s - 1][u].wait_recv()
            elif u == 2:
                pl.when(section == 0)(across.wait_recv)
            if s < m - 1:
                passes[s][u].start()
            if offset:
                shares[2 * s + region].start()
    for copy in shares:
        copy.wait_recv()
    copy = pltpu.make_async_copy(final, out, load_sem.at[0])
    copy.start()
    for t in range(m):
        for region in range(2):
            on_decoder(region, pairs[t][region].wait_send)
    for s in range(m - 1):
        for u, (region, _, _) in enumerate(units):
            on_decoder(region, sends[s][u].wait_send)
            passes[s][u].wait_send()
    for share in shares:
        share.wait_send()
    pl.when(decoder)(across.wait_send)
    copy.wait()


def grad_sum(count, a, b, c, own, mids):
    d = a.shape[1]
    unit = 16 * count
    m = count // 2
    rows1 = -(-(a.shape[0] + b.shape[0] + 16) // unit) * unit
    rows2 = -(-(c.shape[0] + own.shape[0] - 16 + mids.shape[0]) // unit) * unit
    width = (rows1 + rows2) // count
    slots = (m - 1) * 8 + m * 4 + 1
    anywhere = pl.BlockSpec(memory_space=pl.ANY)
    inside = pl.BlockSpec(memory_space=pltpu.VMEM)
    out = pl.pallas_call(
        functools.partial(grad_sum_kernel, count, rows1, rows2),
        name="gradient_sum",
        out_shape=sds((rows1 + rows2, d), BF),
        in_specs=[anywhere] * 3 + [inside] * 2,
        out_specs=anywhere,
        scratch_shapes=[
            vm((rows1 + rows2, d), BF),
            vm((rows1 + rows2, d), BF),
            vm(((m - 1) * width, d), BF),
            vm((m * width, d), BF),
            pltpu.SemaphoreType.DMA((3,)),
            pltpu.SemaphoreType.DMA((slots,)),
            pltpu.SemaphoreType.DMA((slots,)),
        ],
        compiler_params=pltpu.CompilerParams(collective_id=0, has_side_effects=True, vmem_limit_bytes=48 * 2**20),
    )(a, b, c, own, mids)
    return out, rows1


def unpack_kernel(rows1, f, pack, proj, out_w, bias, w_in, b_in, w_out, b_out, gain, offset, c_proj, c_out, c_bias, c_gain, c_offset, pair):
    d = pack.shape[1]

    def put_rows(target, start, size):
        target[...] = pack[start : start + size].astype(F32)

    put_rows(proj, 0, 3 * d)
    put_rows(out_w, 3 * d, d)
    for c in range(f // d):
        w_in[:, c * d : (c + 1) * d] = pack[(4 + c) * d : (5 + c) * d].astype(F32)
    put_rows(w_out, 4 * d + f, f)
    put_rows(c_proj, rows1, 3 * d)
    put_rows(c_out, rows1 + 3 * d, d)
    small = pack[4 * d + 2 * f : 4 * d + 2 * f + 16].astype(F32)
    bias[...] = small[0:3]
    for c in range(f // d):
        b_in[:, c * d : (c + 1) * d] = small[3 + c : 4 + c]
    b_out[...] = small[7:8]
    gain[...] = small[8:10]
    offset[...] = small[10:12]
    small = pack[rows1 + 4 * d : rows1 + 4 * d + 32].astype(F32)
    c_bias[...] = small[0:3]
    c_gain[...] = small[8:9]
    c_offset[...] = small[10:11]
    pair[...] = small[16 : 16 + pair.shape[0]]


def unpack(pack, rows1, f, pairs):
    d = pack.shape[1]
    inside = pl.BlockSpec(memory_space=pltpu.VMEM)
    shapes = [(3 * d, d), (d, d), (3, d), (d, f), (1, f), (f, d), (1, d), (2, d), (2, d), (3 * d, d), (d, d), (3, d), (1, d), (1, d), (pairs, d)]
    return pl.pallas_call(
        functools.partial(unpack_kernel, rows1, f),
        name="unpack",
        out_shape=[sds(s, F32) for s in shapes],
        in_specs=[inside],
        out_specs=[inside] * len(shapes),
        compiler_params=pltpu.CompilerParams(vmem_limit_bytes=50 * 2**20),
    )(pack)


def nothing(*refs):
    pass


def blank(*shapes):
    spec = pl.BlockSpec(memory_space=pl.ANY)
    return pl.pallas_call(nothing, name="blank", out_shape=[sds(*s) for s in shapes], out_specs=[spec] * len(shapes))()


def per_device(
    embeds, cotangent, pair_ids, seq_lengths, alive_count,
    self_proj, self_out, self_bias, ffn_in, ffn_in_bias, ffn_out, ffn_out_bias, norm_gain, norm_bias,
    cross_proj, cross_out, cross_bias, cross_norm_gain, cross_norm_bias, pair_embed,
):
    layer = (self_proj[0], self_out[0], self_bias[0], ffn_in[0], ffn_in_bias, ffn_out[0], ffn_out_bias, norm_gain[0], norm_bias[0])
    cross = (cross_proj, cross_out, cross_bias, cross_norm_gain[None], cross_norm_bias[None])
    place = jnp.asarray(place_matrix(), BF)
    section_zero = lax.axis_index("section") == 0
    x, cot = embeds[0], cotangent[0]
    count, n, d = x.shape
    f = ffn_in.shape[2]
    live = (jnp.arange(count) < alive_count[0])[None, :]
    valid = jnp.where(live, seq_lengths, 0)
    pairs = pair_embed.shape[0]
    onehot = (pair_ids[:, None] == jnp.arange(pairs)[None, :]).astype(F32)
    pair_rows = jnp.dot(onehot, pair_embed, precision=lax.Precision.HIGHEST)
    src = [jnp.stack([seq_lengths[0, s], valid[0, s]]) for s in range(count)]
    tgt = [jnp.stack([seq_lengths[1, s], valid[1, s]]) for s in range(count)]
    mid = [jnp.stack([seq_lengths[0, s], valid[1, s]]) for s in range(count)]
    nd, nf, n1 = (n, d), (n, f), (n, 1)

    def first(s):
        def enc():
            memory, shown, (q, k, v, mt, lse, na, ra, act, slope, nb, rb) = enc_forward(src[s], x[s], layer)
            (wide,) = blank((nd, F32))
            return memory, shown, q, k, v, mt, lse, ra, na, wide, act, slope, nb, rb

        def dec():
            low, q, k, v, mt, lse, na, ra = dec_self(tgt[s], x[s], pair_rows[s : s + 1], layer)
            memory, shown, act, slope, nb, rb = blank((nd, BF), (nd, BF), (nf, BF), (nf, BF), (nd, BF), (n1, F32))
            return memory, shown, q, k, v, mt, lse, ra, low, na, act, slope, nb, rb

        return lax.cond(section_zero, enc, dec)

    def middle(s, saved, memory, prev):
        def enc():
            return (saved[1], *blank((nd, F32), (nd, F32), (nd, BF), ((2 * f, d), BF), ((4 * d, d), BF), ((16, d), F32)))

        def dec():
            return tuple(dec_mid(mid[s], x[s], pair_rows[s : s + 1], saved[9], memory, cot[s], layer, cross, place, prev))

        return lax.cond(section_zero, enc, dec)

    def last(s, saved, done, d_memory, prev, prev_done):
        _, _, q, k, v, mt, lse, ra, na, wide, act, slope, nb, rb = saved

        def enc():
            before = prev and (prev[3], prev[2], prev[1])
            return tuple(enc_back(src[s], x[s], d_memory, cot[s], layer, place, (q, k, v, mt, lse, na, ra, act, slope, nb, rb), before))

        def dec():
            before = prev and (prev[3], prev[1])
            d_x, pack_a, small = dec_self_back(
                tgt[s], na, done[1], done[2], layer, place, (q, k, v, mt, lse, wide, ra), done[6], onehot[s][:, None], before
            )
            return d_x, pack_a, done[4], small

        return lax.cond(section_zero, enc, dec)

    ahead = [(0, 1)]
    behind = [(1, 0)]
    saved, memory, done, grads, d_memory = [], [], [], [], []
    for s in range(count):
        saved.append(first(s))
        memory.append(lax.ppermute(saved[s][0], "section", ahead))
    for s in range(count):
        done.append(middle(s, saved[s], memory[s], (done[s - 1][6], done[s - 1][4], done[s - 1][5]) if s else ()))
        d_memory.append(lax.ppermute(done[s][3], "section", behind))
    for s in range(count):
        grads.append(last(s, saved[s], done[s], d_memory[s], grads[s - 1] if s else (), done[s - 1] if s else ()))
    shown = jnp.stack([done[s][0] for s in range(count)])
    d_x = jnp.stack([grads[s][0] for s in range(count)])
    pack, rows1 = grad_sum(lax.axis_size("dp"), grads[-1][1], grads[-1][2], done[-1][5], grads[-1][3], done[-1][6])
    proj, out_w, bias, w_in, b_in, w_out, b_out, gain, offset, c_proj, c_out, c_bias, c_gain, c_offset, pair = unpack(pack, rows1, f, pairs)
    return (
        shown[None], d_x[None], proj.reshape(1, 3, d, d), out_w[None], bias[None], w_in[None], b_in, w_out[None], b_out, gain[None], offset[None],
        c_proj.reshape(3, d, d), c_out, c_bias, c_gain[0], c_offset[0], pair,
    )


def solution(mesh):
    s, r = "section", P()
    in_specs = (
        P(s, "dp"), P(s, "dp"), P("dp"), P(None, "dp"), P("dp"),
        P(s), P(s), P(s), P(s), P(s), P(s), P(s), P(s), P(s), r, r, r, r, r, r,
    )
    out_specs = (P(s, "dp"), P(s, "dp"), P(s), P(s), P(s), P(s), P(s), P(s), P(s), P(s), P(s), r, r, r, r, r, r)
    return jax.shard_map(per_device, mesh=mesh, in_specs=in_specs, out_specs=out_specs, check_vma=False)
```

```python
import functools

import jax
import jax.numpy as jnp
import numpy as np
from jax import lax
from jax.experimental import pallas as pl
from jax.experimental.pallas import tpu as pltpu
from jax.sharding import PartitionSpec as P

BF = jnp.bfloat16
F32 = jnp.float32
HEADS = 8
PAIRS = 16
MESH = pl.DeviceIdType.MESH
EPSILON = 1e-05
BLOCKED = -1e30
RB = 256
NN = (((1,), (0,)), ((), ()))
NT = (((1,), (1,)), ((), ()))
TN = (((0,), (0,)), ((), ()))


def dot(left, right, dims=NN):
    return lax.dot_general(left, right, dims, preferred_element_type=F32)


def row_block(index, size=RB):
    return pl.ds(pl.multiple_of(index * size, size), size)


def loop(count, body):
    def step(index, carry):
        body(index)
        return carry

    lax.fori_loop(0, count, step, 0)


def lanes_of(half):
    lane = lax.broadcasted_iota(jnp.int32, (1, 128), 1)
    inside = (lane // 64) == half
    spare = lane - 64 * (1 - half)
    ones = (~inside) & (spare < 32)
    block = (~inside) & (spare >= 32)
    flag = (~inside) & (spare == 32)
    return tuple(m.astype(F32) for m in (inside, ones, block, flag))


def norm_rows(value):
    centre = jnp.mean(value, -1, keepdims=True)
    centred = value - centre
    rstd = lax.rsqrt(jnp.mean(centred * centred, -1, keepdims=True) + EPSILON)
    return centred * rstd, rstd


def norm_rows_back(normed, rstd, gain, grad):
    scaled = grad * gain
    return rstd * (
        scaled
        - jnp.mean(scaled, -1, keepdims=True)
        - normed * jnp.mean(scaled * normed, -1, keepdims=True)
    )


def gelu_both(hidden):
    phi = 0.5 + 0.5 * lax.erf(hidden * 0.7071067811865476)
    bell = jnp.exp(-0.5 * hidden * hidden)
    return hidden * phi, phi + hidden * (bell * 0.3989422804014327)


def key_fill(count, length, ones, block):
    position = lax.broadcasted_iota(jnp.int32, (count, 128), 0)
    return ones + jnp.where(position < length, 0.0, BLOCKED) * block


def causal_cut(scores, query_axis):
    query = lax.broadcasted_iota(jnp.int32, scores.shape, query_axis)
    key = lax.broadcasted_iota(jnp.int32, scores.shape, 1 - query_axis)
    return jnp.where(key <= query, scores, BLOCKED)


def mix_forward(queries, keys, values_t, length, causal, mixed_t, lse):
    count = queries.shape[0]
    span = keys.shape[0]
    size = min(512 if causal else 1024, count)

    def pair(index):
        cols = row_block(index, 128)
        q = queries[:, cols].astype(F32) * 0.125
        k = keys[:, cols].astype(F32)
        vt = values_t[cols, :].astype(F32)
        lane = lax.broadcasted_iota(jnp.int32, (128, 1), 0)
        qa, ka, va = [], [], []
        for half in range(2):
            inside, ones, block, flag = lanes_of(half)
            qa.append((q * inside + flag).astype(BF))
            ka.append((k * inside + key_fill(span, length, ones, block)).astype(BF))
            va.append(jnp.where((lane // 64) == half, vt, 1.0).astype(BF))

        def scores_of(part, half):
            here = slice(part * size, (part + 1) * size)
            pieces = [(0, part * size, False), (part * size, size, True)] if causal else [(0, span, False)]
            return [
                (start, reach, cut, dot(ka[half][start : start + reach], qa[half][here], NT))
                for start, reach, cut in pieces
                if reach
            ]

        def finish(part, half, scores):
            here = slice(part * size, (part + 1) * size)
            scores = [(start, reach, causal_cut(s, 1) if cut else s) for start, reach, cut, s in scores]
            top = None
            for _, _, s in scores:
                best = jnp.max(s, axis=0, keepdims=True)
                top = best if top is None else jnp.maximum(top, best)
            total = None
            for start, reach, s in scores:
                o = dot(va[half][:, start : start + reach], jnp.exp(s - top).astype(BF))
                total = o if total is None else total + o
            other = 64 * (1 - half)
            mass = total[other : other + 1]
            own = total[64 * half : 64 * half + 64] / mass
            mixed_t[pl.ds(pl.multiple_of(index * 128 + 64 * half, 64), 64), here] = own.astype(BF)
            lse[index * 2 + half, :, here] = top + jnp.log(mass)

        waiting = None
        for tile in [(part, half) for part in range(count // size) for half in range(2)]:
            scores = scores_of(*tile)
            if waiting:
                finish(*waiting)
            waiting = (*tile, scores)
        finish(*waiting)

    loop(4, pair)


def split3(value):
    high = value.astype(BF).astype(F32)
    middle = (value - high).astype(BF).astype(F32)
    low = (value - high - middle).astype(BF).astype(F32)
    return high, middle, low


def place_matrix():
    out = np.zeros((16, 512), np.float32)
    for half in range(2):
        other = 64 * (1 - half)
        for piece in range(3):
            out[half * 4 + piece, half * 128 + other + piece] = 1
            out[8 + half * 4 + piece, 256 + half * 128 + other + piece] = 1
        out[half * 4 + 3, half * 128 + other + 32] = 1
    return out


def mix_back(queries, keys, values, mixed_t, lse, grad_mixed, place, length, causal, d_q, d_k, d_v):
    count = queries.shape[0]
    span = keys.shape[0]
    size = 256 if causal else min(512, count)

    def pair(index):
        cols = row_block(index, 128)
        q = queries[:, cols].astype(F32) * 0.125
        k_low = keys[:, cols]
        k = k_low.astype(F32)
        v = values[:, cols].astype(F32)
        g_low = grad_mixed[:, cols]
        g = g_low.astype(F32)
        q_t = q.astype(BF).T
        g_t = g_low.T
        product = g_t.astype(F32) * mixed_t[cols, :].astype(F32)
        row = lax.broadcasted_iota(jnp.int32, (16, count), 0)
        spread = jnp.where((row == 3) | (row == 7), 1.0, 0.0)
        for half in range(2):
            shift = -lse[index * 2 + half]
            delta = -jnp.sum(product[64 * half : 64 * half + 64], axis=0, keepdims=True)
            for base, value in ((0, shift), (8, delta)):
                for piece, part in enumerate(split3(value)):
                    spread = jnp.where(row == base + 4 * half + piece, part, spread)
        extra = dot(spread.astype(BF), place[...], TN)
        qa, ka, va, ga = [], [], [], []
        for half in range(2):
            inside, ones, block, flag = lanes_of(half)
            qa.append((q * inside + extra[:, half * 128 : half * 128 + 128]).astype(BF))
            ga.append((g * inside + extra[:, 256 + half * 128 : 384 + half * 128]).astype(BF))
            ka.append((k * inside + key_fill(span, length, ones, block)).astype(BF))
            va.append((v * inside + (1.0 - inside)).astype(BF))
        lane = lax.broadcasted_iota(jnp.int32, (size, 128), 1)
        total_k = [None, None]
        total_v = [None, None]

        def grow(total, value):
            if total is None:
                return value
            if total.shape == value.shape:
                return total + value
            known = total.shape[1]
            return jnp.concatenate([total + value[:, :known], value[:, known:]], axis=1)

        for part in range(count // size):
            here = slice(part * size, (part + 1) * size)
            reach = (part + 1) * size if causal else span
            out_q = []
            for half in range(2):
                s = dot(qa[half][here], ka[half][:reach], NT)
                if causal:
                    if part:
                        s = jnp.concatenate([s[:, : part * size], causal_cut(s[:, part * size :], 0)], axis=1)
                    else:
                        s = causal_cut(s, 0)
                probs = jnp.exp(s)
                grads = dot(ga[half][here], va[half][:reach], NT)
                probs_low = probs.astype(BF)
                d_s = (probs * grads).astype(BF)
                total_v[half] = grow(total_v[half], dot(g_t[:, here], probs_low))
                total_k[half] = grow(total_k[half], dot(q_t[:, here], d_s))
                out_q.append(dot(d_s, k_low[:reach]))
            d_q[here, cols] = (jnp.where(lane < 64, out_q[0], out_q[1]) * 0.125).astype(BF)
        for target, total in ((d_k, total_k), (d_v, total_v)):
            joined = jnp.concatenate([total[0][:64], total[1][64:]], axis=0).astype(BF)
            target[:, cols] = joined.T

    loop(4, pair)


class Late:
    def __init__(self, ref, copy):
        self.ref, self.copy = ref, copy

    def get(self):
        if self.copy is not None:
            self.copy.wait()
            self.copy = None
        return self.ref


class Leaving:
    def __init__(self, ref, out, sem):
        self.ref, self.out, self.sem = ref, out, sem

    def send(self, rows=None):
        if rows is None:
            pltpu.make_async_copy(self.ref, self.out, self.sem).start()
        else:
            pltpu.make_async_copy(self.ref.at[rows], self.out.at[rows], self.sem).start()

    def finish(self):
        pltpu.make_async_copy(self.ref, self.out, self.sem).wait()


def sds(shape, dtype):
    return jax.ShapeDtypeStruct(shape, dtype)


def vm(shape, dtype):
    return pltpu.VMEM(shape, dtype)


def call(kernel, name, args, outs, scratch, flops):
    anywhere = pl.BlockSpec(memory_space=pl.ANY)
    inside = pl.BlockSpec(memory_space=pltpu.VMEM)
    operands, in_specs, out_shapes, out_specs, memory, aliases = [], [], [], [], [], {}
    plan_in, plan_out = [], []
    for value, kind in args:
        operands.append(value)
        if kind == "smem":
            in_specs.append(pl.BlockSpec(memory_space=pltpu.SMEM))
            plan_in.append(None)
        elif kind == "vmem":
            in_specs.append(inside)
            plan_in.append(None)
        else:
            in_specs.append(anywhere)
            index = kind[1] if isinstance(kind, tuple) else None
            plan_in.append((len(memory), index))
            memory.append(vm(value.shape if index is None else value.shape[1:], value.dtype))
    count_in = len(args)
    for position, (shape, dtype, kind) in enumerate(outs):
        if kind == "vmem":
            out_shapes.append(sds(shape, dtype))
            out_specs.append(inside)
            plan_out.append(None)
            continue
        out_specs.append(anywhere)
        index, earlier = None, None
        if isinstance(kind, tuple) and kind[0] == "late":
            index, earlier, total = kind[1:]
            out_shapes.append(sds((total, *shape), dtype))
            if earlier is not None:
                aliases[len(operands)] = position
                operands.append(earlier)
                in_specs.append(anywhere)
        else:
            out_shapes.append(sds(shape, dtype))
        plan_out.append((len(memory), index, len(operands) if isinstance(kind, tuple) and kind[0] == "from" else None))
        memory.append(vm(shape, dtype))
        if isinstance(kind, tuple) and kind[0] == "from":
            operands.append(kind[1])
            in_specs.append(anywhere)
    total_in, count_out, count_memory = len(operands), len(outs), len(memory)

    def body(*refs):
        ins, results = refs[:total_in], refs[total_in : total_in + count_out]
        held = refs[total_in + count_out : total_in + count_out + count_memory]
        own = refs[total_in + count_out + count_memory : -1]
        sems = refs[-1]
        first, last = [], []
        for ref, plan in zip(ins[:count_in], plan_in):
            if plan is None:
                first.append(ref)
                continue
            where, index = plan
            copy = pltpu.make_async_copy(ref if index is None else ref.at[index], held[where], sems.at[where])
            copy.start()
            first.append(Late(held[where], copy))
        for ref, plan in zip(results, plan_out):
            if plan is None:
                last.append(ref)
                continue
            where, index, source = plan
            leaving = Leaving(held[where], ref if index is None else ref.at[index], sems.at[where])
            if source is not None:
                copy = pltpu.make_async_copy(ins[source], held[where], sems.at[where])
                copy.start()
                leaving.begin = Late(held[where], copy)
            last.append(leaving)
        kernel(*first, *last, *own)
        for leaving in last:
            if isinstance(leaving, Leaving):
                leaving.finish()

    return pl.pallas_call(
        body,
        name=name,
        out_shape=out_shapes,
        in_specs=in_specs,
        out_specs=out_specs,
        scratch_shapes=[*memory, *[vm(*s) for s in scratch], pltpu.SemaphoreType.DMA((max(count_memory, 1),))],
        input_output_aliases=aliases,
        compiler_params=pltpu.CompilerParams(vmem_limit_bytes=62 * 2**20),
        cost_estimate=pl.CostEstimate(flops=int(flops), bytes_accessed=20 * 2**20, transcendentals=0),
    )(*operands)


def valid_rows(index, limit, size=RB):
    return (lax.broadcasted_iota(jnp.int32, (size, 1), 0) + index * size < limit).astype(F32)


def ffn_rows(z_low, w_in, c_in, w_out, c_out, act_ref, slope_ref, r):
    total = None
    for c in range(w_in.shape[1] // 512):
        cols = slice(c * 512, c * 512 + 512)
        act, slope = gelu_both(dot(z_low, w_in[:, cols]) + c_in[:, cols])
        act = act.astype(BF)
        act_ref[r, cols] = act
        slope_ref[r, cols] = slope.astype(BF)
        part = dot(act, w_out[cols])
        total = part if total is None else total + part
    return total + c_out[...]


def put(target, rows, value, later):
    target[rows] = (value + target[rows].astype(F32) if later else value).astype(BF)


def ffn_back(grad_low, act, slope, z_low, w_in, w_out, pack, later, small, on_rows):
    def body(index):
        r = row_block(index)
        g = grad_low[r]
        total = None
        for c in range(4):
            cols = slice(c * 512, c * 512 + 512)
            dh = (dot(g, w_out[cols], NT) * slope[r, cols].astype(F32)).astype(BF)
            slope[r, cols] = dh
            small[3 + c : 4 + c] += jnp.sum(dh.astype(F32), axis=0, keepdims=True)
            part = dot(dh, w_in[:, cols], NT)
            total = part if total is None else total + part
        small[7:8] += jnp.sum(g.astype(F32), axis=0, keepdims=True)
        on_rows(r, total)

    loop(grad_low.shape[0] // RB, body)
    z = z_low[...]
    g = grad_low[...]
    act = act.get() if isinstance(act, Late) else act
    if later:
        pack.begin.get()
    for c in range(4):
        cols = slice(c * 512, c * 512 + 512)
        put(pack.ref, cols, dot(z, slope[:, cols], TN), later)
        put(pack.ref, slice(2048 + c * 512, 2560 + c * 512), dot(act[:, cols], g, TN), later)
    pack.send()


def project(count, x_low, proj, bias, q, k, v, v_t):
    def body(index):
        r = row_block(index)
        x = x_low(r)
        q.ref[r] = (dot(x, proj[0]) + bias[0:1]).astype(BF)
        k.ref[r] = dot(x, proj[1]).astype(BF)
        v.ref[r] = (dot(x, proj[2]) + bias[1:2]).astype(BF)

    loop(count // RB, body)
    q.send()
    k.send()
    v.send()
    v_t[...] = v.ref[...].T


def self_back(x, proj, out_w, q, k, v, mixed_t, lse, place, length, causal, grad_low, grad_mixed, d_q, d_k, d_v, pack, later, small, rest):
    grad_mixed[...] = dot(grad_low[...], out_w.get()[...], NT).astype(BF)
    mixed_t = mixed_t.get()
    if later:
        pack.begin.get()
    put(pack.ref, slice(1536, 2048), dot(mixed_t[...], grad_low[...]), later)
    q, k, v, x = q.get(), k.get(), v.get(), x.get()
    mix_back(q, k, v, mixed_t, lse, grad_mixed, place, length, causal, d_q, d_k, d_v)
    small[0:1] += jnp.sum(d_q[...].astype(F32), axis=0, keepdims=True)
    small[1:2] += jnp.sum(d_v[...].astype(F32), axis=0, keepdims=True)
    small[2:3] += jnp.sum(grad_low[...].astype(F32), axis=0, keepdims=True)
    xl = x[...]
    put(pack.ref, slice(0, 512), dot(xl, d_q[...], TN), later)
    put(pack.ref, slice(512, 1024), dot(xl, d_k[...], TN), later)
    put(pack.ref, slice(1024, 1536), dot(xl, d_v[...], TN), later)
    pack.send()
    proj = proj.get()

    def body(index):
        r = row_block(index)
        rest(r, dot(d_q[r], proj[0], NT) + dot(d_k[r], proj[1], NT) + dot(d_v[r], proj[2], NT))

    loop(x.shape[0] // RB, body)


def begin_small(small, earlier):
    small[...] = jnp.zeros(small.shape, F32) if earlier is None else earlier[...]


def enc_forward_kernel(
    length, x, proj, out_w, w_in, w_out, bias, c_in, c_out, gain, offset,
    memory, shown, q, k, v, mixed_t, lse, normed1, rstd1, act, slope, normed2, rstd2, v_t,
):
    x = x.get()
    project(x.shape[0], lambda r: x[r], proj.get(), bias, q, k, v, v_t)
    mix_forward(q.ref, k.ref, v_t, length[0], False, mixed_t.ref, lse)
    mixed_t.send()
    out_w, w_in, w_out = out_w.get(), w_in.get(), w_out.get()

    def body(index):
        r = row_block(index)
        xf = x[r].astype(F32)
        n1, s1 = norm_rows(xf + dot(mixed_t.ref[:, r], out_w[...], TN) + bias[2:3])
        normed1.ref[r] = n1.astype(BF)
        rstd1[r] = s1
        y = n1 * gain[0:1] + offset[0:1]
        f = ffn_rows(y.astype(BF), w_in, c_in, w_out, c_out, act.ref, slope.ref, r)
        n2, s2 = norm_rows(y + f + xf)
        normed2.ref[r] = n2.astype(BF)
        rstd2[r] = s2
        result = n2 * gain[1:2] + offset[1:2]
        memory.ref[r] = result.astype(BF)
        shown.ref[r] = (result * valid_rows(index, length[1])).astype(BF)
        for leaving in (act, slope, memory, shown, normed1, normed2):
            leaving.send(r)

    loop(x.shape[0] // RB, body)


def enc_forward(length, x, s, layer, shown):
    proj, out_w, bias, w_in, c_in, w_out, c_out, gain, offset = layer
    count, n, d = x.shape
    f = w_in.shape[1]
    nd = (n, d)
    args = [(length, "smem"), (x, ("late", s)), (proj, "late"), (out_w, "late"), (w_in, "late"), (w_out, "late")]
    args += [(v, "vmem") for v in (bias, c_in, c_out, gain, offset)]
    outs = [
        (nd, BF, "late"), (nd, BF, ("late", s, shown, count)), (nd, BF, "late"), (nd, BF, "late"), (nd, BF, "late"), ((d, n), BF, "late"),
        ((8, 1, n), F32, "vmem"), (nd, BF, "late"), ((n, 1), F32, "vmem"), ((n, f), BF, "late"), ((n, f), BF, "late"), (nd, BF, "late"), ((n, 1), F32, "vmem"),
    ]
    return call(enc_forward_kernel, "encoder_forward", args, outs, [((d, n), BF)], 15e9)


def enc_back_kernel(
    later, length, cot, d_memory, normed2, normed1, w_out, slope, w_in, act, out_w, mixed_t, q, k, v, x, proj,
    lse, rstd1, rstd2, gain, offset, place, *refs,
):
    earlier = refs[0] if later else None
    d_x, pack_a, pack_b, small, last, grad_low, z_low, grad_mixed, d_q, d_k, d_v = refs[later:]
    begin_small(small, earlier)
    cot, d_memory, normed2, normed1 = cot.get(), d_memory.get(), normed2.get(), normed1.get()

    def top(index):
        r = row_block(index)
        n2 = normed2[r].astype(F32)
        g = cot[r].astype(F32) * valid_rows(index, length[1]) + d_memory[r].astype(F32)
        small[9:10] += jnp.sum(g * n2, axis=0, keepdims=True)
        small[11:12] += jnp.sum(g, axis=0, keepdims=True)
        g = norm_rows_back(n2, rstd2[r], gain[1:2], g)
        last[r] = g
        grad_low[r] = g.astype(BF)
        z_low[r] = (normed1[r].astype(F32) * gain[0:1] + offset[0:1]).astype(BF)

    loop(last.shape[0] // RB, top)

    def middle(r, grad):
        n1 = normed1[r].astype(F32)
        g = last[r] + grad
        small[8:9] += jnp.sum(g * n1, axis=0, keepdims=True)
        small[10:11] += jnp.sum(g, axis=0, keepdims=True)
        g = norm_rows_back(n1, rstd1[r], gain[0:1], g)
        last[r] = last[r] + g
        grad_mixed[r] = g.astype(BF)

    ffn_back(grad_low, act, slope.get(), z_low, w_in.get(), w_out.get(), pack_b, later, small, middle)
    grad_low[...] = grad_mixed[...]

    def rest(r, grad):
        d_x.ref[r] = last[r] + grad
        d_x.send(r)

    self_back(x, proj, out_w, q, k, v, mixed_t, lse, place, length[0], False, grad_low, grad_mixed, d_q, d_k, d_v, pack_a, later, small, rest)


def enc_back(length, x, s, d_memory, cot, layer, place, saved, prev):
    proj, out_w, bias, w_in, c_in, w_out, c_out, gain, offset = layer
    q, k, v, mixed_t, lse, normed1, rstd1, act, slope, normed2, rstd2 = saved
    count, n, d = x.shape
    f = w_in.shape[1]
    nd = (n, d)
    args = [(length, "smem"), (cot, ("late", s))]
    args += [(a, "late") for a in (d_memory, normed2, normed1, w_out, slope, w_in, act, out_w, mixed_t, q, k, v)]
    args += [(x, ("late", s)), (proj, "late")]
    args += [(a, "vmem") for a in (lse, rstd1, rstd2, gain, offset, place)]
    carry = lambda i: ("from", prev[i]) if prev else "late"
    if prev:
        args.append((prev[3], "vmem"))
    outs = [(nd, F32, ("late", s, prev[0] if prev else None, count)), ((4 * d, d), BF, carry(1)), ((2 * f, d), BF, carry(2)), ((16 + PAIRS, d), F32, "vmem")]
    scratch = [(nd, F32)] + [(nd, BF)] * 6
    return call(functools.partial(enc_back_kernel, bool(prev)), "encoder_back", args, outs, scratch, 35e9)


def dec_self_kernel(length, x, proj, out_w, pair_row, bias, gain, offset, x_low, q, k, v, mixed_t, lse, normed1, rstd1, v_t):
    x = x.get()

    def low(r):
        value = (x[r].astype(F32) + pair_row[...]).astype(BF)
        x_low.ref[r] = value
        return value

    project(x.shape[0], low, proj.get(), bias, q, k, v, v_t)
    x_low.send()
    mix_forward(q.ref, k.ref, v_t, length[0], True, mixed_t.ref, lse)
    mixed_t.send()
    out_w = out_w.get()

    def body(index):
        r = row_block(index)
        n1, s1 = norm_rows(x[r].astype(F32) + pair_row[...] + dot(mixed_t.ref[:, r], out_w[...], TN) + bias[2:3])
        normed1.ref[r] = n1.astype(normed1.ref.dtype)
        rstd1[r] = s1
        normed1.send(r)

    loop(x.shape[0] // RB, body)


def dec_self(length, x, s, pair_row, layer):
    proj, out_w, bias, w_in, c_in, w_out, c_out, gain, offset = layer
    count, n, d = x.shape
    nd = (n, d)
    args = [(length, "smem"), (x, ("late", s)), (proj, "late"), (out_w, "late")]
    args += [(v, "vmem") for v in (pair_row, bias, gain, offset)]
    outs = [(nd, BF, "late")] * 4 + [((d, n), BF, "late"), ((8, 1, n), F32, "vmem"), (nd, F32, "late"), ((n, 1), F32, "vmem")]
    return call(dec_self_kernel, "decoder_self", args, outs, [((d, n), BF)], 8e9)


def dec_mid_kernel(
    later, length, normed1, c_proj, memory, c_out, w_in, w_out, x, cot,
    pair_row, c_bias, c_gain, c_offset, c_in, c_out_b, gain, offset, place, *refs,
):
    earlier = refs[0] if later else None
    shown, grad_last, grad_first, d_memory, pack_b, pack_c, small = refs[later : later + 7]
    y_low, z_low, q, k, v, v_t, mixed_t, lse, normed2, rstd2, act, slope, grad_low, grad_mixed, d_q, d_k, d_v = refs[later + 7 :]
    begin_small(small, earlier)
    normed1, c_proj = normed1.get(), c_proj.get()
    count = normed1.shape[0]

    def queries(index):
        r = row_block(index)
        y = (normed1[r].astype(F32) * gain[0:1] + offset[0:1]).astype(BF)
        y_low[r] = y
        q[r] = (dot(y, c_proj[0]) + c_bias[0:1]).astype(BF)

    loop(count // RB, queries)
    memory = memory.get()
    span = memory.shape[0]

    def keys(index):
        r = row_block(index)
        m = memory[r]
        k[r] = dot(m, c_proj[1]).astype(BF)
        v[r] = (dot(m, c_proj[2]) + c_bias[1:2]).astype(BF)

    loop(span // RB, keys)
    v_t[...] = v[...].T
    mix_forward(q, k, v_t, length[0], False, mixed_t, lse)
    c_out, w_in, w_out, x, cot = c_out.get(), w_in.get(), w_out.get(), x.get(), cot.get()

    def forward(index):
        r = row_block(index)
        y = normed1[r].astype(F32) * gain[0:1] + offset[0:1]
        n2, s2 = norm_rows(y + dot(mixed_t[:, r], c_out[...], TN) + c_bias[2:3])
        normed2[r] = n2.astype(BF)
        rstd2[r] = s2
        z = n2 * c_gain[...] + c_offset[...]
        zl = z.astype(BF)
        z_low[r] = zl
        f = ffn_rows(zl, w_in, c_in, w_out, c_out_b, act, slope, r)
        n3, s3 = norm_rows(z + f + x[r].astype(F32) + pair_row[...])
        valid = valid_rows(index, length[1])
        shown.ref[r] = ((n3 * gain[1:2] + offset[1:2]) * valid).astype(BF)
        shown.send(r)
        g = cot[r].astype(F32) * valid
        small[9:10] += jnp.sum(g * n3, axis=0, keepdims=True)
        small[11:12] += jnp.sum(g, axis=0, keepdims=True)
        g = norm_rows_back(n3, s3, gain[1:2], g)
        grad_last.ref[r] = g
        grad_low[r] = g.astype(BF)

    loop(count // RB, forward)
    grad_last.send()

    def middle(r, grad):
        n2 = normed2[r].astype(F32)
        g = grad_last.ref[r] + grad
        small[8:9] += jnp.sum(g * n2, axis=0, keepdims=True)
        small[10:11] += jnp.sum(g, axis=0, keepdims=True)
        g = norm_rows_back(n2, rstd2[r], c_gain[...], g)
        grad_first.ref[r] = g
        grad_mixed[r] = g.astype(BF)

    ffn_back(grad_low, act, slope, z_low, w_in, w_out, pack_b, later, small, middle)
    grad_low[...] = grad_mixed[...]
    grad_mixed[...] = dot(grad_low[...], c_out[...], NT).astype(BF)
    if later:
        pack_c.begin.get()
    put(pack_c.ref, slice(1536, 2048), dot(mixed_t[...], grad_low[...]), later)
    mix_back(q, k, v, mixed_t, lse, grad_mixed, place, length[0], False, d_q, d_k, d_v)

    def back(index):
        r = row_block(index)
        d_memory.ref[r] = (dot(d_k[r], c_proj[1], NT) + dot(d_v[r], c_proj[2], NT)).astype(BF)
        d_memory.send(r)

    loop(span // RB, back)

    def first(index):
        r = row_block(index)
        grad_first.ref[r] += dot(d_q[r], c_proj[0], NT)
        grad_first.send(r)

    loop(count // RB, first)
    small[0:1] += jnp.sum(d_q[...].astype(F32), axis=0, keepdims=True)
    small[1:2] += jnp.sum(d_v[...].astype(F32), axis=0, keepdims=True)
    small[2:3] += jnp.sum(grad_low[...].astype(F32), axis=0, keepdims=True)
    m = memory[...]
    put(pack_c.ref, slice(0, 512), dot(y_low[...], d_q[...], TN), later)
    put(pack_c.ref, slice(512, 1024), dot(m, d_k[...], TN), later)
    put(pack_c.ref, slice(1024, 1536), dot(m, d_v[...], TN), later)
    pack_c.send()


def dec_mid(length, x, s, pair_row, normed1, memory, cot, layer, cross, place, prev):
    proj, out_w, bias, w_in, c_in, w_out, c_out, gain, offset = layer
    c_proj, c_out_w, c_bias, c_gain, c_offset = cross
    count, n, d = x.shape
    m = memory.shape[0]
    f = w_in.shape[1]
    nd, md = (n, d), (m, d)
    args = [(length, "smem")] + [(a, "late") for a in (normed1, c_proj, memory, c_out_w, w_in, w_out)]
    args += [(x, ("late", s)), (cot, ("late", s))]
    args += [(a, "vmem") for a in (pair_row, c_bias, c_gain, c_offset, c_in, c_out, gain, offset, place)]
    if prev:
        args.append((prev[6], "vmem"))
    carry = lambda i: ("from", prev[i]) if prev else "late"
    outs = [
        (nd, BF, ("late", s, prev[0] if prev else None, count)), (nd, F32, "late"), (nd, F32, "late"), (md, BF, "late"),
        ((2 * f, d), BF, carry(4)), ((4 * d, d), BF, carry(5)), ((16, d), F32, "vmem"),
    ]
    scratch = [(nd, BF), (nd, BF), (nd, BF), (md, BF), (md, BF), ((d, m), BF), ((d, n), BF), ((8, 1, n), F32), (nd, BF), ((n, 1), F32)]
    scratch += [((n, f), BF), ((n, f), BF), (nd, BF), (nd, BF), (nd, BF), (md, BF), (md, BF)]
    return call(functools.partial(dec_mid_kernel, bool(prev)), "decoder_middle", args, outs, scratch, 55e9)


def dec_self_back_kernel(
    later, length, grad_first, normed1, grad_last, out_w, mixed_t, q, k, v, x_low, proj,
    lse, rstd1, gain, place, middle_small, pair_mark, *refs,
):
    earlier = refs[0] if later else None
    d_x, pack_a, small, last, grad_low, grad_mixed, d_q, d_k, d_v, column = refs[later:]
    begin_small(small, earlier)
    for here in (3, 4, 5, 6, 7, 9, 11):
        small[here : here + 1] = middle_small[here : here + 1]
    column[...] = jnp.zeros(column.shape, F32)
    grad_first, normed1, grad_last = grad_first.get(), normed1.get(), grad_last.get()

    def top(index):
        r = row_block(index)
        n1 = normed1[r].astype(F32)
        g = grad_first[r].astype(F32)
        small[8:9] += jnp.sum(g * n1, axis=0, keepdims=True)
        small[10:11] += jnp.sum(g, axis=0, keepdims=True)
        g = norm_rows_back(n1, rstd1[r], gain[0:1], g)
        last[r] = grad_last[r].astype(F32) + g
        grad_low[r] = g.astype(BF)

    loop(last.shape[0] // RB, top)

    def rest(r, grad):
        g = last[r] + grad
        d_x.ref[r] = g
        d_x.send(r)
        column[0:1] += jnp.sum(g, axis=0, keepdims=True)

    self_back(x_low, proj, out_w, q, k, v, mixed_t, lse, place, length[0], True, grad_low, grad_mixed, d_q, d_k, d_v, pack_a, later, small, rest)
    small[16:] += pair_mark[...] * column[0:1]


def dec_self_back(length, s, count, grad_last, grad_first, layer, place, saved, middle_small, pair_mark, prev):
    proj, out_w, bias, w_in, c_in, w_out, c_out, gain, offset = layer
    x_low, q, k, v, mixed_t, lse, normed1, rstd1 = saved
    n, d = x_low.shape
    nd = (n, d)
    args = [(length, "smem")] + [(a, "late") for a in (grad_first, normed1, grad_last, out_w, mixed_t, q, k, v, x_low, proj)]
    args += [(a, "vmem") for a in (lse, rstd1, gain, place, middle_small, pair_mark)]
    if prev:
        args.append((prev[3], "vmem"))
    outs = [(nd, F32, ("late", s, prev[0] if prev else None, count)), ((4 * d, d), BF, ("from", prev[1]) if prev else "late"), ((16 + PAIRS, d), F32, "vmem")]
    scratch = [(nd, F32)] + [(nd, BF)] * 5 + [((8, d), F32)]
    return call(functools.partial(dec_self_back_kernel, bool(prev)), "decoder_self_back", args, outs, scratch, 20e9)


def add_rows(target, start, size, sources):
    block = max(b for b in range(16, min(size, 96) + 1, 16) if size % b == 0)

    def body(index):
        here = pl.ds(pl.multiple_of(start + index * block, 16), block)
        value = 0.0
        for ref, begin in sources:
            value = value + ref[pl.ds(pl.multiple_of(begin + index * block, 16), block)].astype(F32)
        target[here] = value.astype(BF)

    loop(size // block, body)


def grad_sum_kernel(count, rows1, rows2, a, b, c, own, mids, out, work, final, inbox, pairbox, load_sem, send_sem, recv_sem):
    m = count // 2
    me = lax.axis_index("dp")
    section = lax.axis_index("section")
    core = me % 2
    chip = me // 2
    decoder = section == 1
    na, nb, nc = a.shape[0], b.shape[0], c.shape[0]
    ns, nm = own.shape[0], mids.shape[0]
    loads = [
        pltpu.make_async_copy(a, work.at[pl.ds(0, na)], load_sem.at[0]),
        pltpu.make_async_copy(b, work.at[pl.ds(na, nb)], load_sem.at[1]),
        pltpu.make_async_copy(c, work.at[pl.ds(rows1, nc)], load_sem.at[2]),
    ]
    for copy in loads:
        copy.start()

    def device_at(place, core):
        place = place % m
        turn = place * (1 - core) + ((m - place) % m) * core
        odd = turn // (m // 2)
        return 2 * (2 * (turn * (1 - odd) + (m - 1 - turn) * odd) + odd) + core

    turn = (chip // 2) * (1 - chip % 2) + (m - 1 - chip // 2) * (chip % 2)
    back = (m - turn) % m
    place = turn * (1 - core) + back * core
    place_other = turn * core + back * (1 - core)
    other = me + 1 - 2 * core
    after = device_at(place + 1, core)
    before = device_at(place + m - 1, core)
    barrier = pltpu.get_barrier_semaphore()
    for device in (after, before, other):
        pl.semaphore_signal(barrier, inc=1, device_id={"dp": device}, device_id_type=MESH)
    pl.semaphore_signal(barrier, inc=1, device_id={"section": 1 - section}, device_id_type=MESH)
    pad1 = rows1 - na - nb
    work[na + nb : rows1] = jnp.concatenate([own[0:16], jnp.zeros((pad1 - 16, own.shape[1]), F32)]).astype(BF)
    pad2 = rows2 - nc
    work[rows1 + nc : rows1 + rows2] = jnp.concatenate(
        [mids[...], own[16:], jnp.zeros((pad2 - nm - ns + 16, own.shape[1]), F32)]
    ).astype(BF)
    for copy in loads:
        copy.wait()
    pl.semaphore_wait(barrier, 4)

    starts, chunks = (0, rows1), (rows1 // count, rows2 // count)
    units = []
    for region in range(2):
        first = chunks[region] // 32 * 16
        units += [(region, 0, first), (region, first, chunks[region] - first)]
    boxes, width = [], 0
    for _, _, size in units:
        boxes.append(width)
        width += size

    def low(region, half, chunk):
        return starts[region] + half * (m * chunks[region]) + (chunk % m) * chunks[region]

    slot = iter(range(10**6))

    def remote(src, dst, device):
        index = next(slot)
        return pltpu.make_async_remote_copy(
            src, dst, send_sem.at[index], recv_sem.at[index], device_id=device, device_id_type=MESH
        )

    def rows(ref, start, size):
        return ref.at[pl.ds(pl.multiple_of(start, 16), size)]

    def on_decoder(region, action):
        if region == 0:
            action()
        else:
            pl.when(decoder)(action)

    def pair_copy(region, t):
        size = chunks[region]
        start = low(region, 1 - core, place_other + 2 * m - 1 - t)
        return remote(rows(work, start, size), rows(pairbox, start - (1 - core) * m * size - starts[region] + (region * m * chunks[0]), size), {"dp": other})

    def pair_low(region, chunk):
        return region * m * chunks[0] + (chunk % m) * chunks[region]

    pairs = [[pair_copy(region, t) for region in range(2)] for t in range(m)]
    for t in range(m):
        for region in range(2):
            on_decoder(region, pairs[t][region].start)
    sends = [[None] * len(units) for _ in range(m - 1)]
    for s in range(m - 1):
        for u, (region, offset, size) in enumerate(units):
            start = low(region, core, place + 2 * m - 1 - s) + offset
            sends[s][u] = remote(rows(work, start, size), inbox.at[pl.ds(s * width + boxes[u], size)], {"dp": after})
    for t in range(m):
        for region in range(2):
            on_decoder(region, pairs[t][region].wait_recv)
        for u, (region, offset, size) in enumerate(units):
            chunk = place + 2 * m - 1 - t

            def step(t=t, u=u, region=region, offset=offset, size=size, chunk=chunk):
                start = low(region, core, chunk) + offset
                sources = [(work, start), (pairbox, pair_low(region, chunk) + offset)]
                if t:
                    sends[t - 1][u].wait_recv()
                    sources.append((inbox, (t - 1) * width + boxes[u]))
                add_rows(work if t < m - 1 else final, start, size, sources)
                if t < m - 1:
                    sends[t][u].start()

            on_decoder(region, step)

    mine = rows(final, low(1, core, place), chunks[1])
    across = remote(mine, mine, {"section": 1 - section})
    pl.when(decoder)(across.start)
    passes = [[None] * len(units) for _ in range(m - 1)]
    for s in range(m - 1):
        for u, (region, offset, size) in enumerate(units):
            here = rows(final, low(region, core, place + 2 * m - s) + offset, size)
            passes[s][u] = remote(here, here, {"dp": after})
    shares = []
    for s in range(m):
        for region in range(2):
            here = rows(final, low(region, core, place + 2 * m - s), chunks[region])
            shares.append(remote(here, here, {"dp": other}))
    for s in range(m):
        for u, (region, offset, size) in enumerate(units):
            if s:
                passes[s - 1][u].wait_recv()
            elif u == 2:
                pl.when(section == 0)(across.wait_recv)
            if s < m - 1:
                passes[s][u].start()
            if offset:
                shares[2 * s + region].start()
    for copy in shares:
        copy.wait_recv()
    copy = pltpu.make_async_copy(final, out, load_sem.at[0])
    copy.start()
    for t in range(m):
        for region in range(2):
            on_decoder(region, pairs[t][region].wait_send)
    for s in range(m - 1):
        for u, (region, _, _) in enumerate(units):
            on_decoder(region, sends[s][u].wait_send)
            passes[s][u].wait_send()
    for share in shares:
        share.wait_send()
    pl.when(decoder)(across.wait_send)
    copy.wait()


def grad_sum(count, a, b, c, own, mids):
    d = a.shape[1]
    unit = 16 * count
    m = count // 2
    rows1 = -(-(a.shape[0] + b.shape[0] + 16) // unit) * unit
    rows2 = -(-(c.shape[0] + own.shape[0] - 16 + mids.shape[0]) // unit) * unit
    width = (rows1 + rows2) // count
    slots = (m - 1) * 8 + m * 4 + 1
    anywhere = pl.BlockSpec(memory_space=pl.ANY)
    inside = pl.BlockSpec(memory_space=pltpu.VMEM)
    out = pl.pallas_call(
        functools.partial(grad_sum_kernel, count, rows1, rows2),
        name="gradient_sum",
        out_shape=sds((rows1 + rows2, d), BF),
        in_specs=[anywhere] * 3 + [inside] * 2,
        out_specs=anywhere,
        scratch_shapes=[
            vm((rows1 + rows2, d), BF),
            vm((rows1 + rows2, d), BF),
            vm(((m - 1) * width, d), BF),
            vm((m * width, d), BF),
            pltpu.SemaphoreType.DMA((3,)),
            pltpu.SemaphoreType.DMA((slots,)),
            pltpu.SemaphoreType.DMA((slots,)),
        ],
        compiler_params=pltpu.CompilerParams(collective_id=0, has_side_effects=True, vmem_limit_bytes=48 * 2**20),
    )(a, b, c, own, mids)
    return out, rows1


def unpack_kernel(rows1, f, pack, proj, out_w, bias, w_in, b_in, w_out, b_out, gain, offset, c_proj, c_out, c_bias, c_gain, c_offset, pair):
    d = pack.shape[1]

    def put_rows(target, start, size):
        target[...] = pack[start : start + size].astype(F32)

    put_rows(proj, 0, 3 * d)
    put_rows(out_w, 3 * d, d)
    for c in range(f // d):
        w_in[:, c * d : (c + 1) * d] = pack[(4 + c) * d : (5 + c) * d].astype(F32)
    put_rows(w_out, 4 * d + f, f)
    put_rows(c_proj, rows1, 3 * d)
    put_rows(c_out, rows1 + 3 * d, d)
    small = pack[4 * d + 2 * f : 4 * d + 2 * f + 16].astype(F32)
    bias[...] = small[0:3]
    for c in range(f // d):
        b_in[:, c * d : (c + 1) * d] = small[3 + c : 4 + c]
    b_out[...] = small[7:8]
    gain[...] = small[8:10]
    offset[...] = small[10:12]
    small = pack[rows1 + 4 * d : rows1 + 4 * d + 32].astype(F32)
    c_bias[...] = small[0:3]
    c_gain[...] = small[8:9]
    c_offset[...] = small[10:11]
    pair[...] = small[16 : 16 + pair.shape[0]]


def unpack(pack, rows1, f, pairs):
    d = pack.shape[1]
    inside = pl.BlockSpec(memory_space=pltpu.VMEM)
    shapes = [(3 * d, d), (d, d), (3, d), (d, f), (1, f), (f, d), (1, d), (2, d), (2, d), (3 * d, d), (d, d), (3, d), (1, d), (1, d), (pairs, d)]
    return pl.pallas_call(
        functools.partial(unpack_kernel, rows1, f),
        name="unpack",
        out_shape=[sds(s, F32) for s in shapes],
        in_specs=[inside],
        out_specs=[inside] * len(shapes),
        compiler_params=pltpu.CompilerParams(vmem_limit_bytes=50 * 2**20),
    )(pack)


def nothing(*refs):
    pass


def blank(*shapes):
    spec = pl.BlockSpec(memory_space=pl.ANY)
    return pl.pallas_call(nothing, name="blank", out_shape=[sds(*s) for s in shapes], out_specs=[spec] * len(shapes))()


def per_device(
    embeds, cotangent, pair_ids, seq_lengths, alive_count,
    self_proj, self_out, self_bias, ffn_in, ffn_in_bias, ffn_out, ffn_out_bias, norm_gain, norm_bias,
    cross_proj, cross_out, cross_bias, cross_norm_gain, cross_norm_bias, pair_embed,
):
    layer = (self_proj[0], self_out[0], self_bias[0], ffn_in[0], ffn_in_bias, ffn_out[0], ffn_out_bias, norm_gain[0], norm_bias[0])
    cross = (cross_proj, cross_out, cross_bias, cross_norm_gain[None], cross_norm_bias[None])
    place = jnp.asarray(place_matrix(), BF)
    section_zero = lax.axis_index("section") == 0
    x, cot = embeds[0], cotangent[0]
    count, n, d = x.shape
    f = ffn_in.shape[2]
    live = (jnp.arange(count) < alive_count[0])[None, :]
    valid = jnp.where(live, seq_lengths, 0)
    pairs = pair_embed.shape[0]
    onehot = (pair_ids[:, None] == jnp.arange(pairs)[None, :]).astype(F32)
    pair_rows = jnp.dot(onehot, pair_embed, precision=lax.Precision.HIGHEST)
    src = [jnp.stack([seq_lengths[0, s], valid[0, s]]) for s in range(count)]
    tgt = [jnp.stack([seq_lengths[1, s], valid[1, s]]) for s in range(count)]
    mid = [jnp.stack([seq_lengths[0, s], valid[1, s]]) for s in range(count)]
    nd, nf, n1 = (n, d), (n, f), (n, 1)

    def first(s, prev):
        def enc():
            memory, shown, q, k, v, mt, lse, na, ra, act, slope, nb, rb = enc_forward(src[s], x, s, layer, prev)
            (wide,) = blank((nd, F32))
            return memory, shown, q, k, v, mt, lse, ra, na, wide, act, slope, nb, rb

        def dec():
            low, q, k, v, mt, lse, na, ra = dec_self(tgt[s], x, s, pair_rows[s : s + 1], layer)
            memory, shown, act, slope, nb, rb = blank((nd, BF), ((count, *nd), BF), (nf, BF), (nf, BF), (nd, BF), (n1, F32))
            return memory, shown, q, k, v, mt, lse, ra, low, na, act, slope, nb, rb

        return lax.cond(section_zero, enc, dec)

    def middle(s, saved, memory, prev):
        def enc():
            return (shown, *blank((nd, F32), (nd, F32), (nd, BF), ((2 * f, d), BF), ((4 * d, d), BF), ((16, d), F32)))

        def dec():
            return tuple(dec_mid(mid[s], x, s, pair_rows[s : s + 1], saved[9], memory, cot, layer, cross, place, prev))

        return lax.cond(section_zero, enc, dec)

    def last(s, saved, done, d_memory, prev):
        _, _, q, k, v, mt, lse, ra, na, wide, act, slope, nb, rb = saved

        def enc():
            return tuple(enc_back(src[s], x, s, d_memory, cot, layer, place, (q, k, v, mt, lse, na, ra, act, slope, nb, rb), prev))

        def dec():
            d_x, pack_a, small = dec_self_back(
                tgt[s], s, count, done[1], done[2], layer, place, (na, q, k, v, mt, lse, wide, ra), done[6], onehot[s][:, None], prev
            )
            return d_x, pack_a, done[4], small

        return lax.cond(section_zero, enc, dec)

    ahead = [(0, 1)]
    behind = [(1, 0)]
    saved, memory, done, grads, d_memory = [], [], [], [], []
    for s in range(count):
        saved.append(first(s, saved[s - 1][1] if s else None))
        memory.append(lax.ppermute(saved[s][0], "section", ahead))
    shown = saved[-1][1]
    for s in range(count):
        done.append(middle(s, saved[s], memory[s], done[s - 1] if s else ()))
        d_memory.append(lax.ppermute(done[s][3], "section", behind))
    for s in range(count):
        grads.append(last(s, saved[s], done[s], d_memory[s], grads[s - 1] if s else ()))
    shown, d_x = done[-1][0], grads[-1][0]
    pack, rows1 = grad_sum(lax.axis_size("dp"), grads[-1][1], grads[-1][2], done[-1][5], grads[-1][3], done[-1][6])
    proj, out_w, bias, w_in, b_in, w_out, b_out, gain, offset, c_proj, c_out, c_bias, c_gain, c_offset, pair = unpack(pack, rows1, f, pairs)
    return (
        shown[None], d_x[None], proj.reshape(1, 3, d, d), out_w[None], bias[None], w_in[None], b_in, w_out[None], b_out, gain[None], offset[None],
        c_proj.reshape(3, d, d), c_out, c_bias, c_gain[0], c_offset[0], pair,
    )


def solution(mesh):
    s, r = "section", P()
    in_specs = (
        P(s, "dp"), P(s, "dp"), P("dp"), P(None, "dp"), P("dp"),
        P(s), P(s), P(s), P(s), P(s), P(s), P(s), P(s), P(s), r, r, r, r, r, r,
    )
    out_specs = (P(s, "dp"), P(s, "dp"), P(s), P(s), P(s), P(s), P(s), P(s), P(s), P(s), P(s), r, r, r, r, r, r)
    return jax.shard_map(per_device, mesh=mesh, in_specs=in_specs, out_specs=out_specs, check_vma=False)
```

```python
import functools

import jax
import jax.numpy as jnp
import numpy as np
from jax import lax
from jax.experimental import pallas as pl
from jax.experimental.pallas import tpu as pltpu
from jax.sharding import PartitionSpec as P

BF = jnp.bfloat16
F32 = jnp.float32
HEADS = 8
PAIRS = 16
MESH = pl.DeviceIdType.MESH
EPSILON = 1e-05
BLOCKED = -1e30
RB = 512
NN = (((1,), (0,)), ((), ()))
NT = (((1,), (1,)), ((), ()))
TN = (((0,), (0,)), ((), ()))


def dot(left, right, dims=NN):
    return lax.dot_general(left, right, dims, preferred_element_type=F32)


def row_block(index, size=RB):
    return pl.ds(pl.multiple_of(index * size, size), size)


def loop(count, body, unroll=1):
    def step(index, carry):
        body(index)
        return carry

    lax.fori_loop(0, count, step, 0, unroll=unroll)


def lanes_of(half):
    lane = lax.broadcasted_iota(jnp.int32, (1, 128), 1)
    inside = (lane // 64) == half
    spare = lane - 64 * (1 - half)
    ones = (~inside) & (spare < 32)
    block = (~inside) & (spare >= 32)
    flag = (~inside) & (spare == 32)
    return tuple(m.astype(F32) for m in (inside, ones, block, flag))


def norm_rows(value):
    centre = jnp.mean(value, -1, keepdims=True)
    centred = value - centre
    rstd = lax.rsqrt(jnp.mean(centred * centred, -1, keepdims=True) + EPSILON)
    return centred * rstd, rstd


def norm_rows_back(normed, rstd, gain, grad):
    scaled = grad * gain
    return rstd * (
        scaled
        - jnp.mean(scaled, -1, keepdims=True)
        - normed * jnp.mean(scaled * normed, -1, keepdims=True)
    )


def gelu_both(hidden):
    phi = 0.5 + 0.5 * lax.erf(hidden * 0.7071067811865476)
    bell = jnp.exp(-0.5 * hidden * hidden)
    return hidden * phi, phi + hidden * (bell * 0.3989422804014327)


def key_fill(count, length, ones, block):
    position = lax.broadcasted_iota(jnp.int32, (count, 128), 0)
    return ones + jnp.where(position < length, 0.0, BLOCKED) * block


def causal_cut(scores, query_axis):
    query = lax.broadcasted_iota(jnp.int32, scores.shape, query_axis)
    key = lax.broadcasted_iota(jnp.int32, scores.shape, 1 - query_axis)
    return jnp.where(key <= query, scores, BLOCKED)


def mix_forward(queries, keys, values_t, length, causal, mixed_t, lse):
    count = queries.shape[0]
    span = keys.shape[0]
    size = min(512 if causal else 1024, count)

    def pair(index):
        cols = row_block(index, 128)
        q = queries[:, cols].astype(F32) * 0.125
        k = keys[:, cols].astype(F32)
        vt = values_t[cols, :].astype(F32)
        lane = lax.broadcasted_iota(jnp.int32, (128, 1), 0)
        qa, ka, va = [], [], []
        for half in range(2):
            inside, ones, block, flag = lanes_of(half)
            qa.append((q * inside + flag).astype(BF))
            ka.append((k * inside + key_fill(span, length, ones, block)).astype(BF))
            va.append(jnp.where((lane // 64) == half, vt, 1.0).astype(BF))

        def scores_of(part, half):
            here = slice(part * size, (part + 1) * size)
            pieces = [(0, part * size, False), (part * size, size, True)] if causal else [(0, span, False)]
            return [
                (start, reach, cut, dot(ka[half][start : start + reach], qa[half][here], NT))
                for start, reach, cut in pieces
                if reach
            ]

        def finish(part, half, scores):
            here = slice(part * size, (part + 1) * size)
            scores = [(start, reach, causal_cut(s, 1) if cut else s) for start, reach, cut, s in scores]
            top = None
            for _, _, s in scores:
                best = jnp.max(s, axis=0, keepdims=True)
                top = best if top is None else jnp.maximum(top, best)
            total = None
            for start, reach, s in scores:
                o = dot(va[half][:, start : start + reach], jnp.exp(s - top).astype(BF))
                total = o if total is None else total + o
            other = 64 * (1 - half)
            mass = total[other : other + 1]
            own = total[64 * half : 64 * half + 64] / mass
            mixed_t[pl.ds(pl.multiple_of(index * 128 + 64 * half, 64), 64), here] = own.astype(BF)
            lse[index * 2 + half, :, here] = top + jnp.log(mass)

        waiting = None
        for tile in [(part, half) for part in range(count // size) for half in range(2)]:
            scores = scores_of(*tile)
            if waiting:
                finish(*waiting)
            waiting = (*tile, scores)
        finish(*waiting)

    loop(4, pair, 2)


def split3(value):
    high = value.astype(BF).astype(F32)
    middle = (value - high).astype(BF).astype(F32)
    low = (value - high - middle).astype(BF).astype(F32)
    return high, middle, low


def place_matrix():
    out = np.zeros((16, 512), np.float32)
    for half in range(2):
        other = 64 * (1 - half)
        for piece in range(3):
            out[half * 4 + piece, half * 128 + other + piece] = 1
            out[8 + half * 4 + piece, 256 + half * 128 + other + piece] = 1
        out[half * 4 + 3, half * 128 + other + 32] = 1
    return out


def mix_back(queries, keys, values, mixed_t, lse, grad_mixed, place, length, causal, d_q, d_k, d_v):
    count = queries.shape[0]
    span = keys.shape[0]
    size = 256 if causal else min(512, count)

    def pair(index):
        cols = row_block(index, 128)
        q = queries[:, cols].astype(F32) * 0.125
        k_low = keys[:, cols]
        k = k_low.astype(F32)
        v = values[:, cols].astype(F32)
        g_low = grad_mixed[:, cols]
        g = g_low.astype(F32)
        q_t = q.astype(BF).T
        g_t = g_low.T
        product = g_t.astype(F32) * mixed_t[cols, :].astype(F32)
        row = lax.broadcasted_iota(jnp.int32, (16, count), 0)
        spread = jnp.where((row == 3) | (row == 7), 1.0, 0.0)
        for half in range(2):
            shift = -lse[index * 2 + half]
            delta = -jnp.sum(product[64 * half : 64 * half + 64], axis=0, keepdims=True)
            for base, value in ((0, shift), (8, delta)):
                for piece, part in enumerate(split3(value)):
                    spread = jnp.where(row == base + 4 * half + piece, part, spread)
        extra = dot(spread.astype(BF), place[...], TN)
        qa, ka, va, ga = [], [], [], []
        for half in range(2):
            inside, ones, block, flag = lanes_of(half)
            qa.append((q * inside + extra[:, half * 128 : half * 128 + 128]).astype(BF))
            ga.append((g * inside + extra[:, 256 + half * 128 : 384 + half * 128]).astype(BF))
            ka.append((k * inside + key_fill(span, length, ones, block)).astype(BF))
            va.append((v * inside + (1.0 - inside)).astype(BF))
        lane = lax.broadcasted_iota(jnp.int32, (size, 128), 1)
        total_k = [None, None]
        total_v = [None, None]

        def grow(total, value):
            if total is None:
                return value
            if total.shape == value.shape:
                return total + value
            known = total.shape[1]
            return jnp.concatenate([total + value[:, :known], value[:, known:]], axis=1)

        for part in range(count // size):
            here = slice(part * size, (part + 1) * size)
            reach = (part + 1) * size if causal else span
            out_q = []
            for half in range(2):
                s = dot(qa[half][here], ka[half][:reach], NT)
                if causal:
                    if part:
                        s = jnp.concatenate([s[:, : part * size], causal_cut(s[:, part * size :], 0)], axis=1)
                    else:
                        s = causal_cut(s, 0)
                probs = jnp.exp(s)
                grads = dot(ga[half][here], va[half][:reach], NT)
                probs_low = probs.astype(BF)
                d_s = (probs * grads).astype(BF)
                total_v[half] = grow(total_v[half], dot(g_t[:, here], probs_low))
                total_k[half] = grow(total_k[half], dot(q_t[:, here], d_s))
                out_q.append(dot(d_s, k_low[:reach]))
            d_q[here, cols] = (jnp.where(lane < 64, out_q[0], out_q[1]) * 0.125).astype(BF)
        for target, total in ((d_k, total_k), (d_v, total_v)):
            joined = jnp.concatenate([total[0][:64], total[1][64:]], axis=0).astype(BF)
            target[:, cols] = joined.T

    loop(4, pair, 2)


class Late:
    def __init__(self, ref, copy):
        self.ref, self.copy = ref, copy

    def get(self):
        if self.copy is not None:
            self.copy.wait()
            self.copy = None
        return self.ref


class Limits:
    def __init__(self, ref, picks):
        self.ref, self.picks = ref, picks

    def __getitem__(self, index):
        if len(self.picks) == 2:
            near, far = self.picks
            return self.ref[near[index] + lax.axis_index("section") * (far[index] - near[index])]
        return self.ref[self.picks[index]]


class Pieces:
    def __init__(self, source, ref, sem):
        self.source, self.ref, self.sem = source, ref, sem

    def wait(self):
        pltpu.make_async_copy(self.source.at[pl.ds(0, self.ref.shape[0])], self.ref, self.sem).wait()


class Leaving:
    def __init__(self, ref, out, sem):
        self.ref, self.out, self.sem = ref, out, sem

    def send(self, rows=None):
        if rows is None:
            pltpu.make_async_copy(self.ref, self.out, self.sem).start()
        else:
            pltpu.make_async_copy(self.ref.at[rows], self.out.at[rows], self.sem).start()

    def part(self, index):
        return Leaving(self.ref.at[index], self.out.at[index], self.sem)

    def finish(self):
        pltpu.make_async_copy(self.ref, self.out, self.sem).wait()


def sds(shape, dtype):
    return jax.ShapeDtypeStruct(shape, dtype)


def vm(shape, dtype):
    return pltpu.VMEM(shape, dtype)


def call(kernel, name, scalars, picks, args, outs, scratch, flops):
    anywhere = pl.BlockSpec(memory_space=pl.ANY)
    inside = pl.BlockSpec(memory_space=pltpu.VMEM)
    operands, in_specs, out_shapes, out_specs, memory, aliases = [], [], [], [], [], {}
    plan_in, plan_out, places = [], [], []
    for value, kind in args:
        places.append(len(operands))
        operands.append(value)
        if kind == "vmem":
            in_specs.append(inside)
            plan_in.append(None)
        else:
            in_specs.append(anywhere)
            if kind[0] == "either":
                _, index, other, other_index = kind
                plan_in.append((len(memory), (index, len(operands), other_index)))
                operands.append(other)
                in_specs.append(anywhere)
                memory.append(vm(value.shape if index is None else value.shape[1:], value.dtype))
                continue
            if kind[0] == "rows":
                plan_in.append((len(memory), kind[2]))
                memory.append(vm(kind[1], value.dtype))
                continue
            index = kind[1] if isinstance(kind, tuple) else None
            plan_in.append((len(memory), index))
            memory.append(vm(value.shape if index is None else value.shape[1:], value.dtype))
    for position, (shape, dtype, kind) in enumerate(outs):
        if kind == "vmem":
            out_shapes.append(sds(shape, dtype))
            out_specs.append(inside)
            plan_out.append(None)
            continue
        out_specs.append(anywhere)
        index, earlier = None, None
        if isinstance(kind, tuple) and kind[0] == "late":
            index, earlier, total = kind[1:]
            out_shapes.append(sds((total, *shape), dtype))
            if earlier is not None:
                aliases[len(operands)] = position
                operands.append(earlier)
                in_specs.append(anywhere)
        else:
            out_shapes.append(sds(shape, dtype))
        plan_out.append((len(memory), index, len(operands) if isinstance(kind, tuple) and kind[0] == "from" else None))
        memory.append(vm(shape, dtype))
        if isinstance(kind, tuple) and kind[0] == "from":
            operands.append(kind[1])
            in_specs.append(anywhere)
    total_in, count_out, count_memory = len(operands), len(outs), len(memory)

    def body(numbers, *refs):
        ins, results = refs[:total_in], refs[total_in : total_in + count_out]
        held = refs[total_in + count_out : total_in + count_out + count_memory]
        own = refs[total_in + count_out + count_memory : -1]
        sems = refs[-1]
        first, last = [], []
        for spot, plan in zip(places, plan_in):
            ref = ins[spot]
            if plan is None:
                first.append(ref)
                continue
            where, index = plan
            if isinstance(index, tuple):
                index, other, other_index = index
                copies = [
                    pltpu.make_async_copy(r if i is None else r.at[i], held[where], sems.at[where])
                    for r, i in ((ref, index), (ins[other], other_index))
                ]
                section = lax.axis_index("section")
                pl.when(section == 0)(copies[0].start)
                pl.when(section == 1)(copies[1].start)
                first.append(Late(held[where], copies[0]))
                continue
            if isinstance(index, list):
                for begin, end, size in index:
                    pltpu.make_async_copy(ref.at[pl.ds(begin, size)], held[where].at[pl.ds(end, size)], sems.at[where]).start()
                first.append(Late(held[where], Pieces(ref, held[where], sems.at[where])))
                continue
            copy = pltpu.make_async_copy(ref if index is None else ref.at[index], held[where], sems.at[where])
            copy.start()
            first.append(Late(held[where], copy))
        for ref, plan in zip(results, plan_out):
            if plan is None:
                last.append(ref)
                continue
            where, index, source = plan
            leaving = Leaving(held[where], ref if index is None else ref.at[index], sems.at[where])
            if source is not None:
                copy = pltpu.make_async_copy(ins[source], held[where], sems.at[where])
                copy.start()
                leaving.begin = Late(held[where], copy)
            last.append(leaving)
        kernel(Limits(numbers, picks), *first, *last, *own)
        for leaving in last:
            if isinstance(leaving, Leaving):
                leaving.finish()

    return pl.pallas_call(
        body,
        name=name,
        out_shape=out_shapes,
        in_specs=[pl.BlockSpec(memory_space=pltpu.SMEM), *in_specs],
        out_specs=out_specs,
        scratch_shapes=[*memory, *[vm(*s) for s in scratch], pltpu.SemaphoreType.DMA((max(count_memory, 1),))],
        input_output_aliases={i + 1: o for i, o in aliases.items()},
        compiler_params=pltpu.CompilerParams(vmem_limit_bytes=62 * 2**20),
        cost_estimate=pl.CostEstimate(flops=int(flops), bytes_accessed=20 * 2**20, transcendentals=0),
    )(scalars, *operands)


def valid_rows(index, limit, size=RB):
    return (lax.broadcasted_iota(jnp.int32, (size, 1), 0) + index * size < limit).astype(F32)


def ffn_rows(z_low, w_in, c_in, w_out, c_out, act_ref, slope_ref, r, flipped=False):
    def hidden(c):
        cols = slice(c * 512, c * 512 + 512)
        return dot(z_low, w_in[cols], NT) + c_in[c : c + 1] if flipped else dot(z_low, w_in[:, cols]) + c_in[:, cols]

    total, coming = None, hidden(0)
    for c in range(4):
        cols = slice(c * 512, c * 512 + 512)
        here = coming
        coming = hidden(c + 1) if c < 3 else None
        act, slope = gelu_both(here)
        act = act.astype(BF)
        act_ref[r, cols] = act
        slope_ref[r, cols] = slope.astype(BF)
        part = dot(act, w_out[cols])
        total = part if total is None else total + part
    return total + c_out[...]


def put(target, rows, value, later):
    target[rows] = (value + target[rows].astype(F32) if later else value).astype(BF)


def ffn_back(grad_low, act, slope, z_low, w_in, w_out, put_rows, small, on_rows, flipped=False):
    def body(index):
        r = row_block(index)
        g = grad_low[r]
        total, coming = None, dot(g, w_out[0:512], NT)
        for c in range(4):
            cols = slice(c * 512, c * 512 + 512)
            here = coming
            coming = dot(g, w_out[512 * c + 512 : 512 * c + 1024], NT) if c < 3 else None
            dh = (here * slope[r, cols].astype(F32)).astype(BF)
            slope[r, cols] = dh
            small[3 + c : 4 + c] += jnp.sum(dh.astype(F32), axis=0, keepdims=True)
            part = dot(dh, w_in[cols]) if flipped else dot(dh, w_in[:, cols], NT)
            total = part if total is None else total + part
        small[7:8] += jnp.sum(g.astype(F32), axis=0, keepdims=True)
        on_rows(r, total)

    loop(grad_low.shape[0] // RB, body)
    z = z_low[...]
    g = grad_low[...]
    act = act.get() if isinstance(act, Late) else act
    for c in range(4):
        cols = slice(c * 512, c * 512 + 512)
        put_rows(c * 512, dot(z, slope[:, cols], TN))
        put_rows(2048 + c * 512, dot(act[:, cols], g, TN))


def project(count, x_low, proj, bias, q, k, v, v_t):
    def body(index):
        r = row_block(index)
        x = x_low(r)
        q.ref[r] = (dot(x, proj[0]) + bias[0:1]).astype(BF)
        k.ref[r] = dot(x, proj[1]).astype(BF)
        v.ref[r] = (dot(x, proj[2]) + bias[1:2]).astype(BF)

    loop(count // RB, body)
    q.send()
    k.send()
    v.send()
    v_t[...] = v.ref[...].T


def self_back(x, proj, out_w, q, k, v, mixed_t, lse, place, length, causal, grad_low, grad_mixed, d_q, d_k, d_v, pack, later, small, rest):
    grad_mixed[...] = dot(grad_low[...], out_w.get()[...], NT).astype(BF)
    mixed_t = mixed_t.get()
    if later:
        pack.begin.get()
    put(pack.ref, slice(1536, 2048), dot(mixed_t[...], grad_low[...]), later)
    q, k, v, x = q.get(), k.get(), v.get(), x.get()
    mix_back(q, k, v, mixed_t, lse, grad_mixed, place, length, causal, d_q, d_k, d_v)
    small[0:1] += jnp.sum(d_q[...].astype(F32), axis=0, keepdims=True)
    small[1:2] += jnp.sum(d_v[...].astype(F32), axis=0, keepdims=True)
    small[2:3] += jnp.sum(grad_low[...].astype(F32), axis=0, keepdims=True)
    xl = x[...]
    put(pack.ref, slice(0, 512), dot(xl, d_q[...], TN), later)
    put(pack.ref, slice(512, 1024), dot(xl, d_k[...], TN), later)
    put(pack.ref, slice(1024, 1536), dot(xl, d_v[...], TN), later)
    pack.send()
    proj = proj.get()

    def body(index):
        r = row_block(index)
        rest(r, dot(d_q[r], proj[0], NT) + dot(d_k[r], proj[1], NT) + dot(d_v[r], proj[2], NT))

    loop(x.shape[0] // RB, body)


def begin_small(small, earlier):
    small[...] = jnp.zeros(small.shape, F32) if earlier is None else earlier[...]


def enc_forward_kernel(
    length, x, proj, out_w, w_in, w_out, bias, c_in, c_out, gain, offset,
    memory, shown, q, k, v, mixed_t, lse, normed1, rstd1, act, slope, normed2, rstd2, v_t,
):
    x = x.get()
    project(x.shape[0], lambda r: x[r], proj.get(), bias, q, k, v, v_t)
    mix_forward(q.ref, k.ref, v_t, length[0], False, mixed_t.ref, lse)
    mixed_t.send()
    out_w, w_in, w_out = out_w.get(), w_in.get(), w_out.get()

    def body(index):
        r = row_block(index)
        xf = x[r].astype(F32)
        n1, s1 = norm_rows(xf + dot(mixed_t.ref[:, r], out_w[...], TN) + bias[2:3])
        normed1.ref[r] = n1.astype(BF)
        rstd1[r] = s1
        y = n1 * gain[0:1] + offset[0:1]
        f = ffn_rows(y.astype(BF), w_in, c_in, w_out, c_out, act.ref, slope.ref, r)
        n2, s2 = norm_rows(y + f + xf)
        normed2.ref[r] = n2.astype(BF)
        rstd2[r] = s2
        result = n2 * gain[1:2] + offset[1:2]
        memory.ref[r] = result.astype(BF)
        shown.ref[r] = (result * valid_rows(index, length[1])).astype(BF)
        for leaving in (act, slope, memory, shown, normed1, normed2):
            leaving.send(r)

    loop(x.shape[0] // RB, body)


def enc_forward(scalars, picks, x, s, layer, shown):
    proj, out_w, bias, w_in, c_in, w_out, c_out, gain, offset = layer
    count, n, d = x.shape
    f = w_in.shape[1]
    nd = (n, d)
    args = [(x, ("late", s)), (proj, "late"), (out_w, "late"), (w_in, "late"), (w_out, "late")]
    args += [(v, "vmem") for v in (bias, c_in, c_out, gain, offset)]
    outs = [
        (nd, BF, "late"), (nd, BF, ("late", s, shown, count)), (nd, BF, "late"), (nd, BF, "late"), (nd, BF, "late"), ((d, n), BF, "late"),
        ((8, 1, n), F32, "vmem"), (nd, BF, "late"), ((n, 1), F32, "vmem"), ((n, f), BF, "late"), ((n, f), BF, "late"), (nd, BF, "late"), ((n, 1), F32, "vmem"),
    ]
    return call(enc_forward_kernel, "encoder_forward", scalars, picks, args, outs, [((d, n), BF)], 15e9)


def enc_back_kernel(
    later, length, cot, d_memory, normed2, normed1, w_out, slope, w_in, act, out_w, mixed_t, q, k, v, x, proj,
    lse, rstd1, rstd2, gain, offset, place, *refs,
):
    earlier = refs[0] if later else None
    d_x, pack_a, pack_b, small, last, grad_low, z_low, grad_mixed, d_q, d_k, d_v = refs[later:]
    begin_small(small, earlier)
    cot, d_memory, normed2, normed1 = cot.get(), d_memory.get(), normed2.get(), normed1.get()

    def top(index):
        r = row_block(index)
        n2 = normed2[r].astype(F32)
        g = cot[r].astype(F32) * valid_rows(index, length[1]) + d_memory[r].astype(F32)
        small[9:10] += jnp.sum(g * n2, axis=0, keepdims=True)
        small[11:12] += jnp.sum(g, axis=0, keepdims=True)
        g = norm_rows_back(n2, rstd2[r], gain[1:2], g)
        last[r] = g
        grad_low[r] = g.astype(BF)
        z_low[r] = (normed1[r].astype(F32) * gain[0:1] + offset[0:1]).astype(BF)

    loop(last.shape[0] // RB, top)

    def middle(r, grad):
        n1 = normed1[r].astype(F32)
        g = last[r] + grad
        small[8:9] += jnp.sum(g * n1, axis=0, keepdims=True)
        small[10:11] += jnp.sum(g, axis=0, keepdims=True)
        g = norm_rows_back(n1, rstd1[r], gain[0:1], g)
        last[r] = last[r] + g
        grad_mixed[r] = g.astype(BF)

    def put_rows(start, value):
        if later:
            pack_b.begin.get()
        put(pack_b.ref, slice(start, start + 512), value, later)

    ffn_back(grad_low, act, slope.get(), z_low, w_in.get(), w_out.get(), put_rows, small, middle)
    pack_b.send()
    grad_low[...] = grad_mixed[...]

    def rest(r, grad):
        d_x.ref[r] = last[r] + grad
        d_x.send(r)

    self_back(x, proj, out_w, q, k, v, mixed_t, lse, place, length[0], False, grad_low, grad_mixed, d_q, d_k, d_v, pack_a, later, small, rest)


def enc_back(scalars, picks, x, s, d_memory, cot, layer, place, saved, prev):
    proj, out_w, bias, w_in, c_in, w_out, c_out, gain, offset = layer
    q, k, v, mixed_t, lse, normed1, rstd1, act, slope, normed2, rstd2 = saved
    count, n, d = x.shape
    f = w_in.shape[1]
    nd = (n, d)
    args = [(cot, ("late", s))]
    args += [(a, "late") for a in (d_memory, normed2, normed1, w_out, slope, w_in, act, out_w, mixed_t, q, k, v)]
    args += [(x, ("late", s)), (proj, "late")]
    args += [(a, "vmem") for a in (lse, rstd1, rstd2, gain, offset, place)]
    carry = lambda i: ("from", prev[i]) if prev else "late"
    if prev:
        args.append((prev[3], "vmem"))
    outs = [(nd, F32, ("late", s, prev[0] if prev else None, count)), ((4 * d, d), BF, carry(1)), ((2 * f, d), BF, carry(2)), ((16 + PAIRS, d), F32, "vmem")]
    scratch = [(nd, F32)] + [(nd, BF)] * 6
    return call(functools.partial(enc_back_kernel, bool(prev)), "encoder_back", scalars, picks, args, outs, scratch, 35e9)


def dec_self_kernel(length, x, proj, out_w, pair_table, bias, gain, offset, x_low, q, k, v, mixed_t, lse, normed1, rstd1, v_t):
    x = x.get()
    pair_row = pair_table[pl.ds(length[2], 1)]

    def low(r):
        value = (x[r].astype(F32) + pair_row).astype(BF)
        x_low.ref[r] = value
        return value

    project(x.shape[0], low, proj.get(), bias, q, k, v, v_t)
    x_low.send()
    mix_forward(q.ref, k.ref, v_t, length[0], True, mixed_t.ref, lse)
    mixed_t.send()
    out_w = out_w.get()

    def body(index):
        r = row_block(index)
        n1, s1 = norm_rows(x[r].astype(F32) + pair_row + dot(mixed_t.ref[:, r], out_w[...], TN) + bias[2:3])
        normed1.ref[r] = n1.astype(normed1.ref.dtype)
        rstd1[r] = s1
        normed1.send(r)

    loop(x.shape[0] // RB, body)


def dec_self(scalars, picks, x, s, pair_table, layer):
    proj, out_w, bias, w_in, c_in, w_out, c_out, gain, offset = layer
    count, n, d = x.shape
    nd = (n, d)
    args = [(x, ("late", s)), (proj, "late"), (out_w, "late")]
    args += [(v, "vmem") for v in (pair_table, bias, gain, offset)]
    outs = [(nd, BF, "late")] * 4 + [((d, n), BF, "late"), ((8, 1, n), F32, "vmem"), (nd, BF, "late"), ((n, 1), F32, "vmem")]
    return call(dec_self_kernel, "decoder_self", scalars, picks, args, outs, [((d, n), BF)], 8e9)


def padded(rows, count):
    return -(-rows // (16 * count)) * (16 * count)


def cross_rows(count, d):
    return padded(4 * d + 16, count)


def dec_mid_kernel(
    share_b, share_c, length, normed1, c_proj, memory, c_out, w_in, w_out, x, cot,
    pair_table, c_bias, c_gain, c_offset, vectors, place,
    shown, two, d_memory, pack,
    small, last, top, y_low, z_low, q, k, v, v_t, mixed_t, lse, normed2, rstd2, act, slope, grad_low, grad_mixed, d_q, d_k, d_v,
):
    small[...] = jnp.zeros(small.shape, F32)
    grad_last, grad_first = (two.part(i) for i in range(2))
    c_in, c_out_b, gain, offset = vectors[0:4], vectors[4:5], vectors[5:7], vectors[7:9]
    pair_row = pair_table[pl.ds(length[2], 1)]

    def put_part(start, value, share, shift):
        value = value.astype(BF)
        done = 0
        while done < value.shape[0]:
            owner, inner = divmod(start + done, share)
            size = min(share - inner, value.shape[0] - done)
            begin = owner * (share_b + share_c) + shift + inner
            pack.ref[begin : begin + size] = value[done : done + size]
            done += size

    def put_b(start, value):
        put_part(start, value, share_b, 0)

    def put_c(start, value):
        put_part(start, value, share_c, share_b)

    normed1, c_proj = normed1.get(), c_proj.get()
    count = normed1.shape[0]

    def queries(index):
        r = row_block(index)
        y = (normed1[r].astype(F32) * gain[0:1] + offset[0:1]).astype(BF)
        y_low[r] = y
        q[r] = (dot(y, c_proj[0]) + c_bias[0:1]).astype(BF)

    loop(count // RB, queries)
    memory = memory.get()
    span = memory.shape[0]

    def keys(index):
        r = row_block(index)
        m = memory[r]
        k[r] = dot(m, c_proj[1]).astype(BF)
        v[r] = (dot(m, c_proj[2]) + c_bias[1:2]).astype(BF)

    loop(span // RB, keys)
    v_t[...] = v[...].T
    mix_forward(q, k, v_t, length[0], False, mixed_t, lse)
    c_out, w_in, w_out, x, cot = c_out.get(), w_in.get(), w_out.get(), x.get(), cot.get()

    def forward(index):
        r = row_block(index)
        y = normed1[r].astype(F32) * gain[0:1] + offset[0:1]
        n2, s2 = norm_rows(y + dot(mixed_t[:, r], c_out[...], TN) + c_bias[2:3])
        normed2[r] = n2.astype(BF)
        rstd2[r] = s2
        z = n2 * c_gain[...] + c_offset[...]
        zl = z.astype(BF)
        z_low[r] = zl
        f = ffn_rows(zl, w_in, c_in, w_out, c_out_b, act, slope, r, True)
        n3, s3 = norm_rows(z + f + x[r].astype(F32) + pair_row)
        valid = valid_rows(index, length[1])
        shown.ref[r] = ((n3 * gain[1:2] + offset[1:2]) * valid).astype(BF)
        shown.send(r)
        g = cot[r].astype(F32) * valid
        small[9:10] += jnp.sum(g * n3, axis=0, keepdims=True)
        small[11:12] += jnp.sum(g, axis=0, keepdims=True)
        g = norm_rows_back(n3, s3, gain[1:2], g)
        last[r] = g
        grad_last.ref[r] = g.astype(BF)

    loop(count // RB, forward)
    grad_last.send()

    def middle(r, grad):
        n2 = normed2[r].astype(F32)
        g = last[r] + grad
        small[8:9] += jnp.sum(g * n2, axis=0, keepdims=True)
        small[10:11] += jnp.sum(g, axis=0, keepdims=True)
        g = norm_rows_back(n2, rstd2[r], c_gain[...], g)
        top[r] = g
        grad_low[r] = g.astype(BF)

    ffn_back(grad_last.ref, act, slope, z_low, w_in, w_out, put_b, small, middle, True)
    grad_mixed[...] = dot(grad_low[...], c_out[...], NT).astype(BF)
    put_c(1536, dot(mixed_t[...], grad_low[...]))
    mix_back(q, k, v, mixed_t, lse, grad_mixed, place, length[0], False, d_q, d_k, d_v)

    def back(index):
        r = row_block(index)
        d_memory.ref[r] = (dot(d_k[r], c_proj[1], NT) + dot(d_v[r], c_proj[2], NT)).astype(BF)
        d_memory.send(r)

    loop(span // RB, back)

    def first(index):
        r = row_block(index)
        grad_first.ref[r] = (top[r] + dot(d_q[r], c_proj[0], NT)).astype(BF)
        grad_first.send(r)

    loop(count // RB, first)
    small[0:1] += jnp.sum(d_q[...].astype(F32), axis=0, keepdims=True)
    small[1:2] += jnp.sum(d_v[...].astype(F32), axis=0, keepdims=True)
    small[2:3] += jnp.sum(grad_low[...].astype(F32), axis=0, keepdims=True)
    m = memory[...]
    put_c(0, dot(y_low[...], d_q[...], TN))
    put_c(512, dot(m, d_k[...], TN))
    put_c(1024, dot(m, d_v[...], TN))
    total_c = pack.ref.shape[0] // (share_b + share_c) * share_c
    put_c(2048, jnp.concatenate([small[...], jnp.zeros((total_c - 2064, 512), F32)]))
    pack.send()


def dec_mid(scalars, picks, x, cot, normed1, memory, pair_table, weights, vectors, cross, place, count):
    c_proj, c_out_w, c_bias, c_gain, c_offset = cross
    n, d = normed1[0].shape
    m = memory[0].shape[0]
    f = weights.shape[0] // 2
    nd, md = (n, d), (m, d)
    part = f // count
    share_b, share_c = 2 * f // count, cross_rows(count, d) // count
    args = [(normed1[0], ("either", None, normed1[1], None)), (c_proj, "late")]
    args += [(memory[0], ("either", None, memory[1], None)), (c_out_w, "late")]
    args += [(weights, ("rows", (f, d), [(2 * part * i + part * j, part * i, part) for i in range(count)])) for j in range(2)]
    args += [(v[0][0], ("either", v[0][1], v[1][0], v[1][1])) for v in (x, cot)]
    args += [(a, "vmem") for a in (pair_table, c_bias, c_gain, c_offset, vectors, place)]
    outs = [(nd, BF, "late"), ((2, n, d), BF, "late"), (md, BF, "late"), ((count * (share_b + share_c), d), BF, "late")]
    scratch = [((16, d), F32), (nd, F32), (nd, F32), (nd, BF), (nd, BF), (nd, BF), (md, BF), (md, BF), ((d, m), BF), ((d, n), BF)]
    scratch += [((8, 1, n), F32), (nd, BF), ((n, 1), F32), ((n, f), BF), ((n, f), BF), (nd, BF), (nd, BF), (nd, BF), (md, BF), (md, BF)]
    return call(functools.partial(dec_mid_kernel, share_b, share_c), "decoder_middle", scalars, picks, args, outs, scratch, 55e9)


def dec_self_back_kernel(
    later, length, grad_first, normed1, grad_last, out_w, mixed_t, q, k, v, x_low, proj,
    lse, rstd1, gain, place, *refs,
):
    earlier = refs[0] if later else None
    d_x, pack_a, small, last, grad_low, grad_mixed, d_q, d_k, d_v, column = refs[later:]
    begin_small(small, earlier)
    column[...] = jnp.zeros(column.shape, F32)
    grad_first, normed1, grad_last = grad_first.get(), normed1.get(), grad_last.get()

    def top(index):
        r = row_block(index)
        n1 = normed1[r].astype(F32)
        g = grad_first[r].astype(F32)
        small[8:9] += jnp.sum(g * n1, axis=0, keepdims=True)
        small[10:11] += jnp.sum(g, axis=0, keepdims=True)
        g = norm_rows_back(n1, rstd1[r], gain[0:1], g)
        last[r] = grad_last[r].astype(F32) + g
        grad_low[r] = g.astype(BF)

    loop(last.shape[0] // RB, top)

    def rest(r, grad):
        g = last[r] + grad
        d_x.ref[r] = g
        d_x.send(r)
        column[0:1] += jnp.sum(g, axis=0, keepdims=True)

    self_back(x_low, proj, out_w, q, k, v, mixed_t, lse, place, length[0], True, grad_low, grad_mixed, d_q, d_k, d_v, pack_a, later, small, rest)
    pair_mark = lax.broadcasted_iota(jnp.int32, (PAIRS, 1), 0) == length[2]
    small[16:] += jnp.where(pair_mark, column[0:1], 0.0)


def dec_self_back(scalars, picks, s, count, two, layer, place, saved, prev):
    proj, out_w, bias, w_in, c_in, w_out, c_out, gain, offset = layer
    x_low, q, k, v, mixed_t, lse, normed1, rstd1 = saved
    n, d = x_low.shape
    nd = (n, d)
    args = [(two, ("late", 1)), (normed1, "late"), (two, ("late", 0))]
    args += [(a, "late") for a in (out_w, mixed_t, q, k, v, x_low, proj)]
    args += [(a, "vmem") for a in (lse, rstd1, gain, place)]
    if prev:
        args.append((prev[3], "vmem"))
    outs = [(nd, F32, ("late", s, prev[0] if prev else None, count)), ((4 * d, d), BF, ("from", prev[1]) if prev else "late"), ((16 + PAIRS, d), F32, "vmem")]
    scratch = [(nd, F32)] + [(nd, BF)] * 5 + [((8, d), F32)]
    return call(functools.partial(dec_self_back_kernel, bool(prev)), "decoder_self_back", scalars, picks, args, outs, scratch, 20e9)


def add_rows(target, start, size, sources):
    block = max(b for b in range(16, min(size, 96) + 1, 16) if size % b == 0)

    def body(index):
        here = pl.ds(pl.multiple_of(start + index * block, 16), block)
        value = 0.0
        for ref, begin in sources:
            value = value + ref[pl.ds(pl.multiple_of(begin + index * block, 16), block)].astype(F32)
        target[here] = value.astype(BF)

    loop(size // block, body)


class Ring:
    def __init__(self, count):
        self.m = m = count // 2
        self.me = lax.axis_index("dp")
        self.core = self.me % 2
        chip = self.me // 2
        turn = (chip // 2) * (1 - chip % 2) + (m - 1 - chip // 2) * (chip % 2)
        back = (m - turn) % m
        self.place = turn * (1 - self.core) + back * self.core
        self.place_other = turn * self.core + back * (1 - self.core)
        self.other = self.me + 1 - 2 * self.core
        self.after = self.device(self.place + 1, self.core)
        self.before = self.device(self.place + m - 1, self.core)

    def device(self, place, core):
        m = self.m
        place = place % m
        turn = place * (1 - core) + ((m - place) % m) * core
        odd = turn // (m // 2)
        return 2 * (2 * (turn * (1 - odd) + (m - 1 - turn) * odd) + odd) + core


def rows_of(ref, start, size):
    return ref.at[pl.ds(pl.multiple_of(start, 16), size)]


class Copies:
    def __init__(self, send_sem, recv_sem):
        self.send_sem, self.recv_sem, self.used = send_sem, recv_sem, 0

    def remote(self, src, dst, device):
        index = self.used
        self.used += 1
        return pltpu.make_async_remote_copy(
            src, dst, self.send_sem.at[index], self.recv_sem.at[index], device_id=device, device_id_type=MESH
        )


def halves(size):
    first = size // 32 * 16
    return [(0, first), (first, size - first)] if first else [(0, size)]


def reduce_kernel(count, shares, a, b, own, out, work, inbox, pairbox, load_sem, send_sem, recv_sem):
    ring = Ring(count)
    m, core, place = ring.m, ring.core, ring.place
    section = lax.axis_index("section")
    na, nb, width = a.shape[0], b.shape[0], a.shape[1]
    bases = (0, count * shares[0], count * (shares[0] + shares[1]))
    starts = (0, shares[0], shares[0] + shares[1])
    loads = [
        pltpu.make_async_copy(a, work.at[pl.ds(0, na)], load_sem.at[0]),
        pltpu.make_async_copy(b, work.at[pl.ds(bases[1], nb)], load_sem.at[1]),
    ]
    for copy in loads:
        copy.start()
    barrier = pltpu.get_barrier_semaphore()
    for device in (ring.after, ring.before, ring.other):
        pl.semaphore_signal(barrier, inc=1, device_id={"dp": device}, device_id_type=MESH)
    blank = jnp.zeros((bases[1] - na - 16, width), F32)
    work[na : bases[1]] = jnp.concatenate([own[0:16], blank]).astype(BF)
    blank = jnp.zeros((count * shares[2] - own.shape[0] + 16, width), F32)
    work[bases[2] : bases[2] + count * shares[2]] = jnp.concatenate([own[16:], blank]).astype(BF)
    for copy in loads:
        copy.wait()
    pl.semaphore_wait(barrier, 3)
    copies = Copies(send_sem, recv_sem)
    units = [(region, offset, size) for region in range(3) for offset, size in halves(shares[region])]
    boxes, total = [], 0
    for _, _, size in units:
        boxes.append(total)
        total += size

    def where(region, action):
        if region == 0:
            action()
        else:
            pl.when(section == region - 1)(action)

    pairs = [[None] * 3 for _ in range(m)]
    for t in range(m):
        owner = ring.device(ring.place_other + 2 * m - 1 - t, 1 - core)
        for region in range(3):
            size = shares[region]
            pairs[t][region] = copies.remote(
                rows_of(work, bases[region] + owner * size, size),
                pairbox.at[pl.ds(t * sum(shares) + starts[region], size)],
                {"dp": ring.other},
            )
            where(region, pairs[t][region].start)
    sends = [[None] * len(units) for _ in range(m - 1)]
    for t in range(m):
        owner = ring.device(place + 2 * m - 1 - t, core)
        for region in range(3):
            where(region, pairs[t][region].wait_recv)
        for u, (region, offset, size) in enumerate(units):
            start = bases[region] + owner * shares[region] + offset
            if t < m - 1:
                sends[t][u] = copies.remote(rows_of(work, start, size), inbox.at[pl.ds(t * total + boxes[u], size)], {"dp": ring.after})

            def step(t=t, u=u, region=region, offset=offset, size=size, start=start):
                sources = [(work, start), (pairbox, t * sum(shares) + starts[region] + offset)]
                if t:
                    sends[t - 1][u].wait_recv()
                    sources.append((inbox, (t - 1) * total + boxes[u]))
                if t < m - 1:
                    add_rows(work, start, size, sources)
                    sends[t][u].start()
                else:
                    add_rows(out, starts[region] + offset, size, sources)

            where(region, step)
    for t in range(m):
        for region in range(3):
            where(region, pairs[t][region].wait_send)
    for t in range(m - 1):
        for u, (region, _, _) in enumerate(units):
            where(region, sends[t][u].wait_send)


def reduce_grads(count, shares, a, b, own):
    d = a.shape[1]
    m = count // 2
    width = sum(shares)
    units = sum(len(halves(s)) for s in shares)
    slots = (m - 1) * units + m * 3
    anywhere = pl.BlockSpec(memory_space=pl.ANY)
    inside = pl.BlockSpec(memory_space=pltpu.VMEM)
    return pl.pallas_call(
        functools.partial(reduce_kernel, count, shares),
        name="gradient_reduce",
        out_shape=sds((width, d), BF),
        in_specs=[anywhere] * 2 + [inside],
        out_specs=inside,
        scratch_shapes=[
            vm((count * width, d), BF),
            vm(((m - 1) * width, d), BF),
            vm((m * width, d), BF),
            pltpu.SemaphoreType.DMA((2,)),
            pltpu.SemaphoreType.DMA((slots,)),
            pltpu.SemaphoreType.DMA((slots,)),
        ],
        compiler_params=pltpu.CompilerParams(collective_id=0, has_side_effects=True, vmem_limit_bytes=48 * 2**20),
    )(a, b, own)


def gather_kernel(count, shares, mine, theirs, own, out, final, out_sem, send_sem, recv_sem):
    ring = Ring(count)
    m, core, place = ring.m, ring.core, ring.place
    section = lax.axis_index("section")
    decoder = section == 1
    barrier = pltpu.get_barrier_semaphore()
    for device in (ring.after, ring.before, ring.other):
        pl.semaphore_signal(barrier, inc=1, device_id={"dp": device}, device_id_type=MESH)
    pl.semaphore_signal(barrier, inc=1, device_id={"section": 1 - section}, device_id_type=MESH)
    bases = [0]
    for share in shares:
        bases.append(bases[-1] + count * share)
    s0, s1, s2, s3 = shares

    def low(region, place, core):
        return bases[region] + ring.device(place, core) * shares[region]

    def here(region):
        return pl.ds(pl.multiple_of(low(region, place, core), 16), shares[region])

    final[here(0)] = own[0:s0]
    final[here(2)] = (mine[s1:].astype(F32) + theirs[s1:].astype(F32)).astype(BF)

    @pl.when(decoder)
    def _():
        final[here(1)] = (mine[0:s1].astype(F32) + theirs[0:s1].astype(F32)).astype(BF)
        final[here(3)] = own[s0 + s1 :]

    @pl.when(section == 0)
    def _():
        final[here(1)] = own[s0 : s0 + s1]

    pl.semaphore_wait(barrier, 4)
    copies = Copies(send_sem, recv_sem)
    pair = rows_of(final, low(3, place, core), s3)
    across = copies.remote(pair, pair, {"section": 1 - section})
    pl.when(decoder)(across.start)
    passes = [[None] * 4 for _ in range(m - 1)]
    shared = []

    def keep(start, size):
        rows = pl.ds(pl.multiple_of(start, 16), size)
        pltpu.make_async_copy(final.at[rows], out.at[rows], out_sem.at[0]).start()

    for s in range(m):
        for region in range(4):
            block = rows_of(final, low(region, place + 2 * m - s, core), shares[region])
            if s:
                passes[s - 1][region].wait_recv()
            elif region == 3:
                pl.when(section == 0)(across.wait_recv)
            if s < m - 1:
                passes[s][region] = copies.remote(block, block, {"dp": ring.after})
                passes[s][region].start()
            shared.append(copies.remote(block, block, {"dp": ring.other}))
            shared[-1].start()
            keep(low(region, place + 2 * m - s, core), shares[region])
    for s in range(m):
        for region in range(4):
            shared[4 * s + region].wait_recv()
            keep(low(region, ring.place_other + 2 * m - s, 1 - core), shares[region])
    for s in range(m - 1):
        for region in range(4):
            passes[s][region].wait_send()
    for share in shared:
        share.wait_send()
    pl.when(decoder)(across.wait_send)
    pltpu.make_async_copy(final, out, out_sem.at[0]).wait()


def gather_grads(count, shares, mine, theirs, own):
    d = own.shape[1]
    m = count // 2
    rows = count * sum(shares)
    slots = (2 * m - 1) * 4 + 1
    inside = pl.BlockSpec(memory_space=pltpu.VMEM)
    return pl.pallas_call(
        functools.partial(gather_kernel, count, shares),
        name="gradient_gather",
        out_shape=sds((rows, d), BF),
        in_specs=[inside] * 3,
        out_specs=pl.BlockSpec(memory_space=pl.ANY),
        scratch_shapes=[
            vm((rows, d), BF),
            pltpu.SemaphoreType.DMA((1,)),
            pltpu.SemaphoreType.DMA((slots,)),
            pltpu.SemaphoreType.DMA((slots,)),
        ],
        compiler_params=pltpu.CompilerParams(collective_id=1, has_side_effects=True, vmem_limit_bytes=48 * 2**20),
    )(mine, theirs, own)


def unpack_kernel(
    bases, f, pack_ref, shown_e, shown_t, shown_far,
    proj, out_w, bias, w_in, b_in, w_out, b_out, gain, offset, c_proj, c_out, c_bias, c_gain, c_offset, pair, shown,
    pack, f_proj, f_out, f_in, f_w_out, f_cproj, f_cout, rows_shown, in_sem, out_sem, shown_sem,
):
    d = pack_ref.shape[1]
    own_b, own_c, own_p = bases
    section = lax.axis_index("section")
    near = [pltpu.make_async_copy(shown_e, rows_shown, shown_sem.at[0])]
    far = [
        pltpu.make_async_copy(shown_t, rows_shown.at[0], shown_sem.at[0]),
        pltpu.make_async_copy(shown_far, rows_shown.at[1], shown_sem.at[1]),
    ]
    spans = [(0, own_b), (own_b, own_b + f), (own_b + f, own_c), (own_c, pack.shape[0])]
    loads = []
    for i, (begin, end) in enumerate(spans):
        rows = pl.ds(begin, end - begin)
        loads.append(pltpu.make_async_copy(pack_ref.at[rows], pack.at[rows], in_sem.at[i]))
        loads[-1].start()

    @pl.when(section == 0)
    def _():
        near[0].start()

    @pl.when(section == 1)
    def _():
        far[0].start()
        far[1].start()

    leaving = []

    def send(held, out):
        leaving.append(pltpu.make_async_copy(held, out, out_sem.at[len(leaving)]))
        leaving[-1].start()

    loads[0].wait()
    f_proj[...] = pack[0 : 3 * d].astype(F32)
    send(f_proj, proj)
    f_out[...] = pack[3 * d : 4 * d].astype(F32)
    send(f_out, out_w)
    loads[1].wait()
    for c in range(f // d):
        f_in[:, c * d : (c + 1) * d] = pack[own_b + c * d : own_b + (c + 1) * d].astype(F32)
    send(f_in, w_in)
    loads[2].wait()
    f_w_out[...] = pack[own_b + f : own_b + 2 * f].astype(F32)
    send(f_w_out, w_out)
    loads[3].wait()

    @pl.when(section == 0)
    def _():
        near[0].wait()

    @pl.when(section == 1)
    def _():
        far[0].wait()
        far[1].wait()

    send(rows_shown, shown)
    f_cproj[...] = pack[own_c : own_c + 3 * d].astype(F32)
    send(f_cproj, c_proj)
    f_cout[...] = pack[own_c + 3 * d : own_c + 4 * d].astype(F32)
    send(f_cout, c_out)
    small = pack[4 * d : 4 * d + 16].astype(F32)
    middle = pack[own_c + 4 * d : own_c + 4 * d + 16].astype(F32)
    bias[...] = small[0:3]
    row = lax.broadcasted_iota(jnp.int32, (16, 1), 0)
    moved = (section == 1) & (row >= 3) & (row <= 11) & (row != 8) & (row != 10)
    small = jnp.where(moved, middle, small)
    for c in range(f // d):
        b_in[:, c * d : (c + 1) * d] = small[3 + c : 4 + c]
    b_out[...] = small[7:8]
    gain[...] = small[8:10]
    offset[...] = small[10:12]
    c_bias[...] = middle[0:3]
    c_gain[...] = middle[8:9]
    c_offset[...] = middle[10:11]
    pair[...] = pack[own_p : own_p + 16].astype(F32)[0 : pair.shape[0]]
    for copy in leaving:
        copy.wait()


def unpack(pack, bases, f, shown_e, shown_t, shown_far):
    d = pack.shape[1]
    inside = pl.BlockSpec(memory_space=pltpu.VMEM)
    anywhere = pl.BlockSpec(memory_space=pl.ANY)
    shapes = [(3 * d, d), (d, d), (3, d), (d, f), (1, f), (f, d), (1, d), (2, d), (2, d), (3 * d, d), (d, d), (3, d), (1, d), (1, d), (PAIRS, d)]
    large = (0, 1, 3, 5, 9, 10)
    return pl.pallas_call(
        functools.partial(unpack_kernel, bases, f),
        name="unpack",
        out_shape=[sds(s, F32) for s in shapes] + [sds(shown_e.shape, BF)],
        in_specs=[anywhere] * 4,
        out_specs=[anywhere if i in large else inside for i in range(len(shapes))] + [anywhere],
        scratch_shapes=[vm(pack.shape, BF)] + [vm(shapes[i], F32) for i in large]
        + [vm(shown_e.shape, BF), pltpu.SemaphoreType.DMA((4,)), pltpu.SemaphoreType.DMA((7,)), pltpu.SemaphoreType.DMA((2,))],
        compiler_params=pltpu.CompilerParams(vmem_limit_bytes=50 * 2**20),
    )(pack, shown_e, shown_t, shown_far)


def nothing(*refs):
    pass


def blank(*shapes):
    spec = pl.BlockSpec(memory_space=pl.ANY)
    return pl.pallas_call(nothing, name="blank", out_shape=[sds(*s) for s in shapes], out_specs=[spec] * len(shapes))()


def per_device(
    embeds, cotangent, pair_ids, seq_lengths, alive_count,
    self_proj, self_out, self_bias, ffn_in, ffn_in_bias, ffn_out, ffn_out_bias, norm_gain, norm_bias,
    cross_proj, cross_out, cross_bias, cross_norm_gain, cross_norm_bias, pair_embed,
):
    layer = (self_proj[0], self_out[0], self_bias[0], ffn_in[0], ffn_in_bias, ffn_out[0], ffn_out_bias, norm_gain[0], norm_bias[0])
    cross = (cross_proj, cross_out, cross_bias, cross_norm_gain[None], cross_norm_bias[None])
    place = jnp.asarray(place_matrix(), BF)
    section_zero = lax.axis_index("section") == 0
    section_one = lax.axis_index("section") == 1
    devices = lax.axis_size("dp")
    x, cot = embeds[0], cotangent[0]
    count, n, d = x.shape
    f = ffn_in.shape[2]
    live = (jnp.arange(count) < alive_count[0])[None, :]
    numbers = jnp.concatenate([seq_lengths.reshape(-1), jnp.where(live, seq_lengths, 0).reshape(-1), pair_ids])
    src = [(s, 2 * count + s, 4 * count + s) for s in range(count)]
    tgt = [(count + s, 3 * count + s, 4 * count + s) for s in range(count)]
    mid = [(s, 3 * count + s, 4 * count + s) for s in range(count)]
    nd, nf, n1 = (n, d), (n, f), (n, 1)
    ahead, behind, both = [(0, 1)], [(1, 0)], [(0, 1), (1, 0)]

    def move(value, way):
        return lax.ppermute(value, "section", way)

    def pick(received, own):
        return jnp.where(section_zero, received, own)

    part = f // devices
    start = lax.axis_index("dp") * part
    share = jnp.concatenate([
        lax.dynamic_slice_in_dim(ffn_in[0], start, part, 1).T, lax.dynamic_slice_in_dim(ffn_out[0], start, part, 0)
    ])
    vectors = jnp.concatenate([ffn_in_bias[:, i : i + d] for i in range(0, f, d)] + [ffn_out_bias, norm_gain[0], norm_bias[0]])
    x, far_share, far_vectors, x_late, cot_late = lax.optimization_barrier(
        (x, move(share, behind), move(vectors, behind), x[1:], cot[1:])
    )
    far_x = move(x_late, behind)
    far_cot = move(cot_late, behind)
    weights = lax.all_gather(pick(far_share, share), "dp", axis=0, tiled=True)
    vectors = pick(far_vectors, vectors)

    def first(e, t, shown):
        def enc():
            memory, shown_e, q, k, v, mt, lse, na, ra, act, slope, nb, rb = enc_forward(numbers, src[e], x, e, layer, shown)
            return memory, shown_e, q, k, v, mt, lse, ra, na, act, slope, nb, rb

        def dec():
            low, q, k, v, mt, lse, na, ra = dec_self(numbers, tgt[t], x, t, pair_embed, layer)
            shown_e, act, slope, nb, rb = blank(((count, *nd), BF), (nf, BF), (nf, BF), (nd, BF), (n1, F32))
            return na, shown_e, q, k, v, mt, lse, ra, low, act, slope, nb, rb

        return lax.cond(section_zero, enc, dec)

    def last(e, t, saved_e, d_memory, grads, saved_t, prev):
        def enc():
            _, _, q, k, v, mt, lse, ra, na, act, slope, nb, rb = saved_e
            return tuple(enc_back(numbers, src[e], x, e, d_memory, cot, layer, place, (q, k, v, mt, lse, na, ra, act, slope, nb, rb), prev))

        def dec():
            na, _, q, k, v, mt, lse, ra, low, _, _, _, _ = saved_t
            d_x, pack_a, small = dec_self_back(
                numbers, tgt[t], t, count, grads, layer, place, (low, q, k, v, mt, lse, na, ra), prev
            )
            return d_x, pack_a, blank(((2 * f, d), BF))[0], small

        return lax.cond(section_one, dec, enc)

    saved = [first(0, 1, None)]
    swapped = move(saved[0][0], both)
    saved.append(first(1, 0, saved[0][1]))
    shown, two, d_memory, pack = dec_mid(
        numbers, (mid[1], mid[0]), ((far_x, 0), (x, 0)), ((far_cot, 0), (cot, 0)), (swapped, saved[1][0]), (saved[1][0], swapped),
        pair_embed, weights, vectors, cross, place, devices,
    )
    near_d_memory = move(d_memory, behind)
    far_two = move(two, ahead)
    mine = lax.psum_scatter(pack, "dp", scatter_dimension=0, tiled=True)
    grads = last(1, 0, saved[1], d_memory, two, saved[1], ())
    shown_late, pack_a = lax.optimization_barrier((shown, grads[1]))
    grads = (grads[0], pack_a, grads[2], grads[3])
    far_shown = move(shown_late, ahead)
    grads = last(0, 1, saved[0], near_d_memory, far_two, saved[0], grads)
    mine, pack_a = lax.optimization_barrier((mine, grads[1]))
    theirs = move(mine, both)
    shares = (padded(4 * d + 16, devices) // devices, 2 * f // devices, cross_rows(devices, d) // devices, 16)
    own = reduce_grads(devices, (shares[0], shares[1], shares[3]), pack_a, grads[2], grads[3])
    pack = gather_grads(devices, shares, mine, theirs, own)
    bases = [devices * sum(shares[:i]) for i in (1, 2, 3)]
    proj, out_w, bias, w_in, b_in, w_out, b_out, gain, offset, c_proj, c_out, c_bias, c_gain, c_offset, pair, shown = unpack(pack, bases, f, saved[1][1], shown, far_shown)
    return (
        shown[None], grads[0][None], proj.reshape(1, 3, d, d), out_w[None], bias[None], w_in[None], b_in, w_out[None], b_out, gain[None], offset[None],
        c_proj.reshape(3, d, d), c_out, c_bias, c_gain[0], c_offset[0], pair,
    )


def solution(mesh):
    s, r = "section", P()
    in_specs = (
        P(s, "dp"), P(s, "dp"), P("dp"), P(None, "dp"), P("dp"),
        P(s), P(s), P(s), P(s), P(s), P(s), P(s), P(s), P(s), r, r, r, r, r, r,
    )
    out_specs = (P(s, "dp"), P(s, "dp"), P(s), P(s), P(s), P(s), P(s), P(s), P(s), P(s), P(s), r, r, r, r, r, r)
    return jax.shard_map(per_device, mesh=mesh, in_specs=in_specs, out_specs=out_specs, check_vma=False)
```

```python
import functools

import jax
import jax.numpy as jnp
import numpy as np
from jax import lax
from jax.experimental import pallas as pl
from jax.experimental.pallas import tpu as pltpu
from jax.sharding import PartitionSpec as P

BF = jnp.bfloat16
F32 = jnp.float32
HEADS = 8
PAIRS = 16
MESH = pl.DeviceIdType.MESH
EPSILON = 1e-05
BLOCKED = -1e30
RB = 512
NN = (((1,), (0,)), ((), ()))
NT = (((1,), (1,)), ((), ()))
TN = (((0,), (0,)), ((), ()))


def dot(left, right, dims=NN):
    return lax.dot_general(left, right, dims, preferred_element_type=F32)


def row_block(index, size=RB):
    return pl.ds(pl.multiple_of(index * size, size), size)


def loop(count, body, unroll=1):
    def step(index, carry):
        body(index)
        return carry

    lax.fori_loop(0, count, step, 0, unroll=unroll)


def lanes_of(half):
    lane = lax.broadcasted_iota(jnp.int32, (1, 128), 1)
    inside = (lane // 64) == half
    spare = lane - 64 * (1 - half)
    ones = (~inside) & (spare < 32)
    block = (~inside) & (spare >= 32)
    flag = (~inside) & (spare == 32)
    return tuple(m.astype(F32) for m in (inside, ones, block, flag))


def norm_rows(value):
    centre = jnp.mean(value, -1, keepdims=True)
    centred = value - centre
    rstd = lax.rsqrt(jnp.mean(centred * centred, -1, keepdims=True) + EPSILON)
    return centred * rstd, rstd


def norm_rows_back(normed, rstd, gain, grad):
    scaled = grad * gain
    return rstd * (
        scaled
        - jnp.mean(scaled, -1, keepdims=True)
        - normed * jnp.mean(scaled * normed, -1, keepdims=True)
    )


def gelu_both(hidden):
    phi = 0.5 + 0.5 * lax.erf(hidden * 0.7071067811865476)
    bell = jnp.exp(-0.5 * hidden * hidden)
    return hidden * phi, phi + hidden * (bell * 0.3989422804014327)


def key_fill(count, length, ones, block):
    position = lax.broadcasted_iota(jnp.int32, (count, 128), 0)
    return ones + jnp.where(position < length, 0.0, BLOCKED) * block


def causal_cut(scores, query_axis):
    query = lax.broadcasted_iota(jnp.int32, scores.shape, query_axis)
    key = lax.broadcasted_iota(jnp.int32, scores.shape, 1 - query_axis)
    return jnp.where(key <= query, scores, BLOCKED)


def mix_forward(queries, keys, values_t, length, causal, mixed_t, lse):
    count = queries.shape[0]
    span = keys.shape[0]
    size = min(512 if causal else 1024, count)

    def pair(index):
        cols = row_block(index, 128)
        q = queries[:, cols].astype(F32) * 0.125
        k = keys[:, cols].astype(F32)
        vt = values_t[cols, :].astype(F32)
        lane = lax.broadcasted_iota(jnp.int32, (128, 1), 0)
        qa, ka, va = [], [], []
        for half in range(2):
            inside, ones, block, flag = lanes_of(half)
            qa.append((q * inside + flag).astype(BF))
            ka.append((k * inside + key_fill(span, length, ones, block)).astype(BF))
            va.append(jnp.where((lane // 64) == half, vt, 1.0).astype(BF))

        def scores_of(part, half):
            here = slice(part * size, (part + 1) * size)
            pieces = [(0, part * size, False), (part * size, size, True)] if causal else [(0, span, False)]
            return [
                (start, reach, cut, dot(ka[half][start : start + reach], qa[half][here], NT))
                for start, reach, cut in pieces
                if reach
            ]

        def finish(part, half, scores):
            here = slice(part * size, (part + 1) * size)
            scores = [(start, reach, causal_cut(s, 1) if cut else s) for start, reach, cut, s in scores]
            top = None
            for _, _, s in scores:
                best = jnp.max(s, axis=0, keepdims=True)
                top = best if top is None else jnp.maximum(top, best)
            total = None
            for start, reach, s in scores:
                o = dot(va[half][:, start : start + reach], jnp.exp(s - top).astype(BF))
                total = o if total is None else total + o
            other = 64 * (1 - half)
            mass = total[other : other + 1]
            own = total[64 * half : 64 * half + 64] / mass
            mixed_t[pl.ds(pl.multiple_of(index * 128 + 64 * half, 64), 64), here] = own.astype(BF)
            lse[index * 2 + half, :, here] = top + jnp.log(mass)

        waiting = None
        for tile in [(part, half) for part in range(count // size) for half in range(2)]:
            scores = scores_of(*tile)
            if waiting:
                finish(*waiting)
            waiting = (*tile, scores)
        finish(*waiting)

    loop(4, pair, 2)


def split3(value):
    high = value.astype(BF).astype(F32)
    middle = (value - high).astype(BF).astype(F32)
    low = (value - high - middle).astype(BF).astype(F32)
    return high, middle, low


def place_matrix():
    out = np.zeros((16, 512), np.float32)
    for half in range(2):
        other = 64 * (1 - half)
        for piece in range(3):
            out[half * 4 + piece, half * 128 + other + piece] = 1
            out[8 + half * 4 + piece, 256 + half * 128 + other + piece] = 1
        out[half * 4 + 3, half * 128 + other + 32] = 1
    return out


def mix_back(queries, keys, values, mixed_t, lse, grad_mixed, place, length, causal, d_q, d_k, d_v):
    count = queries.shape[0]
    span = keys.shape[0]
    size = 256 if causal else min(512, count)

    def pair(index):
        cols = row_block(index, 128)
        q = queries[:, cols].astype(F32) * 0.125
        k_low = keys[:, cols]
        k = k_low.astype(F32)
        v = values[:, cols].astype(F32)
        g_low = grad_mixed[:, cols]
        g = g_low.astype(F32)
        q_t = q.astype(BF).T
        g_t = g_low.T
        product = g_t.astype(F32) * mixed_t[cols, :].astype(F32)
        row = lax.broadcasted_iota(jnp.int32, (16, count), 0)
        spread = jnp.where((row == 3) | (row == 7), 1.0, 0.0)
        for half in range(2):
            shift = -lse[index * 2 + half]
            delta = -jnp.sum(product[64 * half : 64 * half + 64], axis=0, keepdims=True)
            for base, value in ((0, shift), (8, delta)):
                for piece, part in enumerate(split3(value)):
                    spread = jnp.where(row == base + 4 * half + piece, part, spread)
        extra = dot(spread.astype(BF), place[...], TN)
        qa, ka, va, ga = [], [], [], []
        for half in range(2):
            inside, ones, block, flag = lanes_of(half)
            qa.append((q * inside + extra[:, half * 128 : half * 128 + 128]).astype(BF))
            ga.append((g * inside + extra[:, 256 + half * 128 : 384 + half * 128]).astype(BF))
            ka.append((k * inside + key_fill(span, length, ones, block)).astype(BF))
            va.append((v * inside + (1.0 - inside)).astype(BF))
        lane = lax.broadcasted_iota(jnp.int32, (size, 128), 1)
        total_k = [None, None]
        total_v = [None, None]

        def grow(total, value):
            if total is None:
                return value
            if total.shape == value.shape:
                return total + value
            known = total.shape[1]
            return jnp.concatenate([total + value[:, :known], value[:, known:]], axis=1)

        for part in range(count // size):
            here = slice(part * size, (part + 1) * size)
            reach = (part + 1) * size if causal else span
            out_q = []
            for half in range(2):
                s = dot(qa[half][here], ka[half][:reach], NT)
                if causal:
                    if part:
                        s = jnp.concatenate([s[:, : part * size], causal_cut(s[:, part * size :], 0)], axis=1)
                    else:
                        s = causal_cut(s, 0)
                probs = jnp.exp(s)
                grads = dot(ga[half][here], va[half][:reach], NT)
                probs_low = probs.astype(BF)
                d_s = (probs * grads).astype(BF)
                total_v[half] = grow(total_v[half], dot(g_t[:, here], probs_low))
                total_k[half] = grow(total_k[half], dot(q_t[:, here], d_s))
                out_q.append(dot(d_s, k_low[:reach]))
            d_q[here, cols] = (jnp.where(lane < 64, out_q[0], out_q[1]) * 0.125).astype(BF)
        for target, total in ((d_k, total_k), (d_v, total_v)):
            joined = jnp.concatenate([total[0][:64], total[1][64:]], axis=0).astype(BF)
            target[:, cols] = joined.T

    loop(4, pair, 2)


class Late:
    def __init__(self, ref, copy):
        self.ref, self.copy = ref, copy

    def get(self):
        if self.copy is not None:
            self.copy.wait()
            self.copy = None
        return self.ref


class Limits:
    def __init__(self, ref, picks):
        self.ref, self.picks = ref, picks

    def __getitem__(self, index):
        if len(self.picks) == 2:
            near, far = self.picks
            return self.ref[near[index] + lax.axis_index("section") * (far[index] - near[index])]
        return self.ref[self.picks[index]]


class Pieces:
    def __init__(self, source, ref, sem):
        self.source, self.ref, self.sem = source, ref, sem

    def wait(self):
        pltpu.make_async_copy(self.source.at[pl.ds(0, self.ref.shape[0])], self.ref, self.sem).wait()


class Leaving:
    def __init__(self, ref, out, sem):
        self.ref, self.out, self.sem = ref, out, sem

    def send(self, rows=None):
        if rows is None:
            pltpu.make_async_copy(self.ref, self.out, self.sem).start()
        else:
            pltpu.make_async_copy(self.ref.at[rows], self.out.at[rows], self.sem).start()

    def part(self, index):
        return Leaving(self.ref.at[index], self.out.at[index], self.sem)

    def finish(self):
        pltpu.make_async_copy(self.ref, self.out, self.sem).wait()


def sds(shape, dtype):
    return jax.ShapeDtypeStruct(shape, dtype)


def vm(shape, dtype):
    return pltpu.VMEM(shape, dtype)


def call(kernel, name, scalars, picks, args, outs, scratch, flops):
    anywhere = pl.BlockSpec(memory_space=pl.ANY)
    inside = pl.BlockSpec(memory_space=pltpu.VMEM)
    operands, in_specs, out_shapes, out_specs, memory, aliases = [], [], [], [], [], {}
    plan_in, plan_out, places = [], [], []
    for value, kind in args:
        places.append(len(operands))
        operands.append(value)
        if kind == "vmem":
            in_specs.append(inside)
            plan_in.append(None)
        else:
            in_specs.append(anywhere)
            if kind[0] == "either":
                _, index, other, other_index = kind
                plan_in.append((len(memory), (index, len(operands), other_index)))
                operands.append(other)
                in_specs.append(anywhere)
                memory.append(vm(value.shape if index is None else value.shape[1:], value.dtype))
                continue
            if kind[0] == "rows":
                plan_in.append((len(memory), kind[2]))
                memory.append(vm(kind[1], value.dtype))
                continue
            index = kind[1] if isinstance(kind, tuple) else None
            plan_in.append((len(memory), index))
            memory.append(vm(value.shape if index is None else value.shape[1:], value.dtype))
    for position, (shape, dtype, kind) in enumerate(outs):
        if kind == "vmem":
            out_shapes.append(sds(shape, dtype))
            out_specs.append(inside)
            plan_out.append(None)
            continue
        out_specs.append(anywhere)
        index, earlier = None, None
        if isinstance(kind, tuple) and kind[0] == "late":
            index, earlier, total = kind[1:]
            out_shapes.append(sds((total, *shape), dtype))
            if earlier is not None:
                aliases[len(operands)] = position
                operands.append(earlier)
                in_specs.append(anywhere)
        else:
            out_shapes.append(sds(shape, dtype))
        plan_out.append((len(memory), index, len(operands) if isinstance(kind, tuple) and kind[0] == "from" else None))
        memory.append(vm(shape, dtype))
        if isinstance(kind, tuple) and kind[0] == "from":
            operands.append(kind[1])
            in_specs.append(anywhere)
    total_in, count_out, count_memory = len(operands), len(outs), len(memory)

    def body(numbers, *refs):
        ins, results = refs[:total_in], refs[total_in : total_in + count_out]
        held = refs[total_in + count_out : total_in + count_out + count_memory]
        own = refs[total_in + count_out + count_memory : -1]
        sems = refs[-1]
        first, last = [], []
        for spot, plan in zip(places, plan_in):
            ref = ins[spot]
            if plan is None:
                first.append(ref)
                continue
            where, index = plan
            if isinstance(index, tuple):
                index, other, other_index = index
                copies = [
                    pltpu.make_async_copy(r if i is None else r.at[i], held[where], sems.at[where])
                    for r, i in ((ref, index), (ins[other], other_index))
                ]
                section = lax.axis_index("section")
                pl.when(section == 0)(copies[0].start)
                pl.when(section == 1)(copies[1].start)
                first.append(Late(held[where], copies[0]))
                continue
            if isinstance(index, list):
                for begin, end, size in index:
                    pltpu.make_async_copy(ref.at[pl.ds(begin, size)], held[where].at[pl.ds(end, size)], sems.at[where]).start()
                first.append(Late(held[where], Pieces(ref, held[where], sems.at[where])))
                continue
            copy = pltpu.make_async_copy(ref if index is None else ref.at[index], held[where], sems.at[where])
            copy.start()
            first.append(Late(held[where], copy))
        for ref, plan in zip(results, plan_out):
            if plan is None:
                last.append(ref)
                continue
            where, index, source = plan
            leaving = Leaving(held[where], ref if index is None else ref.at[index], sems.at[where])
            if source is not None:
                copy = pltpu.make_async_copy(ins[source], held[where], sems.at[where])
                copy.start()
                leaving.begin = Late(held[where], copy)
            last.append(leaving)
        kernel(Limits(numbers, picks), *first, *last, *own)
        for leaving in last:
            if isinstance(leaving, Leaving):
                leaving.finish()

    return pl.pallas_call(
        body,
        name=name,
        out_shape=out_shapes,
        in_specs=[pl.BlockSpec(memory_space=pltpu.SMEM), *in_specs],
        out_specs=out_specs,
        scratch_shapes=[*memory, *[vm(*s) for s in scratch], pltpu.SemaphoreType.DMA((max(count_memory, 1),))],
        input_output_aliases={i + 1: o for i, o in aliases.items()},
        compiler_params=pltpu.CompilerParams(vmem_limit_bytes=62 * 2**20),
        cost_estimate=pl.CostEstimate(flops=int(flops), bytes_accessed=20 * 2**20, transcendentals=0),
    )(scalars, *operands)


def valid_rows(index, limit, size=RB):
    return (lax.broadcasted_iota(jnp.int32, (size, 1), 0) + index * size < limit).astype(F32)


def ffn_rows(z_low, w_in, c_in, w_out, c_out, act_ref, slope_ref, r, flipped=False):
    def hidden(c):
        cols = slice(c * 512, c * 512 + 512)
        return dot(z_low, w_in[cols], NT) + c_in[c : c + 1] if flipped else dot(z_low, w_in[:, cols]) + c_in[:, cols]

    total, coming = None, hidden(0)
    for c in range(4):
        cols = slice(c * 512, c * 512 + 512)
        here = coming
        coming = hidden(c + 1) if c < 3 else None
        act, slope = gelu_both(here)
        act = act.astype(BF)
        act_ref[r, cols] = act
        slope_ref[r, cols] = slope.astype(BF)
        part = dot(act, w_out[cols])
        total = part if total is None else total + part
    return total + c_out[...]


def put(target, rows, value, later):
    target[rows] = (value + target[rows].astype(F32) if later else value).astype(BF)


def ffn_back(grad_low, act, slope, z_low, w_in, w_out, put_rows, small, on_rows, flipped=False):
    def body(index):
        r = row_block(index)
        g = grad_low[r]
        total, coming = None, dot(g, w_out[0:512], NT)
        for c in range(4):
            cols = slice(c * 512, c * 512 + 512)
            here = coming
            coming = dot(g, w_out[512 * c + 512 : 512 * c + 1024], NT) if c < 3 else None
            dh = (here * slope[r, cols].astype(F32)).astype(BF)
            slope[r, cols] = dh
            small[3 + c : 4 + c] += jnp.sum(dh.astype(F32), axis=0, keepdims=True)
            part = dot(dh, w_in[cols]) if flipped else dot(dh, w_in[:, cols], NT)
            total = part if total is None else total + part
        small[7:8] += jnp.sum(g.astype(F32), axis=0, keepdims=True)
        on_rows(r, total)

    loop(grad_low.shape[0] // RB, body)
    z = z_low[...]
    g = grad_low[...]
    act = act.get() if isinstance(act, Late) else act
    for c in range(4):
        cols = slice(c * 512, c * 512 + 512)
        put_rows(c * 512, dot(z, slope[:, cols], TN))
        put_rows(2048 + c * 512, dot(act[:, cols], g, TN))


def project(count, x_low, proj, bias, q, k, v, v_t):
    def body(index):
        r = row_block(index)
        x = x_low(r)
        q.ref[r] = (dot(x, proj[0]) + bias[0:1]).astype(BF)
        k.ref[r] = dot(x, proj[1]).astype(BF)
        v.ref[r] = (dot(x, proj[2]) + bias[1:2]).astype(BF)

    loop(count // RB, body)
    q.send()
    k.send()
    v.send()
    v_t[...] = v.ref[...].T


def self_back(x, proj, out_w, q, k, v, mixed_t, lse, place, length, causal, grad_low, grad_mixed, d_q, d_k, d_v, pack, later, small, rest):
    grad_mixed[...] = dot(grad_low[...], out_w.get()[...], NT).astype(BF)
    mixed_t = mixed_t.get()
    if later:
        pack.begin.get()
    put(pack.ref, slice(1536, 2048), dot(mixed_t[...], grad_low[...]), later)
    q, k, v, x = q.get(), k.get(), v.get(), x.get()
    mix_back(q, k, v, mixed_t, lse, grad_mixed, place, length, causal, d_q, d_k, d_v)
    small[0:1] += jnp.sum(d_q[...].astype(F32), axis=0, keepdims=True)
    small[1:2] += jnp.sum(d_v[...].astype(F32), axis=0, keepdims=True)
    small[2:3] += jnp.sum(grad_low[...].astype(F32), axis=0, keepdims=True)
    xl = x[...]
    put(pack.ref, slice(0, 512), dot(xl, d_q[...], TN), later)
    put(pack.ref, slice(512, 1024), dot(xl, d_k[...], TN), later)
    put(pack.ref, slice(1024, 1536), dot(xl, d_v[...], TN), later)
    pack.send()
    proj = proj.get()

    def body(index):
        r = row_block(index)
        rest(r, dot(d_q[r], proj[0], NT) + dot(d_k[r], proj[1], NT) + dot(d_v[r], proj[2], NT))

    loop(x.shape[0] // RB, body)


def begin_small(small, earlier):
    small[...] = jnp.zeros(small.shape, F32) if earlier is None else earlier[...]


def enc_forward_kernel(
    length, x, proj, out_w, w_in, w_out, bias, c_in, c_out, gain, offset,
    memory, shown, q, k, v, mixed_t, lse, normed1, rstd1, act, slope, normed2, rstd2, v_t,
):
    x = x.get()
    project(x.shape[0], lambda r: x[r], proj.get(), bias, q, k, v, v_t)
    mix_forward(q.ref, k.ref, v_t, length[0], False, mixed_t.ref, lse)
    mixed_t.send()
    out_w, w_in, w_out = out_w.get(), w_in.get(), w_out.get()

    def body(index):
        r = row_block(index)
        xf = x[r].astype(F32)
        n1, s1 = norm_rows(xf + dot(mixed_t.ref[:, r], out_w[...], TN) + bias[2:3])
        normed1.ref[r] = n1.astype(BF)
        rstd1[r] = s1
        y = n1 * gain[0:1] + offset[0:1]
        f = ffn_rows(y.astype(BF), w_in, c_in, w_out, c_out, act.ref, slope.ref, r)
        n2, s2 = norm_rows(y + f + xf)
        normed2.ref[r] = n2.astype(BF)
        rstd2[r] = s2
        result = n2 * gain[1:2] + offset[1:2]
        memory.ref[r] = result.astype(BF)
        shown.ref[r] = (result * valid_rows(index, length[1])).astype(BF)
        for leaving in (act, slope, memory, shown, normed1, normed2):
            leaving.send(r)

    loop(x.shape[0] // RB, body)


def enc_forward(scalars, picks, x, s, layer, shown):
    proj, out_w, bias, w_in, c_in, w_out, c_out, gain, offset = layer
    count, n, d = x.shape
    f = w_in.shape[1]
    nd = (n, d)
    args = [(x, ("late", s)), (proj, "late"), (out_w, "late"), (w_in, "late"), (w_out, "late")]
    args += [(v, "vmem") for v in (bias, c_in, c_out, gain, offset)]
    outs = [
        (nd, BF, "late"), (nd, BF, ("late", s, shown, count)), (nd, BF, "late"), (nd, BF, "late"), (nd, BF, "late"), ((d, n), BF, "late"),
        ((8, 1, n), F32, "vmem"), (nd, BF, "late"), ((n, 1), F32, "vmem"), ((n, f), BF, "late"), ((n, f), BF, "late"), (nd, BF, "late"), ((n, 1), F32, "vmem"),
    ]
    return call(enc_forward_kernel, "encoder_forward", scalars, picks, args, outs, [((d, n), BF)], 15e9)


def enc_back_kernel(
    later, length, cot, d_memory, normed2, normed1, w_out, slope, w_in, act, out_w, mixed_t, q, k, v, x, proj,
    lse, rstd1, rstd2, gain, offset, place, *refs,
):
    earlier = refs[0] if later else None
    d_x, pack_a, pack_b, small, last, grad_low, z_low, grad_mixed, d_q, d_k, d_v = refs[later:]
    begin_small(small, earlier)
    cot, d_memory, normed2, normed1 = cot.get(), d_memory.get(), normed2.get(), normed1.get()

    def top(index):
        r = row_block(index)
        n2 = normed2[r].astype(F32)
        g = cot[r].astype(F32) * valid_rows(index, length[1]) + d_memory[r].astype(F32)
        small[9:10] += jnp.sum(g * n2, axis=0, keepdims=True)
        small[11:12] += jnp.sum(g, axis=0, keepdims=True)
        g = norm_rows_back(n2, rstd2[r], gain[1:2], g)
        last[r] = g
        grad_low[r] = g.astype(BF)
        z_low[r] = (normed1[r].astype(F32) * gain[0:1] + offset[0:1]).astype(BF)

    loop(last.shape[0] // RB, top)

    def middle(r, grad):
        n1 = normed1[r].astype(F32)
        g = last[r] + grad
        small[8:9] += jnp.sum(g * n1, axis=0, keepdims=True)
        small[10:11] += jnp.sum(g, axis=0, keepdims=True)
        g = norm_rows_back(n1, rstd1[r], gain[0:1], g)
        last[r] = last[r] + g
        grad_mixed[r] = g.astype(BF)

    def put_rows(start, value):
        if later:
            pack_b.begin.get()
        put(pack_b.ref, slice(start, start + 512), value, later)

    ffn_back(grad_low, act, slope.get(), z_low, w_in.get(), w_out.get(), put_rows, small, middle)
    pack_b.send()
    grad_low[...] = grad_mixed[...]

    def rest(r, grad):
        d_x.ref[r] = last[r] + grad
        d_x.send(r)

    self_back(x, proj, out_w, q, k, v, mixed_t, lse, place, length[0], False, grad_low, grad_mixed, d_q, d_k, d_v, pack_a, later, small, rest)


def enc_back(scalars, picks, x, s, d_memory, cot, layer, place, saved, prev):
    proj, out_w, bias, w_in, c_in, w_out, c_out, gain, offset = layer
    q, k, v, mixed_t, lse, normed1, rstd1, act, slope, normed2, rstd2 = saved
    count, n, d = x.shape
    f = w_in.shape[1]
    nd = (n, d)
    args = [(cot, ("late", s))]
    args += [(a, "late") for a in (d_memory, normed2, normed1, w_out, slope, w_in, act, out_w, mixed_t, q, k, v)]
    args += [(x, ("late", s)), (proj, "late")]
    args += [(a, "vmem") for a in (lse, rstd1, rstd2, gain, offset, place)]
    carry = lambda i: ("from", prev[i]) if prev else "late"
    if prev:
        args.append((prev[3], "vmem"))
    outs = [(nd, F32, ("late", s, prev[0] if prev else None, count)), ((4 * d, d), BF, carry(1)), ((2 * f, d), BF, carry(2)), ((16 + PAIRS, d), F32, "vmem")]
    scratch = [(nd, F32)] + [(nd, BF)] * 6
    return call(functools.partial(enc_back_kernel, bool(prev)), "encoder_back", scalars, picks, args, outs, scratch, 35e9)


def dec_self_kernel(length, x, proj, out_w, pair_table, bias, gain, offset, x_low, q, k, v, mixed_t, lse, normed1, rstd1, v_t):
    x = x.get()
    pair_row = pair_table[pl.ds(length[2], 1)]

    def low(r):
        value = (x[r].astype(F32) + pair_row).astype(BF)
        x_low.ref[r] = value
        return value

    project(x.shape[0], low, proj.get(), bias, q, k, v, v_t)
    x_low.send()
    mix_forward(q.ref, k.ref, v_t, length[0], True, mixed_t.ref, lse)
    mixed_t.send()
    out_w = out_w.get()

    def body(index):
        r = row_block(index)
        n1, s1 = norm_rows(x[r].astype(F32) + pair_row + dot(mixed_t.ref[:, r], out_w[...], TN) + bias[2:3])
        normed1.ref[r] = n1.astype(normed1.ref.dtype)
        rstd1[r] = s1
        normed1.send(r)

    loop(x.shape[0] // RB, body)


def dec_self(scalars, picks, x, s, pair_table, layer):
    proj, out_w, bias, w_in, c_in, w_out, c_out, gain, offset = layer
    count, n, d = x.shape
    nd = (n, d)
    args = [(x, ("late", s)), (proj, "late"), (out_w, "late")]
    args += [(v, "vmem") for v in (pair_table, bias, gain, offset)]
    outs = [(nd, BF, "late")] * 4 + [((d, n), BF, "late"), ((8, 1, n), F32, "vmem"), (nd, BF, "late"), ((n, 1), F32, "vmem")]
    return call(dec_self_kernel, "decoder_self", scalars, picks, args, outs, [((d, n), BF)], 8e9)


def padded(rows, count):
    return -(-rows // (16 * count)) * (16 * count)


def cross_rows(count, d):
    return padded(4 * d + 16, count)


def dec_cross_kernel(
    length, normed1, c_proj, memory, c_bias, vectors,
    q, k, v, mixed_t, lse, v_t,
):
    gain, offset = vectors[5:6], vectors[7:8]
    normed1, c_proj = normed1.get(), c_proj.get()

    def queries(index):
        r = row_block(index)
        y = (normed1[r].astype(F32) * gain + offset).astype(BF)
        q.ref[r] = (dot(y, c_proj[0]) + c_bias[0:1]).astype(BF)

    loop(normed1.shape[0] // RB, queries)
    q.send()
    memory = memory.get()

    def keys(index):
        r = row_block(index)
        m = memory[r]
        k.ref[r] = dot(m, c_proj[1]).astype(BF)
        v.ref[r] = (dot(m, c_proj[2]) + c_bias[1:2]).astype(BF)

    loop(memory.shape[0] // RB, keys)
    k.send()
    v.send()
    v_t[...] = v.ref[...].T
    mix_forward(q.ref, k.ref, v_t, length[0], False, mixed_t.ref, lse)
    mixed_t.send()


def dec_mid_kernel(
    share_b, share_c, length, normed1, mixed_t, c_out, w_in, w_out, x, cot, q, k, v, c_proj, memory,
    lse, pair_table, c_bias, c_gain, c_offset, vectors, place,
    shown, two, d_memory, pack,
    small, last, top, y_low, z_low, normed2, rstd2, act, slope, grad_low, grad_mixed, d_q, d_k, d_v,
):
    small[...] = jnp.zeros(small.shape, F32)
    grad_last, grad_first = (two.part(i) for i in range(2))
    c_in, c_out_b, gain, offset = vectors[0:4], vectors[4:5], vectors[5:7], vectors[7:9]
    pair_row = pair_table[pl.ds(length[2], 1)]

    def put_part(start, value, share, shift):
        value = value.astype(BF)
        done = 0
        while done < value.shape[0]:
            owner, inner = divmod(start + done, share)
            size = min(share - inner, value.shape[0] - done)
            begin = owner * (share_b + share_c) + shift + inner
            pack.ref[begin : begin + size] = value[done : done + size]
            done += size

    def put_b(start, value):
        put_part(start, value, share_b, 0)

    def put_c(start, value):
        put_part(start, value, share_c, share_b)

    normed1, mixed_t, c_out, w_in, w_out, x, cot = (a.get() for a in (normed1, mixed_t, c_out, w_in, w_out, x, cot))
    count = normed1.shape[0]

    def forward(index):
        r = row_block(index)
        y = normed1[r].astype(F32) * gain[0:1] + offset[0:1]
        y_low[r] = y.astype(BF)
        n2, s2 = norm_rows(y + dot(mixed_t[:, r], c_out[...], TN) + c_bias[2:3])
        normed2[r] = n2.astype(BF)
        rstd2[r] = s2
        z = n2 * c_gain[...] + c_offset[...]
        zl = z.astype(BF)
        z_low[r] = zl
        f = ffn_rows(zl, w_in, c_in, w_out, c_out_b, act, slope, r, True)
        n3, s3 = norm_rows(z + f + x[r].astype(F32) + pair_row)
        valid = valid_rows(index, length[1])
        shown.ref[r] = ((n3 * gain[1:2] + offset[1:2]) * valid).astype(BF)
        shown.send(r)
        g = cot[r].astype(F32) * valid
        small[9:10] += jnp.sum(g * n3, axis=0, keepdims=True)
        small[11:12] += jnp.sum(g, axis=0, keepdims=True)
        g = norm_rows_back(n3, s3, gain[1:2], g)
        last[r] = g
        grad_last.ref[r] = g.astype(BF)

    loop(count // RB, forward)
    grad_last.send()

    def middle(r, grad):
        n2 = normed2[r].astype(F32)
        g = last[r] + grad
        small[8:9] += jnp.sum(g * n2, axis=0, keepdims=True)
        small[10:11] += jnp.sum(g, axis=0, keepdims=True)
        g = norm_rows_back(n2, rstd2[r], c_gain[...], g)
        top[r] = g
        grad_low[r] = g.astype(BF)

    ffn_back(grad_last.ref, act, slope, z_low, w_in, w_out, put_b, small, middle, True)
    grad_mixed[...] = dot(grad_low[...], c_out[...], NT).astype(BF)
    put_c(1536, dot(mixed_t[...], grad_low[...]))
    q, k, v = q.get(), k.get(), v.get()
    mix_back(q, k, v, mixed_t, lse, grad_mixed, place, length[0], False, d_q, d_k, d_v)
    c_proj, memory = c_proj.get(), memory.get()
    span = memory.shape[0]

    def back(index):
        r = row_block(index)
        d_memory.ref[r] = (dot(d_k[r], c_proj[1], NT) + dot(d_v[r], c_proj[2], NT)).astype(BF)
        d_memory.send(r)

    loop(span // RB, back)

    def first(index):
        r = row_block(index)
        grad_first.ref[r] = (top[r] + dot(d_q[r], c_proj[0], NT)).astype(BF)
        grad_first.send(r)

    loop(count // RB, first)
    small[0:1] += jnp.sum(d_q[...].astype(F32), axis=0, keepdims=True)
    small[1:2] += jnp.sum(d_v[...].astype(F32), axis=0, keepdims=True)
    small[2:3] += jnp.sum(grad_low[...].astype(F32), axis=0, keepdims=True)
    m = memory[...]
    put_c(0, dot(y_low[...], d_q[...], TN))
    put_c(512, dot(m, d_k[...], TN))
    put_c(1024, dot(m, d_v[...], TN))
    total_c = pack.ref.shape[0] // (share_b + share_c) * share_c
    put_c(2048, jnp.concatenate([small[...], jnp.zeros((total_c - 2064, 512), F32)]))
    pack.send()


def dec_mid(scalars, picks, x, cot, normed1, memory, crossed, pair_table, weights, vectors, cross, place, count):
    c_proj, c_out_w, c_bias, c_gain, c_offset = cross
    q, k, v, mixed_t, lse = crossed
    n, d = normed1[0].shape
    m = memory[0].shape[0]
    f = weights.shape[0] // 2
    nd, md = (n, d), (m, d)
    part = f // count
    share_b, share_c = 2 * f // count, cross_rows(count, d) // count
    either = lambda pair: (pair[0], ("either", None, pair[1], None))
    args = [either(normed1), (mixed_t, "late"), (c_out_w, "late")]
    args += [(weights, ("rows", (f, d), [(2 * part * i + part * j, part * i, part) for i in range(count)])) for j in range(2)]
    args += [(a[0][0], ("either", a[0][1], a[1][0], a[1][1])) for a in (x, cot)]
    args += [(a, "late") for a in (q, k, v, c_proj)] + [either(memory)]
    args += [(a, "vmem") for a in (lse, pair_table, c_bias, c_gain, c_offset, vectors, place)]
    outs = [(nd, BF, "late"), ((2, n, d), BF, "late"), (md, BF, "late"), ((count * (share_b + share_c), d), BF, "late")]
    scratch = [((16, d), F32), (nd, F32), (nd, F32), (nd, BF), (nd, BF)]
    scratch += [(nd, BF), ((n, 1), F32), ((n, f), BF), ((n, f), BF), (nd, BF), (nd, BF), (nd, BF), (md, BF), (md, BF)]
    return call(functools.partial(dec_mid_kernel, share_b, share_c), "decoder_middle", scalars, picks, args, outs, scratch, 45e9)


def dec_cross(scalars, picks, normed1, memory, vectors, cross):
    c_proj, c_out_w, c_bias, c_gain, c_offset = cross
    n, d = normed1[0].shape
    m = memory[0].shape[0]
    either = lambda pair: (pair[0], ("either", None, pair[1], None))
    args = [either(normed1), (c_proj, "late"), either(memory), (c_bias, "vmem"), (vectors, "vmem")]
    outs = [((n, d), BF, "late"), ((m, d), BF, "late"), ((m, d), BF, "late"), ((d, n), BF, "late"), ((8, 1, n), F32, "vmem")]
    return call(dec_cross_kernel, "decoder_cross", scalars, picks, args, outs, [((d, m), BF)], 11e9)


def dec_self_back_kernel(
    later, length, grad_first, normed1, grad_last, out_w, mixed_t, q, k, v, x_low, proj,
    lse, rstd1, gain, place, *refs,
):
    earlier = refs[0] if later else None
    d_x, pack_a, small, last, grad_low, grad_mixed, d_q, d_k, d_v, column = refs[later:]
    begin_small(small, earlier)
    column[...] = jnp.zeros(column.shape, F32)
    grad_first, normed1, grad_last = grad_first.get(), normed1.get(), grad_last.get()

    def top(index):
        r = row_block(index)
        n1 = normed1[r].astype(F32)
        g = grad_first[r].astype(F32)
        small[8:9] += jnp.sum(g * n1, axis=0, keepdims=True)
        small[10:11] += jnp.sum(g, axis=0, keepdims=True)
        g = norm_rows_back(n1, rstd1[r], gain[0:1], g)
        last[r] = grad_last[r].astype(F32) + g
        grad_low[r] = g.astype(BF)

    loop(last.shape[0] // RB, top)

    def rest(r, grad):
        g = last[r] + grad
        d_x.ref[r] = g
        d_x.send(r)
        column[0:1] += jnp.sum(g, axis=0, keepdims=True)

    self_back(x_low, proj, out_w, q, k, v, mixed_t, lse, place, length[0], True, grad_low, grad_mixed, d_q, d_k, d_v, pack_a, later, small, rest)
    pair_mark = lax.broadcasted_iota(jnp.int32, (PAIRS, 1), 0) == length[2]
    small[16:] += jnp.where(pair_mark, column[0:1], 0.0)


def dec_self_back(scalars, picks, s, count, two, layer, place, saved, prev):
    proj, out_w, bias, w_in, c_in, w_out, c_out, gain, offset = layer
    x_low, q, k, v, mixed_t, lse, normed1, rstd1 = saved
    n, d = x_low.shape
    nd = (n, d)
    args = [(two, ("late", 1)), (normed1, "late"), (two, ("late", 0))]
    args += [(a, "late") for a in (out_w, mixed_t, q, k, v, x_low, proj)]
    args += [(a, "vmem") for a in (lse, rstd1, gain, place)]
    if prev:
        args.append((prev[3], "vmem"))
    outs = [(nd, F32, ("late", s, prev[0] if prev else None, count)), ((4 * d, d), BF, ("from", prev[1]) if prev else "late"), ((16 + PAIRS, d), F32, "vmem")]
    scratch = [(nd, F32)] + [(nd, BF)] * 5 + [((8, d), F32)]
    return call(functools.partial(dec_self_back_kernel, bool(prev)), "decoder_self_back", scalars, picks, args, outs, scratch, 20e9)


def add_rows(target, start, size, sources):
    block = max(b for b in range(16, min(size, 96) + 1, 16) if size % b == 0)

    def body(index):
        here = pl.ds(pl.multiple_of(start + index * block, 16), block)
        value = 0.0
        for ref, begin in sources:
            value = value + ref[pl.ds(pl.multiple_of(begin + index * block, 16), block)].astype(F32)
        target[here] = value.astype(BF)

    loop(size // block, body)


class Ring:
    def __init__(self, count):
        self.m = m = count // 2
        self.me = lax.axis_index("dp")
        self.core = self.me % 2
        chip = self.me // 2
        turn = (chip // 2) * (1 - chip % 2) + (m - 1 - chip // 2) * (chip % 2)
        back = (m - turn) % m
        self.place = turn * (1 - self.core) + back * self.core
        self.place_other = turn * self.core + back * (1 - self.core)
        self.other = self.me + 1 - 2 * self.core
        self.after = self.device(self.place + 1, self.core)
        self.before = self.device(self.place + m - 1, self.core)

    def device(self, place, core):
        m = self.m
        place = place % m
        turn = place * (1 - core) + ((m - place) % m) * core
        odd = turn // (m // 2)
        return 2 * (2 * (turn * (1 - odd) + (m - 1 - turn) * odd) + odd) + core


def rows_of(ref, start, size):
    return ref.at[pl.ds(pl.multiple_of(start, 16), size)]


class Copies:
    def __init__(self, send_sem, recv_sem):
        self.send_sem, self.recv_sem, self.used = send_sem, recv_sem, 0

    def remote(self, src, dst, device):
        index = self.used
        self.used += 1
        return pltpu.make_async_remote_copy(
            src, dst, self.send_sem.at[index], self.recv_sem.at[index], device_id=device, device_id_type=MESH
        )


def halves(size):
    first = size // 32 * 16
    return [(0, first), (first, size - first)] if first else [(0, size)]


def reduce_kernel(count, shares, a, b, own, out, work, inbox, pairbox, load_sem, send_sem, recv_sem):
    ring = Ring(count)
    m, core, place = ring.m, ring.core, ring.place
    section = lax.axis_index("section")
    na, nb, width = a.shape[0], b.shape[0], a.shape[1]
    bases = (0, count * shares[0], count * (shares[0] + shares[1]))
    starts = (0, shares[0], shares[0] + shares[1])
    loads = [
        pltpu.make_async_copy(a, work.at[pl.ds(0, na)], load_sem.at[0]),
        pltpu.make_async_copy(b, work.at[pl.ds(bases[1], nb)], load_sem.at[1]),
    ]
    for copy in loads:
        copy.start()
    barrier = pltpu.get_barrier_semaphore()
    for device in (ring.after, ring.before, ring.other):
        pl.semaphore_signal(barrier, inc=1, device_id={"dp": device}, device_id_type=MESH)
    blank = jnp.zeros((bases[1] - na - 16, width), F32)
    work[na : bases[1]] = jnp.concatenate([own[0:16], blank]).astype(BF)
    blank = jnp.zeros((count * shares[2] - own.shape[0] + 16, width), F32)
    work[bases[2] : bases[2] + count * shares[2]] = jnp.concatenate([own[16:], blank]).astype(BF)
    for copy in loads:
        copy.wait()
    pl.semaphore_wait(barrier, 3)
    copies = Copies(send_sem, recv_sem)
    units = [(region, offset, size) for region in range(3) for offset, size in halves(shares[region])]
    boxes, total = [], 0
    for _, _, size in units:
        boxes.append(total)
        total += size

    def where(region, action):
        if region == 0:
            action()
        else:
            pl.when(section == region - 1)(action)

    near, far = m // 2, m - 1 - m // 2

    def order(place):
        chunks = []
        for s in range(near):
            chunks.append(place + near - s)
            if s < far:
                chunks.append(place + 2 * m - far + s)
        return chunks + [place + m]

    pairs = []
    for t, chunk in enumerate(order(ring.place_other)):
        owner = ring.device(chunk, 1 - core)
        row = []
        for region in range(3):
            size = shares[region]
            row.append(
                copies.remote(
                    rows_of(work, bases[region] + owner * size, size),
                    pairbox.at[pl.ds(t * sum(shares) + starts[region], size)],
                    {"dp": ring.other},
                )
            )
            where(region, row[region].start)
        pairs.append(row)
    slots = [(s, way) for s in range(near) for way in range(2) if way == 0 or s < far]
    box_of = {slot: i for i, slot in enumerate(slots)}
    sends = {}
    for t, chunk in enumerate(order(place)):
        s, way = slots[t] if t < m - 1 else (None, None)
        owner = ring.device(chunk, core)
        for region in range(3):
            where(region, pairs[t][region].wait_recv)
        for u, (region, offset, size) in enumerate(units):
            start = bases[region] + owner * shares[region] + offset
            if s is None:
                before = [(near - 1, 0), (far - 1, 1)] if far else [(near - 1, 0)]
            else:
                before = [(s - 1, way)] if s else []
                target = ring.after if way == 0 else ring.before
                box = box_of[(s, way)] * total + boxes[u]
                sends[(s, way, u)] = copies.remote(rows_of(work, start, size), inbox.at[pl.ds(box, size)], {"dp": target})

            def step(t=t, s=s, way=way, u=u, region=region, offset=offset, size=size, start=start, before=before):
                sources = [(work, start), (pairbox, t * sum(shares) + starts[region] + offset)]
                for slot in before:
                    sends[(*slot, u)].wait_recv()
                    sources.append((inbox, box_of[slot] * total + boxes[u]))
                if s is None:
                    add_rows(out, starts[region] + offset, size, sources)
                else:
                    add_rows(work, start, size, sources)
                    sends[(s, way, u)].start()

            where(region, step)
    for row in pairs:
        for region in range(3):
            where(region, row[region].wait_send)
    for (s, way, u), copy in sends.items():
        where(units[u][0], copy.wait_send)


def reduce_grads(count, shares, a, b, own):
    d = a.shape[1]
    m = count // 2
    width = sum(shares)
    units = sum(len(halves(s)) for s in shares)
    slots = (m - 1) * units + m * 3
    anywhere = pl.BlockSpec(memory_space=pl.ANY)
    inside = pl.BlockSpec(memory_space=pltpu.VMEM)
    return pl.pallas_call(
        functools.partial(reduce_kernel, count, shares),
        name="gradient_reduce",
        out_shape=sds((width, d), BF),
        in_specs=[anywhere] * 2 + [inside],
        out_specs=inside,
        scratch_shapes=[
            vm((count * width, d), BF),
            vm(((m - 1) * width, d), BF),
            vm((m * width, d), BF),
            pltpu.SemaphoreType.DMA((2,)),
            pltpu.SemaphoreType.DMA((slots,)),
            pltpu.SemaphoreType.DMA((slots,)),
        ],
        compiler_params=pltpu.CompilerParams(collective_id=0, has_side_effects=True, vmem_limit_bytes=48 * 2**20),
    )(a, b, own)


def gather_kernel(count, shares, mine, theirs, own, out, final, out_sem, send_sem, recv_sem):
    ring = Ring(count)
    m, core, place = ring.m, ring.core, ring.place
    section = lax.axis_index("section")
    decoder = section == 1
    barrier = pltpu.get_barrier_semaphore()
    for device in (ring.after, ring.before, ring.other):
        pl.semaphore_signal(barrier, inc=1, device_id={"dp": device}, device_id_type=MESH)
    pl.semaphore_signal(barrier, inc=1, device_id={"section": 1 - section}, device_id_type=MESH)
    bases = [0]
    for share in shares:
        bases.append(bases[-1] + count * share)
    s0, s1, s2, s3 = shares

    def low(region, place, core):
        return bases[region] + ring.device(place, core) * shares[region]

    def here(region):
        return pl.ds(pl.multiple_of(low(region, place, core), 16), shares[region])

    final[here(0)] = own[0:s0]
    final[here(2)] = (mine[s1:].astype(F32) + theirs[s1:].astype(F32)).astype(BF)

    @pl.when(decoder)
    def _():
        final[here(1)] = (mine[0:s1].astype(F32) + theirs[0:s1].astype(F32)).astype(BF)
        final[here(3)] = own[s0 + s1 :]

    @pl.when(section == 0)
    def _():
        final[here(1)] = own[s0 : s0 + s1]

    pl.semaphore_wait(barrier, 4)
    copies = Copies(send_sem, recv_sem)
    pair = rows_of(final, low(3, place, core), s3)
    across = copies.remote(pair, pair, {"section": 1 - section})
    pl.when(decoder)(across.start)
    near, far = m // 2, m - 1 - m // 2
    passes, shared, arrived = {}, [], []

    def keep(start, size):
        rows = pl.ds(pl.multiple_of(start, 16), size)
        pltpu.make_async_copy(final.at[rows], out.at[rows], out_sem.at[0]).start()

    for s in range(near + 1):
        for way in range(2):
            if (way == 1 and s > far) or (s == 0 and way == 1 and not far):
                continue
            shift = 2 * m - s if way == 0 else s
            limit, target = (near, ring.after) if way == 0 else (far, ring.before)
            for region in range(4):
                block = rows_of(final, low(region, place + shift, core), shares[region])
                if s:
                    passes[(s - 1, way, region)].wait_recv()
                elif region == 3 and way == 0:
                    pl.when(section == 0)(across.wait_recv)
                if s < limit:
                    passes[(s, way, region)] = copies.remote(block, block, {"dp": target})
                    passes[(s, way, region)].start()
                if s or way == 0:
                    shared.append(copies.remote(block, block, {"dp": ring.other}))
                    shared[-1].start()
                    keep(low(region, place + shift, core), shares[region])
                    arrived.append((region, shift))
    for copy, (region, shift) in zip(shared, arrived):
        copy.wait_recv()
        keep(low(region, ring.place_other + shift, 1 - core), shares[region])
    for copy in passes.values():
        copy.wait_send()
    for share in shared:
        share.wait_send()
    pl.when(decoder)(across.wait_send)
    pltpu.make_async_copy(final, out, out_sem.at[0]).wait()


def gather_grads(count, shares, mine, theirs, own):
    d = own.shape[1]
    m = count // 2
    rows = count * sum(shares)
    slots = (2 * m - 1) * 4 + 1
    inside = pl.BlockSpec(memory_space=pltpu.VMEM)
    return pl.pallas_call(
        functools.partial(gather_kernel, count, shares),
        name="gradient_gather",
        out_shape=sds((rows, d), BF),
        in_specs=[inside] * 3,
        out_specs=pl.BlockSpec(memory_space=pl.ANY),
        scratch_shapes=[
            vm((rows, d), BF),
            pltpu.SemaphoreType.DMA((1,)),
            pltpu.SemaphoreType.DMA((slots,)),
            pltpu.SemaphoreType.DMA((slots,)),
        ],
        compiler_params=pltpu.CompilerParams(collective_id=1, has_side_effects=True, vmem_limit_bytes=48 * 2**20),
    )(mine, theirs, own)


def unpack_kernel(
    bases, f, pack_ref, shown_e, shown_t, shown_far,
    proj, out_w, bias, w_in, b_in, w_out, b_out, gain, offset, c_proj, c_out, c_bias, c_gain, c_offset, pair, shown,
    pack, f_proj, f_out, f_in, f_w_out, f_cproj, f_cout, rows_shown, in_sem, out_sem, shown_sem,
):
    d = pack_ref.shape[1]
    own_b, own_c, own_p = bases
    section = lax.axis_index("section")
    leave = pltpu.make_async_copy(rows_shown, shown, shown_sem.at[0])
    far = [
        pltpu.make_async_copy(shown_t, rows_shown.at[0], shown_sem.at[0]),
        pltpu.make_async_copy(shown_far, rows_shown.at[1], shown_sem.at[1]),
    ]
    spans = [(0, own_b), (own_b, own_b + f), (own_b + f, own_c), (own_c, pack.shape[0])]
    loads = []
    for i, (begin, end) in enumerate(spans):
        rows = pl.ds(begin, end - begin)
        loads.append(pltpu.make_async_copy(pack_ref.at[rows], pack.at[rows], in_sem.at[i]))
        loads[-1].start()

    @pl.when(section == 1)
    def _():
        far[0].start()
        far[1].start()

    leaving = []

    def send(held, out):
        leaving.append(pltpu.make_async_copy(held, out, out_sem.at[len(leaving)]))
        leaving[-1].start()

    loads[0].wait()
    f_proj[...] = pack[0 : 3 * d].astype(F32)
    send(f_proj, proj)
    f_out[...] = pack[3 * d : 4 * d].astype(F32)
    send(f_out, out_w)
    loads[1].wait()
    for c in range(f // d):
        f_in[:, c * d : (c + 1) * d] = pack[own_b + c * d : own_b + (c + 1) * d].astype(F32)
    send(f_in, w_in)
    loads[2].wait()
    f_w_out[...] = pack[own_b + f : own_b + 2 * f].astype(F32)
    send(f_w_out, w_out)
    loads[3].wait()

    @pl.when(section == 1)
    def _():
        far[0].wait()
        far[1].wait()
        leave.start()

    f_cproj[...] = pack[own_c : own_c + 3 * d].astype(F32)
    send(f_cproj, c_proj)
    f_cout[...] = pack[own_c + 3 * d : own_c + 4 * d].astype(F32)
    send(f_cout, c_out)
    small = pack[4 * d : 4 * d + 16].astype(F32)
    middle = pack[own_c + 4 * d : own_c + 4 * d + 16].astype(F32)
    bias[...] = small[0:3]
    row = lax.broadcasted_iota(jnp.int32, (16, 1), 0)
    moved = (section == 1) & (row >= 3) & (row <= 11) & (row != 8) & (row != 10)
    small = jnp.where(moved, middle, small)
    for c in range(f // d):
        b_in[:, c * d : (c + 1) * d] = small[3 + c : 4 + c]
    b_out[...] = small[7:8]
    gain[...] = small[8:10]
    offset[...] = small[10:12]
    c_bias[...] = middle[0:3]
    c_gain[...] = middle[8:9]
    c_offset[...] = middle[10:11]
    pair[...] = pack[own_p : own_p + 16].astype(F32)[0 : pair.shape[0]]
    for copy in leaving:
        copy.wait()
    pl.when(section == 1)(leave.wait)


def unpack(pack, bases, f, shown_e, shown_t, shown_far):
    d = pack.shape[1]
    inside = pl.BlockSpec(memory_space=pltpu.VMEM)
    anywhere = pl.BlockSpec(memory_space=pl.ANY)
    shapes = [(3 * d, d), (d, d), (3, d), (d, f), (1, f), (f, d), (1, d), (2, d), (2, d), (3 * d, d), (d, d), (3, d), (1, d), (1, d), (PAIRS, d)]
    large = (0, 1, 3, 5, 9, 10)
    return pl.pallas_call(
        functools.partial(unpack_kernel, bases, f),
        name="unpack",
        out_shape=[sds(s, F32) for s in shapes] + [sds(shown_e.shape, BF)],
        in_specs=[anywhere] * 4,
        out_specs=[anywhere if i in large else inside for i in range(len(shapes))] + [anywhere],
        input_output_aliases={1: len(shapes)},
        scratch_shapes=[vm(pack.shape, BF)] + [vm(shapes[i], F32) for i in large]
        + [vm(shown_e.shape, BF), pltpu.SemaphoreType.DMA((4,)), pltpu.SemaphoreType.DMA((6,)), pltpu.SemaphoreType.DMA((2,))],
        compiler_params=pltpu.CompilerParams(vmem_limit_bytes=50 * 2**20),
    )(pack, shown_e, shown_t, shown_far)


def nothing(*refs):
    pass


def blank(*shapes):
    spec = pl.BlockSpec(memory_space=pl.ANY)
    return pl.pallas_call(nothing, name="blank", out_shape=[sds(*s) for s in shapes], out_specs=[spec] * len(shapes))()


def per_device(
    embeds, cotangent, pair_ids, seq_lengths, alive_count,
    self_proj, self_out, self_bias, ffn_in, ffn_in_bias, ffn_out, ffn_out_bias, norm_gain, norm_bias,
    cross_proj, cross_out, cross_bias, cross_norm_gain, cross_norm_bias, pair_embed,
):
    layer = (self_proj[0], self_out[0], self_bias[0], ffn_in[0], ffn_in_bias, ffn_out[0], ffn_out_bias, norm_gain[0], norm_bias[0])
    cross = (cross_proj, cross_out, cross_bias, cross_norm_gain[None], cross_norm_bias[None])
    place = jnp.asarray(place_matrix(), BF)
    section_zero = lax.axis_index("section") == 0
    section_one = lax.axis_index("section") == 1
    devices = lax.axis_size("dp")
    x, cot = embeds[0], cotangent[0]
    count, n, d = x.shape
    f = ffn_in.shape[2]
    live = (jnp.arange(count) < alive_count[0])[None, :]
    numbers = jnp.concatenate([seq_lengths.reshape(-1), jnp.where(live, seq_lengths, 0).reshape(-1), pair_ids])
    src = [(s, 2 * count + s, 4 * count + s) for s in range(count)]
    tgt = [(count + s, 3 * count + s, 4 * count + s) for s in range(count)]
    mid = [(s, 3 * count + s, 4 * count + s) for s in range(count)]
    nd, nf, n1 = (n, d), (n, f), (n, 1)
    ahead, behind, both = [(0, 1)], [(1, 0)], [(0, 1), (1, 0)]

    def move(value, way):
        return lax.ppermute(value, "section", way)

    def pick(received, own):
        return jnp.where(section_zero, received, own)

    part = f // devices
    start = lax.axis_index("dp") * part
    share = jnp.concatenate([
        lax.dynamic_slice_in_dim(ffn_in[0], start, part, 1).T, lax.dynamic_slice_in_dim(ffn_out[0], start, part, 0)
    ])
    vectors = jnp.concatenate([ffn_in_bias[:, i : i + d] for i in range(0, f, d)] + [ffn_out_bias, norm_gain[0], norm_bias[0]])
    x, far_share, far_vectors, x_late, cot_late = lax.optimization_barrier(
        (x, move(share, behind), move(vectors, behind), x[1:], cot[1:])
    )
    far_x = move(x_late, behind)
    weights = lax.all_gather(pick(far_share, share), "dp", axis=0, tiled=True)
    vectors = pick(far_vectors, vectors)

    def first(e, t, shown):
        def enc():
            memory, shown_e, q, k, v, mt, lse, na, ra, act, slope, nb, rb = enc_forward(numbers, src[e], x, e, layer, shown)
            return memory, shown_e, q, k, v, mt, lse, ra, na, act, slope, nb, rb

        def dec():
            low, q, k, v, mt, lse, na, ra = dec_self(numbers, tgt[t], x, t, pair_embed, layer)
            shown_e, act, slope, nb, rb = blank(((count, *nd), BF), (nf, BF), (nf, BF), (nd, BF), (n1, F32))
            return na, shown_e, q, k, v, mt, lse, ra, low, act, slope, nb, rb

        return lax.cond(section_zero, enc, dec)

    def last(e, t, saved_e, d_memory, grads, saved_t, prev):
        def enc():
            _, _, q, k, v, mt, lse, ra, na, act, slope, nb, rb = saved_e
            return tuple(enc_back(numbers, src[e], x, e, d_memory, cot, layer, place, (q, k, v, mt, lse, na, ra, act, slope, nb, rb), prev))

        def dec():
            na, _, q, k, v, mt, lse, ra, low, _, _, _, _ = saved_t
            d_x, pack_a, small = dec_self_back(
                numbers, tgt[t], t, count, grads, layer, place, (low, q, k, v, mt, lse, na, ra), prev
            )
            return d_x, pack_a, blank(((2 * f, d), BF))[0], small

        return lax.cond(section_one, dec, enc)

    saved = [first(0, 1, None)]
    swapped = move(saved[0][0], both)
    near_first, cot_late = lax.optimization_barrier((saved[0][0], cot_late))
    far_cot = move(cot_late, behind)
    x, far_x = lax.optimization_barrier((x, far_x))
    saved.append(first(1, 0, saved[0][1]))
    normed = (swapped, saved[1][0])
    memory = (saved[1][0], swapped)
    crossed = dec_cross(numbers, (mid[1], mid[0]), normed, memory, vectors, cross)
    shown, two, d_memory, pack = dec_mid(
        numbers, (mid[1], mid[0]), ((far_x, 0), (x, 0)), ((far_cot, 0), (cot, 0)), normed, memory, crossed,
        pair_embed, weights, vectors, cross, place, devices,
    )
    near_d_memory = move(d_memory, behind)
    far_two = move(two, ahead)
    mine = lax.psum_scatter(pack, "dp", scatter_dimension=0, tiled=True)
    grads = last(1, 0, saved[1], d_memory, two, saved[1], ())
    shown_late, pack_a = lax.optimization_barrier((shown, grads[1]))
    grads = (grads[0], pack_a, grads[2], grads[3])
    far_shown = move(shown_late, ahead)
    grads = last(0, 1, saved[0], near_d_memory, far_two, saved[0], grads)
    mine, pack_a = lax.optimization_barrier((mine, grads[1]))
    theirs = move(mine, both)
    shares = (padded(4 * d + 16, devices) // devices, 2 * f // devices, cross_rows(devices, d) // devices, 16)
    own = reduce_grads(devices, (shares[0], shares[1], shares[3]), pack_a, grads[2], grads[3])
    pack = gather_grads(devices, shares, mine, theirs, own)
    bases = [devices * sum(shares[:i]) for i in (1, 2, 3)]
    proj, out_w, bias, w_in, b_in, w_out, b_out, gain, offset, c_proj, c_out, c_bias, c_gain, c_offset, pair, shown = unpack(pack, bases, f, saved[1][1], shown, far_shown)
    return (
        shown[None], grads[0][None], proj.reshape(1, 3, d, d), out_w[None], bias[None], w_in[None], b_in, w_out[None], b_out, gain[None], offset[None],
        c_proj.reshape(3, d, d), c_out, c_bias, c_gain[0], c_offset[0], pair,
    )


def solution(mesh):
    s, r = "section", P()
    in_specs = (
        P(s, "dp"), P(s, "dp"), P("dp"), P(None, "dp"), P("dp"),
        P(s), P(s), P(s), P(s), P(s), P(s), P(s), P(s), P(s), r, r, r, r, r, r,
    )
    out_specs = (P(s, "dp"), P(s, "dp"), P(s), P(s), P(s), P(s), P(s), P(s), P(s), P(s), P(s), r, r, r, r, r, r)
    return jax.shard_map(per_device, mesh=mesh, in_specs=in_specs, out_specs=out_specs, check_vma=False)
```

```python
import functools

import jax
import jax.numpy as jnp
import numpy as np
from jax import lax
from jax.experimental import pallas as pl
from jax.experimental.pallas import tpu as pltpu
from jax.sharding import PartitionSpec as P

BF = jnp.bfloat16
F32 = jnp.float32
HEADS = 8
PAIRS = 16
MESH = pl.DeviceIdType.MESH
EPSILON = 1e-05
BLOCKED = -1e30
RB = 512
NN = (((1,), (0,)), ((), ()))
NT = (((1,), (1,)), ((), ()))
TN = (((0,), (0,)), ((), ()))


def dot(left, right, dims=NN):
    return lax.dot_general(left, right, dims, preferred_element_type=F32)


def row_block(index, size=RB):
    return pl.ds(pl.multiple_of(index * size, size), size)


def loop(count, body, unroll=1):
    def step(index, carry):
        body(index)
        return carry

    lax.fori_loop(0, count, step, 0, unroll=unroll)


def lanes_of(half):
    lane = lax.broadcasted_iota(jnp.int32, (1, 128), 1)
    inside = (lane // 64) == half
    spare = lane - 64 * (1 - half)
    ones = (~inside) & (spare < 32)
    block = (~inside) & (spare >= 32)
    flag = (~inside) & (spare == 32)
    return tuple(m.astype(F32) for m in (inside, ones, block, flag))


def inside_of(half):
    return (lax.broadcasted_iota(jnp.int32, (1, 128), 1) // 64) == half


def norm_rows(value):
    centre = jnp.mean(value, -1, keepdims=True)
    centred = value - centre
    rstd = lax.rsqrt(jnp.mean(centred * centred, -1, keepdims=True) + EPSILON)
    return centred * rstd, rstd


def norm_rows_back(normed, rstd, gain, grad):
    scaled = grad * gain
    return rstd * (
        scaled
        - jnp.mean(scaled, -1, keepdims=True)
        - normed * jnp.mean(scaled * normed, -1, keepdims=True)
    )


def gelu_both(hidden):
    phi = 0.5 + 0.5 * lax.erf(hidden * 0.7071067811865476)
    bell = jnp.exp(-0.5 * hidden * hidden)
    return hidden * phi, phi + hidden * (bell * 0.3989422804014327)


def key_fill(count, length):
    position = lax.broadcasted_iota(jnp.int32, (count, 128), 0)
    spare = lax.broadcasted_iota(jnp.int32, (count, 128), 1) % 64
    return jnp.where((spare < 32) | (position < length), jnp.where(spare < 32, 1.0, 0.0), BLOCKED)


def spare_keys(count, length, ones, block):
    position = lax.broadcasted_iota(jnp.int32, (count, 128), 0)
    return ones + jnp.where(position < length, 0.0, BLOCKED) * block


def causal_cut(scores, query_axis):
    query = lax.broadcasted_iota(jnp.int32, scores.shape, query_axis)
    key = lax.broadcasted_iota(jnp.int32, scores.shape, 1 - query_axis)
    return jnp.where(key <= query, scores, BLOCKED)


def mix_forward(queries, keys, values, length, causal, mixed_t, lse):
    count = queries.shape[0]
    span = keys.shape[0]
    size = min(512 if causal else 1024, count)

    def pair(index):
        cols = row_block(index, 128)
        q = queries[:, cols].astype(F32) * 0.125
        k = keys[:, cols].astype(F32)
        vt = values[:, cols].T.astype(F32)
        lane = lax.broadcasted_iota(jnp.int32, (128, 1), 0)
        qa, ka, va = [], [], []
        for half in range(2):
            inside, ones, block, flag = lanes_of(half)
            qa.append((q * inside + flag).astype(BF))
            ka.append((k * inside + spare_keys(span, length, ones, block)).astype(BF))
            va.append(jnp.where((lane // 64) == half, vt, 1.0).astype(BF))

        def scores_of(part, half):
            here = slice(part * size, (part + 1) * size)
            pieces = [(0, part * size, False), (part * size, size, True)] if causal else [(0, span, False)]
            return [
                (start, reach, cut, dot(ka[half][start : start + reach], qa[half][here], NT))
                for start, reach, cut in pieces
                if reach
            ]

        def finish(part, half, scores):
            here = slice(part * size, (part + 1) * size)
            scores = [(start, reach, causal_cut(s, 1) if cut else s) for start, reach, cut, s in scores]
            top = None
            for _, _, s in scores:
                best = jnp.max(s, axis=0, keepdims=True)
                top = best if top is None else jnp.maximum(top, best)
            total = None
            for start, reach, s in scores:
                o = dot(va[half][:, start : start + reach], jnp.exp(s - top).astype(BF))
                total = o if total is None else total + o
            other = 64 * (1 - half)
            mass = total[other : other + 1]
            own = total[64 * half : 64 * half + 64] / mass
            mixed_t[pl.ds(pl.multiple_of(index * 128 + 64 * half, 64), 64), here] = own.astype(BF)
            lse[index * 2 + half, :, here] = top + jnp.log(mass)

        waiting = None
        for tile in [(part, half) for part in range(count // size) for half in range(2)]:
            scores = scores_of(*tile)
            if waiting:
                finish(*waiting)
            waiting = (*tile, scores)
        finish(*waiting)

    loop(4, pair, 2)


def split3(value):
    high = value.astype(BF).astype(F32)
    middle = (value - high).astype(BF).astype(F32)
    low = (value - high - middle).astype(BF).astype(F32)
    return high, middle, low


def place_matrix():
    out = np.zeros((16, 256), np.float32)
    for half in range(2):
        other = 64 * (1 - half)
        for piece in range(3):
            out[half * 4 + piece, other + piece] = 1
            out[8 + half * 4 + piece, 128 + other + piece] = 1
        out[half * 4 + 3, other + 32] = 1
    return out


def mix_back(queries, keys, values, mixed_t, lse, grad_mixed, place, length, causal, d_q, d_k, d_v):
    count = queries.shape[0]
    span = keys.shape[0]
    size = 256 if causal else min(512, count)
    fill = key_fill(span, length)

    def pair(index):
        cols = row_block(index, 128)
        q = queries[:, cols].astype(F32) * 0.125
        k_low = keys[:, cols]
        k = k_low.astype(F32)
        v = values[:, cols].astype(F32)
        g_low = grad_mixed[:, cols]
        g = g_low.astype(F32)
        q_t = q.astype(BF).T
        g_t = g_low.T
        product = g_t.astype(F32) * mixed_t[cols, :].astype(F32)
        row = lax.broadcasted_iota(jnp.int32, (16, count), 0)
        spread = jnp.where((row == 3) | (row == 7), 1.0, 0.0)
        for half in range(2):
            shift = -lse[index * 2 + half]
            delta = -jnp.sum(product[64 * half : 64 * half + 64], axis=0, keepdims=True)
            for base, value in ((0, shift), (8, delta)):
                for piece, part in enumerate(split3(value)):
                    spread = jnp.where(row == base + 4 * half + piece, part, spread)
        extra = dot(spread.astype(BF), place[...], TN)
        qa, ka, va, ga = [], [], [], []
        for half in range(2):
            inside = inside_of(half)
            qa.append(jnp.where(inside, q, extra[:, 0:128]).astype(BF))
            ga.append(jnp.where(inside, g, extra[:, 128:256]).astype(BF))
            ka.append(jnp.where(inside, k, fill).astype(BF))
            va.append(jnp.where(inside, v, 1.0).astype(BF))
        lane = lax.broadcasted_iota(jnp.int32, (size, 128), 1)
        total_k = [None, None]
        total_v = [None, None]

        def grow(total, value):
            if total is None:
                return value
            if total.shape == value.shape:
                return total + value
            known = total.shape[1]
            return jnp.concatenate([total + value[:, :known], value[:, known:]], axis=1)

        for part in range(count // size):
            here = slice(part * size, (part + 1) * size)
            reach = (part + 1) * size if causal else span
            out_q = []
            for half in range(2):
                s = dot(qa[half][here], ka[half][:reach], NT)
                if causal:
                    if part:
                        s = jnp.concatenate([s[:, : part * size], causal_cut(s[:, part * size :], 0)], axis=1)
                    else:
                        s = causal_cut(s, 0)
                probs = jnp.exp(s)
                grads = dot(ga[half][here], va[half][:reach], NT)
                probs_low = probs.astype(BF)
                d_s = (probs * grads).astype(BF)
                total_v[half] = grow(total_v[half], dot(g_t[:, here], probs_low))
                total_k[half] = grow(total_k[half], dot(q_t[:, here], d_s))
                out_q.append(dot(d_s, k_low[:reach]))
            d_q[here, cols] = (jnp.where(lane < 64, out_q[0], out_q[1]) * 0.125).astype(BF)
        for target, total in ((d_k, total_k), (d_v, total_v)):
            joined = jnp.concatenate([total[0][:64], total[1][64:]], axis=0).astype(BF)
            target[:, cols] = joined.T

    loop(4, pair, 2)


class Late:
    def __init__(self, ref, copy):
        self.ref, self.copy = ref, copy

    def get(self):
        if self.copy is not None:
            self.copy.wait()
            self.copy = None
        return self.ref


class Limits:
    def __init__(self, ref, picks):
        self.ref, self.picks = ref, picks

    def __getitem__(self, index):
        if len(self.picks) == 2:
            near, far = self.picks
            return self.ref[near[index] + lax.axis_index("section") * (far[index] - near[index])]
        return self.ref[self.picks[index]]


class Pieces:
    def __init__(self, source, ref, sem):
        self.source, self.ref, self.sem = source, ref, sem

    def wait(self):
        pltpu.make_async_copy(self.source.at[pl.ds(0, self.ref.shape[0])], self.ref, self.sem).wait()


class Leaving:
    def __init__(self, ref, out, sem):
        self.ref, self.out, self.sem = ref, out, sem

    def send(self, rows=None):
        if rows is None:
            pltpu.make_async_copy(self.ref, self.out, self.sem).start()
        else:
            pltpu.make_async_copy(self.ref.at[rows], self.out.at[rows], self.sem).start()

    def part(self, index):
        return Leaving(self.ref.at[index], self.out.at[index], self.sem)

    def finish(self):
        pltpu.make_async_copy(self.ref, self.out, self.sem).wait()


def sds(shape, dtype):
    return jax.ShapeDtypeStruct(shape, dtype)


def vm(shape, dtype):
    return pltpu.VMEM(shape, dtype)


def call(kernel, name, scalars, picks, args, outs, scratch, flops):
    anywhere = pl.BlockSpec(memory_space=pl.ANY)
    inside = pl.BlockSpec(memory_space=pltpu.VMEM)
    operands, in_specs, out_shapes, out_specs, memory, aliases = [], [], [], [], [], {}
    plan_in, plan_out, places = [], [], []
    for value, kind in args:
        places.append(len(operands))
        operands.append(value)
        if kind == "vmem":
            in_specs.append(inside)
            plan_in.append(None)
        else:
            in_specs.append(anywhere)
            if kind[0] == "either":
                _, index, other, other_index = kind
                plan_in.append((len(memory), (index, len(operands), other_index)))
                operands.append(other)
                in_specs.append(anywhere)
                memory.append(vm(value.shape if index is None else value.shape[1:], value.dtype))
                continue
            if kind[0] == "rows":
                plan_in.append((len(memory), kind[2]))
                memory.append(vm(kind[1], value.dtype))
                continue
            index = kind[1] if isinstance(kind, tuple) else None
            plan_in.append((len(memory), index))
            memory.append(vm(value.shape if index is None else value.shape[1:], value.dtype))
    for position, (shape, dtype, kind) in enumerate(outs):
        if kind == "vmem":
            out_shapes.append(sds(shape, dtype))
            out_specs.append(inside)
            plan_out.append(None)
            continue
        out_specs.append(anywhere)
        index, earlier = None, None
        if isinstance(kind, tuple) and kind[0] == "late":
            index, earlier, total = kind[1:]
            out_shapes.append(sds((total, *shape), dtype))
            if earlier is not None:
                aliases[len(operands)] = position
                operands.append(earlier)
                in_specs.append(anywhere)
        else:
            out_shapes.append(sds(shape, dtype))
        plan_out.append((len(memory), index, len(operands) if isinstance(kind, tuple) and kind[0] == "from" else None))
        memory.append(vm(shape, dtype))
        if isinstance(kind, tuple) and kind[0] == "from":
            operands.append(kind[1])
            in_specs.append(anywhere)
    total_in, count_out, count_memory = len(operands), len(outs), len(memory)

    def body(numbers, *refs):
        ins, results = refs[:total_in], refs[total_in : total_in + count_out]
        held = refs[total_in + count_out : total_in + count_out + count_memory]
        own = refs[total_in + count_out + count_memory : -1]
        sems = refs[-1]
        first, last = [], []
        for spot, plan in zip(places, plan_in):
            ref = ins[spot]
            if plan is None:
                first.append(ref)
                continue
            where, index = plan
            if isinstance(index, tuple):
                index, other, other_index = index
                copies = [
                    pltpu.make_async_copy(r if i is None else r.at[i], held[where], sems.at[where])
                    for r, i in ((ref, index), (ins[other], other_index))
                ]
                section = lax.axis_index("section")
                pl.when(section == 0)(copies[0].start)
                pl.when(section == 1)(copies[1].start)
                first.append(Late(held[where], copies[0]))
                continue
            if isinstance(index, list):
                for begin, end, size in index:
                    pltpu.make_async_copy(ref.at[pl.ds(begin, size)], held[where].at[pl.ds(end, size)], sems.at[where]).start()
                first.append(Late(held[where], Pieces(ref, held[where], sems.at[where])))
                continue
            copy = pltpu.make_async_copy(ref if index is None else ref.at[index], held[where], sems.at[where])
            copy.start()
            first.append(Late(held[where], copy))
        for ref, plan in zip(results, plan_out):
            if plan is None:
                last.append(ref)
                continue
            where, index, source = plan
            leaving = Leaving(held[where], ref if index is None else ref.at[index], sems.at[where])
            if source is not None:
                copy = pltpu.make_async_copy(ins[source], held[where], sems.at[where])
                copy.start()
                leaving.begin = Late(held[where], copy)
            last.append(leaving)
        kernel(Limits(numbers, picks), *first, *last, *own)
        for leaving in last:
            if isinstance(leaving, Leaving):
                leaving.finish()

    return pl.pallas_call(
        body,
        name=name,
        out_shape=out_shapes,
        in_specs=[pl.BlockSpec(memory_space=pltpu.SMEM), *in_specs],
        out_specs=out_specs,
        scratch_shapes=[*memory, *[vm(*s) for s in scratch], pltpu.SemaphoreType.DMA((max(count_memory, 1),))],
        input_output_aliases={i + 1: o for i, o in aliases.items()},
        compiler_params=pltpu.CompilerParams(vmem_limit_bytes=62 * 2**20),
        cost_estimate=pl.CostEstimate(flops=int(flops), bytes_accessed=20 * 2**20, transcendentals=0),
    )(scalars, *operands)


def valid_rows(index, limit, size=RB):
    return (lax.broadcasted_iota(jnp.int32, (size, 1), 0) + index * size < limit).astype(F32)


def ffn_rows(z_low, w_in, c_in, w_out, c_out, act_ref, slope_ref, r, flipped=False):
    def hidden(c):
        cols = slice(c * 512, c * 512 + 512)
        return dot(z_low, w_in[cols], NT) + c_in[c : c + 1] if flipped else dot(z_low, w_in[:, cols]) + c_in[:, cols]

    total, coming = None, hidden(0)
    for c in range(4):
        cols = slice(c * 512, c * 512 + 512)
        here = coming
        coming = hidden(c + 1) if c < 3 else None
        act, slope = gelu_both(here)
        act = act.astype(BF)
        act_ref[r, cols] = act
        slope_ref[r, cols] = slope.astype(BF)
        part = dot(act, w_out[cols])
        total = part if total is None else total + part
    return total + c_out[...]


def put(target, rows, value, later):
    target[rows] = (value + target[rows].astype(F32) if later else value).astype(BF)


def ffn_back(grad_low, act, slope, z_low, w_in, w_out, put_rows, small, on_rows, flipped=False):
    def body(index):
        r = row_block(index)
        g = grad_low[r]
        total, coming = None, dot(g, w_out[0:512], NT)
        for c in range(4):
            cols = slice(c * 512, c * 512 + 512)
            here = coming
            coming = dot(g, w_out[512 * c + 512 : 512 * c + 1024], NT) if c < 3 else None
            dh = (here * slope[r, cols].astype(F32)).astype(BF)
            slope[r, cols] = dh
            small[3 + c : 4 + c] += jnp.sum(dh.astype(F32), axis=0, keepdims=True)
            part = dot(dh, w_in[cols]) if flipped else dot(dh, w_in[:, cols], NT)
            total = part if total is None else total + part
        small[7:8] += jnp.sum(g.astype(F32), axis=0, keepdims=True)
        on_rows(r, total)

    loop(grad_low.shape[0] // RB, body)
    z = z_low[...]
    g = grad_low[...]
    act = act.get() if isinstance(act, Late) else act
    for c in range(4):
        cols = slice(c * 512, c * 512 + 512)
        put_rows(c * 512, dot(z, slope[:, cols], TN))
        put_rows(2048 + c * 512, dot(act[:, cols], g, TN))


def project(count, x_low, proj, bias, q, k, v):
    def body(index):
        r = row_block(index)
        x = x_low(r)
        q.ref[r] = (dot(x, proj[0]) + bias[0:1]).astype(BF)
        k.ref[r] = dot(x, proj[1]).astype(BF)
        v.ref[r] = (dot(x, proj[2]) + bias[1:2]).astype(BF)

    loop(count // RB, body)
    q.send()
    k.send()
    v.send()


def self_back(x, proj, out_w, q, k, v, mixed_t, lse, place, length, causal, grad_low, grad_mixed, d_q, d_k, d_v, pack, later, small, rest):
    grad_mixed[...] = dot(grad_low[...], out_w.get()[...], NT).astype(BF)
    mixed_t = mixed_t.get()
    if later:
        pack.begin.get()
    put(pack.ref, slice(1536, 2048), dot(mixed_t[...], grad_low[...]), later)
    q, k, v, x = q.get(), k.get(), v.get(), x.get()
    mix_back(q, k, v, mixed_t, lse, grad_mixed, place, length, causal, d_q, d_k, d_v)
    small[0:1] += jnp.sum(d_q[...].astype(F32), axis=0, keepdims=True)
    small[1:2] += jnp.sum(d_v[...].astype(F32), axis=0, keepdims=True)
    small[2:3] += jnp.sum(grad_low[...].astype(F32), axis=0, keepdims=True)
    xl = x[...]
    put(pack.ref, slice(0, 512), dot(xl, d_q[...], TN), later)
    put(pack.ref, slice(512, 1024), dot(xl, d_k[...], TN), later)
    put(pack.ref, slice(1024, 1536), dot(xl, d_v[...], TN), later)
    pack.send()
    proj = proj.get()

    def body(index):
        r = row_block(index)
        rest(r, dot(d_q[r], proj[0], NT) + dot(d_k[r], proj[1], NT) + dot(d_v[r], proj[2], NT))

    loop(x.shape[0] // RB, body)


def begin_small(small, earlier):
    small[...] = jnp.zeros(small.shape, F32) if earlier is None else earlier[...]


def enc_forward_kernel(
    length, x, proj, out_w, w_in, w_out, bias, c_in, c_out, gain, offset,
    memory, shown, q, k, v, mixed_t, lse, normed1, rstd1, act, slope, normed2, rstd2,
):
    x = x.get()
    project(x.shape[0], lambda r: x[r], proj.get(), bias, q, k, v)
    mix_forward(q.ref, k.ref, v.ref, length[0], False, mixed_t.ref, lse)
    mixed_t.send()
    out_w, w_in, w_out = out_w.get(), w_in.get(), w_out.get()

    def body(index):
        r = row_block(index)
        xf = x[r].astype(F32)
        n1, s1 = norm_rows(xf + dot(mixed_t.ref[:, r], out_w[...], TN) + bias[2:3])
        normed1.ref[r] = n1.astype(BF)
        rstd1[r] = s1
        y = n1 * gain[0:1] + offset[0:1]
        f = ffn_rows(y.astype(BF), w_in, c_in, w_out, c_out, act.ref, slope.ref, r)
        n2, s2 = norm_rows(y + f + xf)
        normed2.ref[r] = n2.astype(BF)
        rstd2[r] = s2
        result = n2 * gain[1:2] + offset[1:2]
        memory.ref[r] = result.astype(BF)
        shown.ref[r] = (result * valid_rows(index, length[1])).astype(BF)
        for leaving in (act, slope, memory, shown, normed1, normed2):
            leaving.send(r)

    loop(x.shape[0] // RB, body)


def enc_forward(scalars, picks, x, s, layer, shown):
    proj, out_w, bias, w_in, c_in, w_out, c_out, gain, offset = layer
    count, n, d = x.shape
    f = w_in.shape[1]
    nd = (n, d)
    args = [(x, ("late", s)), (proj, "late"), (out_w, "late"), (w_in, "late"), (w_out, "late")]
    args += [(v, "vmem") for v in (bias, c_in, c_out, gain, offset)]
    outs = [
        (nd, BF, "late"), (nd, BF, ("late", s, shown, count)), (nd, BF, "late"), (nd, BF, "late"), (nd, BF, "late"), ((d, n), BF, "late"),
        ((8, 1, n), F32, "vmem"), (nd, BF, "late"), ((n, 1), F32, "vmem"), ((n, f), BF, "late"), ((n, f), BF, "late"), (nd, BF, "late"), ((n, 1), F32, "vmem"),
    ]
    return call(enc_forward_kernel, "encoder_forward", scalars, picks, args, outs, [], 15e9)


def enc_back_kernel(
    later, length, cot, d_memory, normed2, normed1, w_out, slope, w_in, act, out_w, mixed_t, q, k, v, x, proj,
    lse, rstd1, rstd2, gain, offset, place, *refs,
):
    earlier = refs[0] if later else None
    d_x, pack_a, pack_b, small, last, grad_low, z_low, grad_mixed, d_q, d_k, d_v = refs[later:]
    begin_small(small, earlier)
    cot, d_memory, normed2, normed1 = cot.get(), d_memory.get(), normed2.get(), normed1.get()

    def top(index):
        r = row_block(index)
        n2 = normed2[r].astype(F32)
        g = cot[r].astype(F32) * valid_rows(index, length[1]) + d_memory[r].astype(F32)
        small[9:10] += jnp.sum(g * n2, axis=0, keepdims=True)
        small[11:12] += jnp.sum(g, axis=0, keepdims=True)
        g = norm_rows_back(n2, rstd2[r], gain[1:2], g)
        last[r] = g
        grad_low[r] = g.astype(BF)
        z_low[r] = (normed1[r].astype(F32) * gain[0:1] + offset[0:1]).astype(BF)

    loop(last.shape[0] // RB, top)

    def middle(r, grad):
        n1 = normed1[r].astype(F32)
        g = last[r] + grad
        small[8:9] += jnp.sum(g * n1, axis=0, keepdims=True)
        small[10:11] += jnp.sum(g, axis=0, keepdims=True)
        g = norm_rows_back(n1, rstd1[r], gain[0:1], g)
        last[r] = last[r] + g
        grad_mixed[r] = g.astype(BF)

    def put_rows(start, value):
        if later:
            pack_b.begin.get()
        put(pack_b.ref, slice(start, start + 512), value, later)

    ffn_back(grad_low, act, slope.get(), z_low, w_in.get(), w_out.get(), put_rows, small, middle)
    pack_b.send()
    grad_low[...] = grad_mixed[...]

    def rest(r, grad):
        d_x.ref[r] = last[r] + grad
        d_x.send(r)

    self_back(x, proj, out_w, q, k, v, mixed_t, lse, place, length[0], False, grad_low, grad_mixed, d_q, d_k, d_v, pack_a, later, small, rest)


def enc_back(scalars, picks, x, s, d_memory, cot, layer, place, saved, prev):
    proj, out_w, bias, w_in, c_in, w_out, c_out, gain, offset = layer
    q, k, v, mixed_t, lse, normed1, rstd1, act, slope, normed2, rstd2 = saved
    count, n, d = x.shape
    f = w_in.shape[1]
    nd = (n, d)
    args = [(cot, ("late", s))]
    args += [(a, "late") for a in (d_memory, normed2, normed1, w_out, slope, w_in, act, out_w, mixed_t, q, k, v)]
    args += [(x, ("late", s)), (proj, "late")]
    args += [(a, "vmem") for a in (lse, rstd1, rstd2, gain, offset, place)]
    carry = lambda i: ("from", prev[i]) if prev else "late"
    if prev:
        args.append((prev[3], "vmem"))
    outs = [(nd, F32, ("late", s, prev[0] if prev else None, count)), ((4 * d, d), BF, carry(1)), ((2 * f, d), BF, carry(2)), ((16 + PAIRS, d), F32, "vmem")]
    scratch = [(nd, F32)] + [(nd, BF)] * 6
    return call(functools.partial(enc_back_kernel, bool(prev)), "encoder_back", scalars, picks, args, outs, scratch, 35e9)


def dec_self_kernel(length, x, proj, out_w, pair_table, bias, gain, offset, x_low, q, k, v, mixed_t, lse, normed1, rstd1):
    x = x.get()
    pair_row = pair_table[pl.ds(length[2], 1)]

    def low(r):
        value = (x[r].astype(F32) + pair_row).astype(BF)
        x_low.ref[r] = value
        return value

    project(x.shape[0], low, proj.get(), bias, q, k, v)
    x_low.send()
    mix_forward(q.ref, k.ref, v.ref, length[0], True, mixed_t.ref, lse)
    mixed_t.send()
    out_w = out_w.get()

    def body(index):
        r = row_block(index)
        n1, s1 = norm_rows(x[r].astype(F32) + pair_row + dot(mixed_t.ref[:, r], out_w[...], TN) + bias[2:3])
        normed1.ref[r] = n1.astype(normed1.ref.dtype)
        rstd1[r] = s1
        normed1.send(r)

    loop(x.shape[0] // RB, body)


def dec_self(scalars, picks, x, s, pair_table, layer):
    proj, out_w, bias, w_in, c_in, w_out, c_out, gain, offset = layer
    count, n, d = x.shape
    nd = (n, d)
    args = [(x, ("late", s)), (proj, "late"), (out_w, "late")]
    args += [(v, "vmem") for v in (pair_table, bias, gain, offset)]
    outs = [(nd, BF, "late")] * 4 + [((d, n), BF, "late"), ((8, 1, n), F32, "vmem"), (nd, BF, "late"), ((n, 1), F32, "vmem")]
    return call(dec_self_kernel, "decoder_self", scalars, picks, args, outs, [], 8e9)


def padded(rows, count):
    return -(-rows // (16 * count)) * (16 * count)


def cross_rows(count, d):
    return padded(4 * d, count)


def dec_cross_kernel(
    length, normed1, c_proj, memory, c_bias, vectors,
    q, k, v, mixed_t, lse,
):
    gain, offset = vectors[5:6], vectors[7:8]
    normed1, c_proj = normed1.get(), c_proj.get()

    def queries(index):
        r = row_block(index)
        y = (normed1[r].astype(F32) * gain + offset).astype(BF)
        q.ref[r] = (dot(y, c_proj[0]) + c_bias[0:1]).astype(BF)

    loop(normed1.shape[0] // RB, queries)
    q.send()
    memory = memory.get()

    def keys(index):
        r = row_block(index)
        m = memory[r]
        k.ref[r] = dot(m, c_proj[1]).astype(BF)
        v.ref[r] = (dot(m, c_proj[2]) + c_bias[1:2]).astype(BF)

    loop(memory.shape[0] // RB, keys)
    k.send()
    v.send()
    mix_forward(q.ref, k.ref, v.ref, length[0], False, mixed_t.ref, lse)
    mixed_t.send()


def dec_mid_kernel(
    share_b, share_c, length, normed1, mixed_t, c_out, w_in, w_out, x, cot, q, k, v, c_proj, memory,
    lse, pair_table, c_bias, c_gain, c_offset, vectors, place,
    shown, two, d_memory, pack,
    small, last, top, y_low, z_low, normed2, rstd2, act, slope, grad_low, grad_mixed, d_q, d_k, d_v,
):
    small[...] = jnp.zeros(small.shape, F32)
    grad_last, grad_first = (two.part(i) for i in range(2))
    c_in, c_out_b, gain, offset = vectors[0:4], vectors[4:5], vectors[5:7], vectors[7:9]
    pair_row = pair_table[pl.ds(length[2], 1)]

    def put_part(start, value, share, shift):
        value = value.astype(BF)
        done = 0
        while done < value.shape[0]:
            owner, inner = divmod(start + done, share)
            size = min(share - inner, value.shape[0] - done)
            begin = owner * (share_b + share_c + 16) + shift + inner
            pack.ref[begin : begin + size] = value[done : done + size]
            done += size

    def put_b(start, value):
        put_part(start, value, share_b, 0)

    def put_c(start, value):
        put_part(start, value, share_c, share_b)

    normed1, mixed_t, c_out, w_in, w_out, x, cot = (a.get() for a in (normed1, mixed_t, c_out, w_in, w_out, x, cot))
    count = normed1.shape[0]

    def forward(index):
        r = row_block(index)
        y = normed1[r].astype(F32) * gain[0:1] + offset[0:1]
        y_low[r] = y.astype(BF)
        n2, s2 = norm_rows(y + dot(mixed_t[:, r], c_out[...], TN) + c_bias[2:3])
        normed2[r] = n2.astype(BF)
        rstd2[r] = s2
        z = n2 * c_gain[...] + c_offset[...]
        zl = z.astype(BF)
        z_low[r] = zl
        f = ffn_rows(zl, w_in, c_in, w_out, c_out_b, act, slope, r, True)
        n3, s3 = norm_rows(z + f + x[r].astype(F32) + pair_row)
        valid = valid_rows(index, length[1])
        shown.ref[r] = ((n3 * gain[1:2] + offset[1:2]) * valid).astype(BF)
        shown.send(r)
        g = cot[r].astype(F32) * valid
        small[9:10] += jnp.sum(g * n3, axis=0, keepdims=True)
        small[11:12] += jnp.sum(g, axis=0, keepdims=True)
        g = norm_rows_back(n3, s3, gain[1:2], g)
        last[r] = g
        grad_last.ref[r] = g.astype(BF)

    loop(count // RB, forward)
    grad_last.send()

    def middle(r, grad):
        n2 = normed2[r].astype(F32)
        g = last[r] + grad
        small[8:9] += jnp.sum(g * n2, axis=0, keepdims=True)
        small[10:11] += jnp.sum(g, axis=0, keepdims=True)
        g = norm_rows_back(n2, rstd2[r], c_gain[...], g)
        top[r] = g
        grad_low[r] = g.astype(BF)

    ffn_back(grad_last.ref, act, slope, z_low, w_in, w_out, put_b, small, middle, True)
    grad_mixed[...] = dot(grad_low[...], c_out[...], NT).astype(BF)
    put_c(1536, dot(mixed_t[...], grad_low[...]))
    q, k, v = q.get(), k.get(), v.get()
    mix_back(q, k, v, mixed_t, lse, grad_mixed, place, length[0], False, d_q, d_k, d_v)
    c_proj, memory = c_proj.get(), memory.get()
    span = memory.shape[0]

    def back(index):
        r = row_block(index)
        d_memory.ref[r] = (dot(d_k[r], c_proj[1], NT) + dot(d_v[r], c_proj[2], NT)).astype(BF)
        d_memory.send(r)

    loop(span // RB, back)

    def first(index):
        r = row_block(index)
        grad_first.ref[r] = (top[r] + dot(d_q[r], c_proj[0], NT)).astype(BF)
        grad_first.send(r)

    loop(count // RB, first)
    small[0:1] += jnp.sum(d_q[...].astype(F32), axis=0, keepdims=True)
    small[1:2] += jnp.sum(d_v[...].astype(F32), axis=0, keepdims=True)
    small[2:3] += jnp.sum(grad_low[...].astype(F32), axis=0, keepdims=True)
    m = memory[...]
    put_c(0, dot(y_low[...], d_q[...], TN))
    put_c(512, dot(m, d_k[...], TN))
    put_c(1024, dot(m, d_v[...], TN))
    for owner in range(pack.ref.shape[0] // (share_b + share_c + 16)):
        begin = owner * (share_b + share_c + 16) + share_b + share_c
        pack.ref[begin : begin + 16] = (small[...] if owner == 2 else jnp.zeros((16, 512), F32)).astype(BF)
    pack.send()


def dec_mid(scalars, picks, x, cot, normed1, memory, crossed, pair_table, weights, vectors, cross, place, count):
    c_proj, c_out_w, c_bias, c_gain, c_offset = cross
    q, k, v, mixed_t, lse = crossed
    n, d = normed1[0].shape
    m = memory[0].shape[0]
    f = weights.shape[0] // 2
    nd, md = (n, d), (m, d)
    part = f // count
    share_b, share_c = 2 * f // count, cross_rows(count, d) // count
    either = lambda pair: (pair[0], ("either", None, pair[1], None))
    args = [either(normed1), (mixed_t, "late"), (c_out_w, "late")]
    args += [(weights, ("rows", (f, d), [(2 * part * i + part * j, part * i, part) for i in range(count)])) for j in range(2)]
    args += [(a[0][0], ("either", a[0][1], a[1][0], a[1][1])) for a in (x, cot)]
    args += [(a, "late") for a in (q, k, v, c_proj)] + [either(memory)]
    args += [(a, "vmem") for a in (lse, pair_table, c_bias, c_gain, c_offset, vectors, place)]
    outs = [(nd, BF, "late"), ((2, n, d), BF, "late"), (md, BF, "late"), ((count * (share_b + share_c + 16), d), BF, "late")]
    scratch = [((16, d), F32), (nd, F32), (nd, F32), (nd, BF), (nd, BF)]
    scratch += [(nd, BF), ((n, 1), F32), ((n, f), BF), ((n, f), BF), (nd, BF), (nd, BF), (nd, BF), (md, BF), (md, BF)]
    return call(functools.partial(dec_mid_kernel, share_b, share_c), "decoder_middle", scalars, picks, args, outs, scratch, 45e9)


def dec_cross(scalars, picks, normed1, memory, vectors, cross):
    c_proj, c_out_w, c_bias, c_gain, c_offset = cross
    n, d = normed1[0].shape
    m = memory[0].shape[0]
    either = lambda pair: (pair[0], ("either", None, pair[1], None))
    args = [either(normed1), (c_proj, "late"), either(memory), (c_bias, "vmem"), (vectors, "vmem")]
    outs = [((n, d), BF, "late"), ((m, d), BF, "late"), ((m, d), BF, "late"), ((d, n), BF, "late"), ((8, 1, n), F32, "vmem")]
    return call(dec_cross_kernel, "decoder_cross", scalars, picks, args, outs, [], 11e9)


def dec_self_back_kernel(
    later, length, grad_first, normed1, grad_last, out_w, mixed_t, q, k, v, x_low, proj,
    lse, rstd1, gain, place, *refs,
):
    earlier = refs[0] if later else None
    d_x, pack_a, small, last, grad_low, grad_mixed, d_q, d_k, d_v, column = refs[later:]
    begin_small(small, earlier)
    column[...] = jnp.zeros(column.shape, F32)
    grad_first, normed1, grad_last = grad_first.get(), normed1.get(), grad_last.get()

    def top(index):
        r = row_block(index)
        n1 = normed1[r].astype(F32)
        g = grad_first[r].astype(F32)
        small[8:9] += jnp.sum(g * n1, axis=0, keepdims=True)
        small[10:11] += jnp.sum(g, axis=0, keepdims=True)
        g = norm_rows_back(n1, rstd1[r], gain[0:1], g)
        last[r] = grad_last[r].astype(F32) + g
        grad_low[r] = g.astype(BF)

    loop(last.shape[0] // RB, top)

    def rest(r, grad):
        g = last[r] + grad
        d_x.ref[r] = g
        d_x.send(r)
        column[0:1] += jnp.sum(g, axis=0, keepdims=True)

    self_back(x_low, proj, out_w, q, k, v, mixed_t, lse, place, length[0], True, grad_low, grad_mixed, d_q, d_k, d_v, pack_a, later, small, rest)
    pair_mark = lax.broadcasted_iota(jnp.int32, (PAIRS, 1), 0) == length[2]
    small[16:] += jnp.where(pair_mark, column[0:1], 0.0)


def dec_self_back(scalars, picks, s, count, two, layer, place, saved, prev):
    proj, out_w, bias, w_in, c_in, w_out, c_out, gain, offset = layer
    x_low, q, k, v, mixed_t, lse, normed1, rstd1 = saved
    n, d = x_low.shape
    nd = (n, d)
    args = [(two, ("late", 1)), (normed1, "late"), (two, ("late", 0))]
    args += [(a, "late") for a in (out_w, mixed_t, q, k, v, x_low, proj)]
    args += [(a, "vmem") for a in (lse, rstd1, gain, place)]
    if prev:
        args.append((prev[3], "vmem"))
    outs = [(nd, F32, ("late", s, prev[0] if prev else None, count)), ((4 * d, d), BF, ("from", prev[1]) if prev else "late"), ((16 + PAIRS, d), F32, "vmem")]
    scratch = [(nd, F32)] + [(nd, BF)] * 5 + [((8, d), F32)]
    return call(functools.partial(dec_self_back_kernel, bool(prev)), "decoder_self_back", scalars, picks, args, outs, scratch, 20e9)


def add_rows(target, start, size, sources):
    block = max(b for b in range(16, min(size, 96) + 1, 16) if size % b == 0)

    def body(index):
        here = pl.ds(pl.multiple_of(start + index * block, 16), block)
        value = 0.0
        for ref, begin in sources:
            value = value + ref[pl.ds(pl.multiple_of(begin + index * block, 16), block)].astype(F32)
        target[here] = value.astype(BF)

    loop(size // block, body)


class Ring:
    def __init__(self, count):
        self.m = m = count // 2
        self.me = lax.axis_index("dp")
        self.core = self.me % 2
        chip = self.me // 2
        turn = (chip // 2) * (1 - chip % 2) + (m - 1 - chip // 2) * (chip % 2)
        back = (m - turn) % m
        self.place = turn * (1 - self.core) + back * self.core
        self.place_other = turn * self.core + back * (1 - self.core)
        self.other = self.me + 1 - 2 * self.core
        self.after = self.device(self.place + 1, self.core)
        self.before = self.device(self.place + m - 1, self.core)

    def device(self, place, core):
        m = self.m
        place = place % m
        turn = place * (1 - core) + ((m - place) % m) * core
        odd = turn // (m // 2)
        return 2 * (2 * (turn * (1 - odd) + (m - 1 - turn) * odd) + odd) + core


def rows_of(ref, start, size):
    return ref.at[pl.ds(pl.multiple_of(start, 16), size)]


class Copies:
    def __init__(self, send_sem, recv_sem):
        self.send_sem, self.recv_sem, self.used = send_sem, recv_sem, 0

    def remote(self, src, dst, device):
        index = self.used
        self.used += 1
        return pltpu.make_async_remote_copy(
            src, dst, self.send_sem.at[index], self.recv_sem.at[index], device_id=device, device_id_type=MESH
        )


def halves(size):
    first = size // 32 * 16
    return [(0, first), (first, size - first)] if first else [(0, size)]


def reduce_kernel(count, shares, a, b, own, out, work, inbox, pairbox, load_sem, send_sem, recv_sem):
    ring = Ring(count)
    m, core, place = ring.m, ring.core, ring.place
    section = lax.axis_index("section")
    na, nb, width = a.shape[0], b.shape[0], a.shape[1]
    bases = (0, count * shares[0], count * (shares[0] + shares[1]))
    starts = (0, shares[0], shares[0] + shares[1])
    loads = [
        pltpu.make_async_copy(a, work.at[pl.ds(0, na)], load_sem.at[0]),
        pltpu.make_async_copy(b, work.at[pl.ds(bases[1], nb)], load_sem.at[1]),
    ]
    for copy in loads:
        copy.start()
    barrier = pltpu.get_barrier_semaphore()
    for device in (ring.after, ring.before, ring.other):
        pl.semaphore_signal(barrier, inc=1, device_id={"dp": device}, device_id_type=MESH)
    blank = jnp.zeros((count * shares[2] - own.shape[0], width), F32)
    work[bases[2] : bases[2] + count * shares[2]] = jnp.concatenate([own[16:32], own[0:16], blank]).astype(BF)
    for copy in loads:
        copy.wait()
    pl.semaphore_wait(barrier, 3)
    copies = Copies(send_sem, recv_sem)
    units = [(region, offset, size) for region in range(3) for offset, size in halves(shares[region])]
    boxes, total = [], 0
    for _, _, size in units:
        boxes.append(total)
        total += size

    def where(region, action):
        if region == 1:
            pl.when(section == 0)(action)
        else:
            action()

    near, far = m // 2, m - 1 - m // 2

    def order(place):
        chunks = []
        for s in range(near):
            chunks.append(place + near - s)
            if s < far:
                chunks.append(place + 2 * m - far + s)
        return chunks + [place + m]

    pairs = []
    for t, chunk in enumerate(order(ring.place_other)):
        owner = ring.device(chunk, 1 - core)
        row = []
        for region in range(3):
            size = shares[region]
            row.append(
                copies.remote(
                    rows_of(work, bases[region] + owner * size, size),
                    pairbox.at[pl.ds(t * sum(shares) + starts[region], size)],
                    {"dp": ring.other},
                )
            )
            where(region, row[region].start)
        pairs.append(row)
    slots = [(s, way) for s in range(near) for way in range(2) if way == 0 or s < far]
    box_of = {slot: i for i, slot in enumerate(slots)}
    sends = {}
    for t, chunk in enumerate(order(place)):
        s, way = slots[t] if t < m - 1 else (None, None)
        owner = ring.device(chunk, core)
        for region in range(3):
            where(region, pairs[t][region].wait_recv)
        for u, (region, offset, size) in enumerate(units):
            start = bases[region] + owner * shares[region] + offset
            if s is None:
                before = [(near - 1, 0), (far - 1, 1)] if far else [(near - 1, 0)]
            else:
                before = [(s - 1, way)] if s else []
                target = ring.after if way == 0 else ring.before
                box = box_of[(s, way)] * total + boxes[u]
                sends[(s, way, u)] = copies.remote(rows_of(work, start, size), inbox.at[pl.ds(box, size)], {"dp": target})

            def step(t=t, s=s, way=way, u=u, region=region, offset=offset, size=size, start=start, before=before):
                sources = [(work, start), (pairbox, t * sum(shares) + starts[region] + offset)]
                for slot in before:
                    sends[(*slot, u)].wait_recv()
                    sources.append((inbox, box_of[slot] * total + boxes[u]))
                if s is None:
                    add_rows(out, starts[region] + offset, size, sources)
                else:
                    add_rows(work, start, size, sources)
                    sends[(s, way, u)].start()

            where(region, step)
    for row in pairs:
        for region in range(3):
            where(region, row[region].wait_send)
    for (s, way, u), copy in sends.items():
        where(units[u][0], copy.wait_send)


def reduce_grads(count, shares, a, b, own):
    d = a.shape[1]
    m = count // 2
    width = sum(shares)
    units = sum(len(halves(s)) for s in shares)
    slots = (m - 1) * units + m * 3
    anywhere = pl.BlockSpec(memory_space=pl.ANY)
    inside = pl.BlockSpec(memory_space=pltpu.VMEM)
    return pl.pallas_call(
        functools.partial(reduce_kernel, count, shares),
        name="gradient_reduce",
        out_shape=sds((width, d), BF),
        in_specs=[anywhere] * 2 + [inside],
        out_specs=inside,
        scratch_shapes=[
            vm((count * width, d), BF),
            vm(((m - 1) * width, d), BF),
            vm((m * width, d), BF),
            pltpu.SemaphoreType.DMA((2,)),
            pltpu.SemaphoreType.DMA((slots,)),
            pltpu.SemaphoreType.DMA((slots,)),
        ],
        compiler_params=pltpu.CompilerParams(collective_id=0, has_side_effects=True, vmem_limit_bytes=48 * 2**20),
    )(a, b, own)


def gather_kernel(count, shares, mine, theirs, own, shown, out, shown_far, final, out_sem, send_sem, recv_sem):
    ring = Ring(count)
    m, core, place = ring.m, ring.core, ring.place
    section = lax.axis_index("section")
    decoder = section == 1
    barrier = pltpu.get_barrier_semaphore()
    for device in (ring.after, ring.before, ring.other):
        pl.semaphore_signal(barrier, inc=1, device_id={"dp": device}, device_id_type=MESH)
    pl.semaphore_signal(barrier, inc=1, device_id={"section": 1 - section}, device_id_type=MESH)
    bases = [0]
    for share in shares:
        bases.append(bases[-1] + count * share)
    s0, s1, s2, s3 = shares
    me = ring.me
    split = s2 % 32 == 0
    half = s2 // 2 if split else s2
    near_half = section * half if split else 0
    far_half = half - near_half

    def low(region, place, core):
        return bases[region] + ring.device(place, core) * shares[region]

    def part(region, place, core):
        start = low(region, place, core)
        return (start + near_half, half) if region == 2 else (start, shares[region])

    def here(region):
        return pl.ds(pl.multiple_of(low(region, place, core), 16), shares[region])

    final[here(0)] = own[0:s0]
    final[here(2)] = (mine[s1 : s1 + s2].astype(F32) + theirs[s1 : s1 + s2].astype(F32)).astype(BF)

    @pl.when(decoder)
    def _():
        final[here(1)] = (mine[0:s1].astype(F32) + theirs[0:s1].astype(F32)).astype(BF)

    @pl.when(section == 0)
    def _():
        final[here(1)] = own[s0 : s0 + s1]

    @pl.when(me == 2)
    def _():
        final[here(3)] = (mine[s1 + s2 :].astype(F32) + theirs[s1 + s2 :].astype(F32)).astype(BF)

    @pl.when((me != 2) & ((me != 0) | decoder))
    def _():
        final[here(3)] = own[s0 + s1 :]

    pl.semaphore_wait(barrier, 4)
    copies = Copies(send_sem, recv_sem)
    pair = rows_of(final, low(3, place, core), s3)
    across = copies.remote(pair, pair, {"section": 1 - section})
    pl.when(decoder & (me == 0))(across.start)
    hand = copies.remote(shown, shown_far, {"section": 1 - section})
    pl.when(section == 0)(hand.start)
    near, far = m // 2, m - 1 - m // 2
    passes, shared, arrived, crossed, waiting = {}, [], [], [], []

    def keep(start, size):
        rows = pl.ds(pl.multiple_of(start, 16), size)
        pltpu.make_async_copy(final.at[rows], out.at[rows], out_sem.at[0]).start()

    def give(start, size, far_start):
        block = rows_of(final, start, size)
        shared.append(copies.remote(block, block, {"dp": ring.other}))
        shared[-1].start()
        keep(start, size)
        arrived.append((far_start, size))

    def take_crossed():
        while waiting:
            copy, shift = waiting.pop(0)
            copy.wait_recv()
            give(low(2, place + shift, core) + far_half, half, low(2, ring.place_other + shift, 1 - core) + far_half)

    for s in range(near + 1):
        fresh = []
        for way in range(2):
            if (way == 1 and s > far) or (s == 0 and way == 1 and not far):
                continue
            shift = 2 * m - s if way == 0 else s
            limit, target = (near, ring.after) if way == 0 else (far, ring.before)
            for region in range(4):
                start, size = part(region, place + shift, core)
                block = rows_of(final, start, size)
                if s:
                    passes[(s - 1, way, region)].wait_recv()
                elif region == 3 and way == 0:
                    pl.when((section == 0) & (me == 0))(across.wait_recv)
                if s < limit:
                    passes[(s, way, region)] = copies.remote(block, block, {"dp": target})
                    passes[(s, way, region)].start()
                if s:
                    if region == 2 and split:
                        crossed.append(copies.remote(block, block, {"section": 1 - section}))
                        crossed[-1].start()
                        fresh.append((crossed[-1], shift))
                    give(start, size, part(region, ring.place_other + shift, 1 - core)[0])
                elif way == 0:
                    give(low(region, place, core), shares[region], low(region, ring.place_other, 1 - core))
        take_crossed()
        waiting.extend(fresh)
    take_crossed()
    for copy, (start, size) in zip(shared, arrived):
        copy.wait_recv()
        keep(start, size)
    for copy in [*passes.values(), *shared, *crossed]:
        copy.wait_send()
    pl.when(decoder & (me == 0))(across.wait_send)
    pl.when(section == 0)(hand.wait_send)
    pl.when(decoder)(hand.wait_recv)
    pltpu.make_async_copy(final, out, out_sem.at[0]).wait()


def gather_grads(count, shares, mine, theirs, own, shown):
    d = own.shape[1]
    m = count // 2
    rows = count * sum(shares)
    slots = (2 * m - 1) * 4 + 2 + 2 * (m - 1)
    inside = pl.BlockSpec(memory_space=pltpu.VMEM)
    return pl.pallas_call(
        functools.partial(gather_kernel, count, shares),
        name="gradient_gather",
        out_shape=[sds((rows, d), BF), sds(shown.shape, BF)],
        in_specs=[inside] * 3 + [pl.BlockSpec(memory_space=pl.ANY)],
        out_specs=[pl.BlockSpec(memory_space=pl.ANY)] * 2,
        scratch_shapes=[
            vm((rows, d), BF),
            pltpu.SemaphoreType.DMA((1,)),
            pltpu.SemaphoreType.DMA((slots,)),
            pltpu.SemaphoreType.DMA((slots,)),
        ],
        compiler_params=pltpu.CompilerParams(collective_id=1, has_side_effects=True, vmem_limit_bytes=48 * 2**20),
    )(mine, theirs, own, shown)


def unpack_kernel(
    bases, f, pack_ref, shown_e, shown_t, shown_far,
    proj, out_w, bias, w_in, b_in, w_out, b_out, gain, offset, c_proj, c_out, c_bias, c_gain, c_offset, pair, shown,
    pack, f_proj, f_out, f_in, f_w_out, f_cproj, f_cout, rows_shown, in_sem, out_sem, shown_sem,
):
    d = pack_ref.shape[1]
    own_b, own_c, own_p = bases
    section = lax.axis_index("section")
    leave = pltpu.make_async_copy(rows_shown, shown, shown_sem.at[0])
    far = [
        pltpu.make_async_copy(shown_t, rows_shown.at[0], shown_sem.at[0]),
        pltpu.make_async_copy(shown_far, rows_shown.at[1], shown_sem.at[1]),
    ]
    spans = [(0, own_b), (own_b, own_b + f), (own_b + f, own_c), (own_c, pack.shape[0])]
    loads = []
    for i, (begin, end) in enumerate(spans):
        rows = pl.ds(begin, end - begin)
        loads.append(pltpu.make_async_copy(pack_ref.at[rows], pack.at[rows], in_sem.at[i]))
        loads[-1].start()

    @pl.when(section == 1)
    def _():
        far[0].start()
        far[1].start()

    leaving = []

    def send(held, out):
        leaving.append(pltpu.make_async_copy(held, out, out_sem.at[len(leaving)]))
        leaving[-1].start()

    loads[0].wait()
    f_proj[...] = pack[0 : 3 * d].astype(F32)
    send(f_proj, proj)
    f_out[...] = pack[3 * d : 4 * d].astype(F32)
    send(f_out, out_w)
    loads[1].wait()
    for c in range(f // d):
        f_in[:, c * d : (c + 1) * d] = pack[own_b + c * d : own_b + (c + 1) * d].astype(F32)
    send(f_in, w_in)
    loads[2].wait()
    f_w_out[...] = pack[own_b + f : own_b + 2 * f].astype(F32)
    send(f_w_out, w_out)
    loads[3].wait()

    @pl.when(section == 1)
    def _():
        far[0].wait()
        far[1].wait()
        leave.start()

    f_cproj[...] = pack[own_c : own_c + 3 * d].astype(F32)
    send(f_cproj, c_proj)
    f_cout[...] = pack[own_c + 3 * d : own_c + 4 * d].astype(F32)
    send(f_cout, c_out)
    small = pack[own_p + 16 : own_p + 32].astype(F32)
    middle = pack[own_p + 32 : own_p + 48].astype(F32)
    bias[...] = small[0:3]
    row = lax.broadcasted_iota(jnp.int32, (16, 1), 0)
    moved = (section == 1) & (row >= 3) & (row <= 11) & (row != 8) & (row != 10)
    small = jnp.where(moved, middle, small)
    for c in range(f // d):
        b_in[:, c * d : (c + 1) * d] = small[3 + c : 4 + c]
    b_out[...] = small[7:8]
    gain[...] = small[8:10]
    offset[...] = small[10:12]
    c_bias[...] = middle[0:3]
    c_gain[...] = middle[8:9]
    c_offset[...] = middle[10:11]
    pair[...] = pack[own_p : own_p + 16].astype(F32)[0 : pair.shape[0]]
    for copy in leaving:
        copy.wait()
    pl.when(section == 1)(leave.wait)


def unpack(pack, bases, f, shown_e, shown_t, shown_far):
    d = pack.shape[1]
    inside = pl.BlockSpec(memory_space=pltpu.VMEM)
    anywhere = pl.BlockSpec(memory_space=pl.ANY)
    shapes = [(3 * d, d), (d, d), (3, d), (d, f), (1, f), (f, d), (1, d), (2, d), (2, d), (3 * d, d), (d, d), (3, d), (1, d), (1, d), (PAIRS, d)]
    large = (0, 1, 3, 5, 9, 10)
    return pl.pallas_call(
        functools.partial(unpack_kernel, bases, f),
        name="unpack",
        out_shape=[sds(s, F32) for s in shapes] + [sds(shown_e.shape, BF)],
        in_specs=[anywhere] * 4,
        out_specs=[anywhere if i in large else inside for i in range(len(shapes))] + [anywhere],
        input_output_aliases={1: len(shapes)},
        scratch_shapes=[vm(pack.shape, BF)] + [vm(shapes[i], F32) for i in large]
        + [vm(shown_e.shape, BF), pltpu.SemaphoreType.DMA((4,)), pltpu.SemaphoreType.DMA((6,)), pltpu.SemaphoreType.DMA((2,))],
        compiler_params=pltpu.CompilerParams(vmem_limit_bytes=50 * 2**20),
    )(pack, shown_e, shown_t, shown_far)


def nothing(*refs):
    pass


def blank(*shapes):
    spec = pl.BlockSpec(memory_space=pl.ANY)
    return pl.pallas_call(nothing, name="blank", out_shape=[sds(*s) for s in shapes], out_specs=[spec] * len(shapes))()


def per_device(
    embeds, cotangent, pair_ids, seq_lengths, alive_count,
    self_proj, self_out, self_bias, ffn_in, ffn_in_bias, ffn_out, ffn_out_bias, norm_gain, norm_bias,
    cross_proj, cross_out, cross_bias, cross_norm_gain, cross_norm_bias, pair_embed,
):
    layer = (self_proj[0], self_out[0], self_bias[0], ffn_in[0], ffn_in_bias, ffn_out[0], ffn_out_bias, norm_gain[0], norm_bias[0])
    cross = (cross_proj, cross_out, cross_bias, cross_norm_gain[None], cross_norm_bias[None])
    place = jnp.asarray(place_matrix(), BF)
    section_zero = lax.axis_index("section") == 0
    section_one = lax.axis_index("section") == 1
    devices = lax.axis_size("dp")
    x, cot = embeds[0], cotangent[0]
    count, n, d = x.shape
    f = ffn_in.shape[2]
    live = (jnp.arange(count) < alive_count[0])[None, :]
    numbers = jnp.concatenate([seq_lengths.reshape(-1), jnp.where(live, seq_lengths, 0).reshape(-1), pair_ids])
    src = [(s, 2 * count + s, 4 * count + s) for s in range(count)]
    tgt = [(count + s, 3 * count + s, 4 * count + s) for s in range(count)]
    mid = [(s, 3 * count + s, 4 * count + s) for s in range(count)]
    nd, nf, n1 = (n, d), (n, f), (n, 1)
    ahead, behind, both = [(0, 1)], [(1, 0)], [(0, 1), (1, 0)]

    def move(value, way):
        return lax.ppermute(value, "section", way)

    def pick(received, own):
        return jnp.where(section_zero, received, own)

    part = f // devices
    start = lax.axis_index("dp") * part
    share = jnp.concatenate([
        lax.dynamic_slice_in_dim(ffn_in[0], start, part, 1).T, lax.dynamic_slice_in_dim(ffn_out[0], start, part, 0)
    ])
    share, bias_in = lax.optimization_barrier((share, ffn_in_bias))
    vectors = jnp.concatenate([bias_in[:, i : i + d] for i in range(0, f, d)] + [ffn_out_bias, norm_gain[0], norm_bias[0]])
    x, far_share, far_vectors, x_late, cot_late = lax.optimization_barrier(
        (x, move(share, behind), move(vectors, behind), x[1:], cot[1:])
    )
    far_x = move(x_late, behind)
    weights = lax.all_gather(pick(far_share, share), "dp", axis=0, tiled=True)
    vectors = pick(far_vectors, vectors)

    def first(e, t, shown):
        def enc():
            memory, shown_e, q, k, v, mt, lse, na, ra, act, slope, nb, rb = enc_forward(numbers, src[e], x, e, layer, shown)
            return memory, shown_e, q, k, v, mt, lse, ra, na, act, slope, nb, rb

        def dec():
            low, q, k, v, mt, lse, na, ra = dec_self(numbers, tgt[t], x, t, pair_embed, layer)
            shown_e, act, slope, nb, rb = blank(((count, *nd), BF), (nf, BF), (nf, BF), (nd, BF), (n1, F32))
            return na, shown_e, q, k, v, mt, lse, ra, low, act, slope, nb, rb

        return lax.cond(section_zero, enc, dec)

    def last(e, t, saved_e, d_memory, grads, saved_t, prev):
        def enc():
            _, _, q, k, v, mt, lse, ra, na, act, slope, nb, rb = saved_e
            return tuple(enc_back(numbers, src[e], x, e, d_memory, cot, layer, place, (q, k, v, mt, lse, na, ra, act, slope, nb, rb), prev))

        def dec():
            na, _, q, k, v, mt, lse, ra, low, _, _, _, _ = saved_t
            d_x, pack_a, small = dec_self_back(
                numbers, tgt[t], t, count, grads, layer, place, (low, q, k, v, mt, lse, na, ra), prev
            )
            return d_x, pack_a, blank(((2 * f, d), BF))[0], small

        return lax.cond(section_one, dec, enc)

    saved = [first(0, 1, None)]
    swapped = move(saved[0][0], both)
    near_first, cot_late = lax.optimization_barrier((saved[0][0], cot_late))
    far_cot = move(cot_late, behind)
    x, far_x = lax.optimization_barrier((x, far_x))
    saved.append(first(1, 0, saved[0][1]))
    normed = (swapped, saved[1][0])
    memory = (saved[1][0], swapped)
    crossed = dec_cross(numbers, (mid[1], mid[0]), normed, memory, vectors, cross)
    shown, two, d_memory, pack = dec_mid(
        numbers, (mid[1], mid[0]), ((far_x, 0), (x, 0)), ((far_cot, 0), (cot, 0)), normed, memory, crossed,
        pair_embed, weights, vectors, cross, place, devices,
    )
    near_d_memory = move(d_memory, behind)
    far_two = move(two, ahead)
    mine = lax.psum_scatter(pack, "dp", scatter_dimension=0, tiled=True)
    grads = last(1, 0, saved[1], d_memory, two, saved[1], ())
    grads = last(0, 1, saved[0], near_d_memory, far_two, saved[0], grads)
    mine, pack_a = lax.optimization_barrier((mine, grads[1]))
    theirs = move(mine, both)
    shares = (padded(4 * d, devices) // devices, 2 * f // devices, cross_rows(devices, d) // devices, 16)
    own = reduce_grads(devices, (shares[0], shares[1], shares[3]), pack_a, grads[2], grads[3])
    pack, far_shown = gather_grads(devices, shares, mine, theirs, own, shown)
    bases = [devices * sum(shares[:i]) for i in (1, 2, 3)]
    proj, out_w, bias, w_in, b_in, w_out, b_out, gain, offset, c_proj, c_out, c_bias, c_gain, c_offset, pair, shown = unpack(pack, bases, f, saved[1][1], shown, far_shown)
    return (
        shown[None], grads[0][None], proj.reshape(1, 3, d, d), out_w[None], bias[None], w_in[None], b_in, w_out[None], b_out, gain[None], offset[None],
        c_proj.reshape(3, d, d), c_out, c_bias, c_gain[0], c_offset[0], pair,
    )


def solution(mesh):
    s, r = "section", P()
    in_specs = (
        P(s, "dp"), P(s, "dp"), P("dp"), P(None, "dp"), P("dp"),
        P(s), P(s), P(s), P(s), P(s), P(s), P(s), P(s), P(s), r, r, r, r, r, r,
    )
    out_specs = (P(s, "dp"), P(s, "dp"), P(s), P(s), P(s), P(s), P(s), P(s), P(s), P(s), P(s), r, r, r, r, r, r)
    return jax.shard_map(per_device, mesh=mesh, in_specs=in_specs, out_specs=out_specs, check_vma=False)
```

```python
import functools

import jax
import jax.numpy as jnp
import numpy as np
from jax import lax
from jax.experimental import pallas as pl
from jax.experimental.pallas import tpu as pltpu
from jax.sharding import PartitionSpec as P

BF = jnp.bfloat16
F32 = jnp.float32
HEADS = 8
PAIRS = 16
MESH = pl.DeviceIdType.MESH
EPSILON = 1e-05
BLOCKED = -1e30
RB = 512
NN = (((1,), (0,)), ((), ()))
NT = (((1,), (1,)), ((), ()))
TN = (((0,), (0,)), ((), ()))


def dot(left, right, dims=NN):
    return lax.dot_general(left, right, dims, preferred_element_type=F32)


def row_block(index, size=RB):
    return pl.ds(pl.multiple_of(index * size, size), size)


def loop(count, body, unroll=1):
    def step(index, carry):
        body(index)
        return carry

    lax.fori_loop(0, count, step, 0, unroll=unroll)


def lanes_of(half):
    lane = lax.broadcasted_iota(jnp.int32, (1, 128), 1)
    inside = (lane // 64) == half
    spare = lane - 64 * (1 - half)
    ones = (~inside) & (spare < 32)
    block = (~inside) & (spare >= 32)
    flag = (~inside) & (spare == 32)
    return tuple(m.astype(F32) for m in (inside, ones, block, flag))


def inside_of(half):
    return (lax.broadcasted_iota(jnp.int32, (1, 128), 1) // 64) == half


def norm_rows(value):
    centre = jnp.mean(value, -1, keepdims=True)
    centred = value - centre
    rstd = lax.rsqrt(jnp.mean(centred * centred, -1, keepdims=True) + EPSILON)
    return centred * rstd, rstd


def norm_rows_back(normed, rstd, gain, grad):
    scaled = grad * gain
    return rstd * (
        scaled
        - jnp.mean(scaled, -1, keepdims=True)
        - normed * jnp.mean(scaled * normed, -1, keepdims=True)
    )


def gelu_both(hidden):
    phi = 0.5 + 0.5 * lax.erf(hidden * 0.7071067811865476)
    bell = jnp.exp(-0.5 * hidden * hidden)
    return hidden * phi, phi + hidden * (bell * 0.3989422804014327)


def key_fill(count, length):
    position = lax.broadcasted_iota(jnp.int32, (count, 128), 0)
    spare = lax.broadcasted_iota(jnp.int32, (count, 128), 1) % 64
    return jnp.where((spare < 32) | (position < length), jnp.where(spare < 32, 1.0, 0.0), BLOCKED)


def spare_keys(count, length, ones, block):
    position = lax.broadcasted_iota(jnp.int32, (count, 128), 0)
    return ones + jnp.where(position < length, 0.0, BLOCKED) * block


def causal_cut(scores, query_axis):
    query = lax.broadcasted_iota(jnp.int32, scores.shape, query_axis)
    key = lax.broadcasted_iota(jnp.int32, scores.shape, 1 - query_axis)
    return jnp.where(key <= query, scores, BLOCKED)


def mix_forward(queries, keys, values, length, causal, mixed_t, lse):
    count = queries.shape[0]
    span = keys.shape[0]
    size = min(512 if causal else 1024, count)

    def pair(index):
        cols = row_block(index, 128)
        q = queries[:, cols].astype(F32) * 0.125
        k = keys[:, cols].astype(F32)
        vt = values[:, cols].T.astype(F32)
        lane = lax.broadcasted_iota(jnp.int32, (128, 1), 0)
        qa, ka, va = [], [], []
        for half in range(2):
            inside, ones, block, flag = lanes_of(half)
            qa.append((q * inside + flag).astype(BF))
            ka.append((k * inside + spare_keys(span, length, ones, block)).astype(BF))
            va.append(jnp.where((lane // 64) == half, vt, 1.0).astype(BF))

        def scores_of(part, half):
            here = slice(part * size, (part + 1) * size)
            pieces = [(0, part * size, False), (part * size, size, True)] if causal else [(0, span, False)]
            return [
                (start, reach, cut, dot(ka[half][start : start + reach], qa[half][here], NT))
                for start, reach, cut in pieces
                if reach
            ]

        def finish(part, half, scores):
            here = slice(part * size, (part + 1) * size)
            scores = [(start, reach, causal_cut(s, 1) if cut else s) for start, reach, cut, s in scores]
            top = None
            for _, _, s in scores:
                best = jnp.max(s, axis=0, keepdims=True)
                top = best if top is None else jnp.maximum(top, best)
            total = None
            for start, reach, s in scores:
                o = dot(va[half][:, start : start + reach], jnp.exp(s - top).astype(BF))
                total = o if total is None else total + o
            other = 64 * (1 - half)
            mass = total[other : other + 1]
            own = total[64 * half : 64 * half + 64] / mass
            mixed_t[pl.ds(pl.multiple_of(index * 128 + 64 * half, 64), 64), here] = own.astype(BF)
            lse[index * 2 + half, :, here] = top + jnp.log(mass)

        waiting = None
        for tile in [(part, half) for part in range(count // size) for half in range(2)]:
            scores = scores_of(*tile)
            if waiting:
                finish(*waiting)
            waiting = (*tile, scores)
        finish(*waiting)

    loop(4, pair, 2)


def split3(value):
    high = value.astype(BF).astype(F32)
    middle = (value - high).astype(BF).astype(F32)
    low = (value - high - middle).astype(BF).astype(F32)
    return high, middle, low


def place_matrix():
    out = np.zeros((16, 256), np.float32)
    for half in range(2):
        other = 64 * (1 - half)
        for piece in range(3):
            out[half * 4 + piece, other + piece] = 1
            out[8 + half * 4 + piece, 128 + other + piece] = 1
        out[half * 4 + 3, other + 32] = 1
    return out


def mix_back(queries, keys, values, mixed_t, lse, grad_mixed, place, length, causal, d_q, d_k, d_v):
    count = queries.shape[0]
    span = keys.shape[0]
    size = 256 if causal else min(512, count)
    fill = key_fill(span, length)

    def pair(index):
        cols = row_block(index, 128)
        q = queries[:, cols].astype(F32) * 0.125
        k_low = keys[:, cols]
        k = k_low.astype(F32)
        v = values[:, cols].astype(F32)
        g_low = grad_mixed[:, cols]
        g = g_low.astype(F32)
        q_t = q.astype(BF).T
        g_t = g_low.T
        product = g_t.astype(F32) * mixed_t[cols, :].astype(F32)
        row = lax.broadcasted_iota(jnp.int32, (16, count), 0)
        spread = jnp.where((row == 3) | (row == 7), 1.0, 0.0)
        for half in range(2):
            shift = -lse[index * 2 + half]
            delta = -jnp.sum(product[64 * half : 64 * half + 64], axis=0, keepdims=True)
            for base, value in ((0, shift), (8, delta)):
                for piece, part in enumerate(split3(value)):
                    spread = jnp.where(row == base + 4 * half + piece, part, spread)
        extra = dot(spread.astype(BF), place[...], TN)
        qa, ka, va, ga = [], [], [], []
        for half in range(2):
            inside = inside_of(half)
            qa.append(jnp.where(inside, q, extra[:, 0:128]).astype(BF))
            ga.append(jnp.where(inside, g, extra[:, 128:256]).astype(BF))
            ka.append(jnp.where(inside, k, fill).astype(BF))
            va.append(jnp.where(inside, v, 1.0).astype(BF))
        lane = lax.broadcasted_iota(jnp.int32, (size, 128), 1)
        total_k = [None, None]
        total_v = [None, None]

        def grow(total, value):
            if total is None:
                return value
            if total.shape == value.shape:
                return total + value
            known = total.shape[1]
            return jnp.concatenate([total + value[:, :known], value[:, known:]], axis=1)

        for part in range(count // size):
            here = slice(part * size, (part + 1) * size)
            reach = (part + 1) * size if causal else span
            out_q = []
            for half in range(2):
                s = dot(qa[half][here], ka[half][:reach], NT)
                if causal:
                    if part:
                        s = jnp.concatenate([s[:, : part * size], causal_cut(s[:, part * size :], 0)], axis=1)
                    else:
                        s = causal_cut(s, 0)
                probs = jnp.exp(s)
                grads = dot(ga[half][here], va[half][:reach], NT)
                probs_low = probs.astype(BF)
                d_s = (probs * grads).astype(BF)
                total_v[half] = grow(total_v[half], dot(g_t[:, here], probs_low))
                total_k[half] = grow(total_k[half], dot(q_t[:, here], d_s))
                out_q.append(dot(d_s, k_low[:reach]))
            d_q[here, cols] = (jnp.where(lane < 64, out_q[0], out_q[1]) * 0.125).astype(BF)
        for target, total in ((d_k, total_k), (d_v, total_v)):
            joined = jnp.concatenate([total[0][:64], total[1][64:]], axis=0).astype(BF)
            target[:, cols] = joined.T

    loop(4, pair, 2)


class Late:
    def __init__(self, ref, copy):
        self.ref, self.copy = ref, copy

    def get(self):
        if self.copy is not None:
            self.copy.wait()
            self.copy = None
        return self.ref


class Limits:
    def __init__(self, ref, picks):
        self.ref, self.picks = ref, picks

    def __getitem__(self, index):
        if len(self.picks) == 2:
            near, far = self.picks
            return self.ref[near[index] + lax.axis_index("section") * (far[index] - near[index])]
        return self.ref[self.picks[index]]


class Pieces:
    def __init__(self, source, ref, sem):
        self.source, self.ref, self.sem = source, ref, sem

    def wait(self):
        pltpu.make_async_copy(self.source.at[pl.ds(0, self.ref.shape[0])], self.ref, self.sem).wait()


class Leaving:
    def __init__(self, ref, out, sem):
        self.ref, self.out, self.sem = ref, out, sem

    def send(self, rows=None):
        if rows is None:
            pltpu.make_async_copy(self.ref, self.out, self.sem).start()
        else:
            pltpu.make_async_copy(self.ref.at[rows], self.out.at[rows], self.sem).start()

    def part(self, index):
        return Leaving(self.ref.at[index], self.out.at[index], self.sem)

    def finish(self):
        pltpu.make_async_copy(self.ref, self.out, self.sem).wait()


def sds(shape, dtype):
    return jax.ShapeDtypeStruct(shape, dtype)


def vm(shape, dtype):
    return pltpu.VMEM(shape, dtype)


def call(kernel, name, scalars, picks, args, outs, scratch, flops):
    anywhere = pl.BlockSpec(memory_space=pl.ANY)
    inside = pl.BlockSpec(memory_space=pltpu.VMEM)
    operands, in_specs, out_shapes, out_specs, memory, aliases = [], [], [], [], [], {}
    plan_in, plan_out, places = [], [], []
    for value, kind in args:
        places.append(len(operands))
        operands.append(value)
        if kind == "vmem":
            in_specs.append(inside)
            plan_in.append(None)
        else:
            in_specs.append(anywhere)
            if kind[0] == "either":
                _, index, other, other_index = kind
                plan_in.append((len(memory), (index, len(operands), other_index)))
                operands.append(other)
                in_specs.append(anywhere)
                memory.append(vm(value.shape if index is None else value.shape[1:], value.dtype))
                continue
            if kind[0] == "rows":
                plan_in.append((len(memory), kind[2]))
                memory.append(vm(kind[1], value.dtype))
                continue
            index = kind[1] if isinstance(kind, tuple) else None
            plan_in.append((len(memory), index))
            memory.append(vm(value.shape if index is None else value.shape[1:], value.dtype))
    for position, (shape, dtype, kind) in enumerate(outs):
        if kind == "vmem":
            out_shapes.append(sds(shape, dtype))
            out_specs.append(inside)
            plan_out.append(None)
            continue
        out_specs.append(anywhere)
        index, earlier = None, None
        if isinstance(kind, tuple) and kind[0] == "late":
            index, earlier, total = kind[1:]
            out_shapes.append(sds((total, *shape), dtype))
            if earlier is not None:
                aliases[len(operands)] = position
                operands.append(earlier)
                in_specs.append(anywhere)
        else:
            out_shapes.append(sds(shape, dtype))
        plan_out.append((len(memory), index, len(operands) if isinstance(kind, tuple) and kind[0] == "from" else None))
        memory.append(vm(shape, dtype))
        if isinstance(kind, tuple) and kind[0] == "from":
            operands.append(kind[1])
            in_specs.append(anywhere)
    total_in, count_out, count_memory = len(operands), len(outs), len(memory)

    def body(numbers, *refs):
        ins, results = refs[:total_in], refs[total_in : total_in + count_out]
        held = refs[total_in + count_out : total_in + count_out + count_memory]
        own = refs[total_in + count_out + count_memory : -1]
        sems = refs[-1]
        first, last = [], []
        for spot, plan in zip(places, plan_in):
            ref = ins[spot]
            if plan is None:
                first.append(ref)
                continue
            where, index = plan
            if isinstance(index, tuple):
                index, other, other_index = index
                copies = [
                    pltpu.make_async_copy(r if i is None else r.at[i], held[where], sems.at[where])
                    for r, i in ((ref, index), (ins[other], other_index))
                ]
                section = lax.axis_index("section")
                pl.when(section == 0)(copies[0].start)
                pl.when(section == 1)(copies[1].start)
                first.append(Late(held[where], copies[0]))
                continue
            if isinstance(index, list):
                for begin, end, size in index:
                    pltpu.make_async_copy(ref.at[pl.ds(begin, size)], held[where].at[pl.ds(end, size)], sems.at[where]).start()
                first.append(Late(held[where], Pieces(ref, held[where], sems.at[where])))
                continue
            copy = pltpu.make_async_copy(ref if index is None else ref.at[index], held[where], sems.at[where])
            copy.start()
            first.append(Late(held[where], copy))
        for ref, plan in zip(results, plan_out):
            if plan is None:
                last.append(ref)
                continue
            where, index, source = plan
            leaving = Leaving(held[where], ref if index is None else ref.at[index], sems.at[where])
            if source is not None:
                copy = pltpu.make_async_copy(ins[source], held[where], sems.at[where])
                copy.start()
                leaving.begin = Late(held[where], copy)
            last.append(leaving)
        kernel(Limits(numbers, picks), *first, *last, *own)
        for leaving in last:
            if isinstance(leaving, Leaving):
                leaving.finish()

    return pl.pallas_call(
        body,
        name=name,
        out_shape=out_shapes,
        in_specs=[pl.BlockSpec(memory_space=pltpu.SMEM), *in_specs],
        out_specs=out_specs,
        scratch_shapes=[*memory, *[vm(*s) for s in scratch], pltpu.SemaphoreType.DMA((max(count_memory, 1),))],
        input_output_aliases={i + 1: o for i, o in aliases.items()},
        compiler_params=pltpu.CompilerParams(vmem_limit_bytes=62 * 2**20),
        cost_estimate=pl.CostEstimate(flops=int(flops), bytes_accessed=20 * 2**20, transcendentals=0),
    )(scalars, *operands)


def valid_rows(index, limit, size=RB):
    return (lax.broadcasted_iota(jnp.int32, (size, 1), 0) + index * size < limit).astype(F32)


def ffn_rows(z_low, w_in, c_in, w_out, c_out, act_ref, slope_ref, r, flipped=False):
    def hidden(c):
        cols = slice(c * 512, c * 512 + 512)
        return dot(z_low, w_in[cols], NT) + c_in[c : c + 1] if flipped else dot(z_low, w_in[:, cols]) + c_in[:, cols]

    total, coming = None, hidden(0)
    for c in range(4):
        cols = slice(c * 512, c * 512 + 512)
        here = coming
        coming = hidden(c + 1) if c < 3 else None
        act, slope = gelu_both(here)
        act = act.astype(BF)
        act_ref[r, cols] = act
        slope_ref[r, cols] = slope.astype(BF)
        part = dot(act, w_out[cols])
        total = part if total is None else total + part
    return total + c_out[...]


def put(target, rows, value, later):
    target[rows] = (value + target[rows].astype(F32) if later else value).astype(BF)


def ffn_back(grad_low, act, slope, z_low, w_in, w_out, put_rows, small, on_rows, flipped=False):
    def body(index):
        r = row_block(index)
        g = grad_low[r]
        total, coming = None, dot(g, w_out[0:512], NT)
        for c in range(4):
            cols = slice(c * 512, c * 512 + 512)
            here = coming
            coming = dot(g, w_out[512 * c + 512 : 512 * c + 1024], NT) if c < 3 else None
            dh = (here * slope[r, cols].astype(F32)).astype(BF)
            slope[r, cols] = dh
            small[3 + c : 4 + c] += jnp.sum(dh.astype(F32), axis=0, keepdims=True)
            part = dot(dh, w_in[cols]) if flipped else dot(dh, w_in[:, cols], NT)
            total = part if total is None else total + part
        small[7:8] += jnp.sum(g.astype(F32), axis=0, keepdims=True)
        on_rows(r, total)

    loop(grad_low.shape[0] // RB, body)
    z = z_low[...]
    g = grad_low[...]
    act = act.get() if isinstance(act, Late) else act
    for c in range(4):
        cols = slice(c * 512, c * 512 + 512)
        put_rows(c * 512, dot(z, slope[:, cols], TN))
        put_rows(2048 + c * 512, dot(act[:, cols], g, TN))


def project(count, x_low, proj, bias, q, k, v):
    def body(index):
        r = row_block(index)
        x = x_low(r)
        q.ref[r] = (dot(x, proj[0]) + bias[0:1]).astype(BF)
        k.ref[r] = dot(x, proj[1]).astype(BF)
        v.ref[r] = (dot(x, proj[2]) + bias[1:2]).astype(BF)

    loop(count // RB, body)
    q.send()
    k.send()
    v.send()


def self_back(x, proj, out_w, q, k, v, mixed_t, lse, place, length, causal, grad_low, grad_mixed, d_q, d_k, d_v, pack, later, small, rest):
    grad_mixed[...] = dot(grad_low[...], out_w.get()[...], NT).astype(BF)
    mixed_t = mixed_t.get()
    if later:
        pack.begin.get()
    put(pack.ref, slice(1536, 2048), dot(mixed_t[...], grad_low[...]), later)
    q, k, v, x = q.get(), k.get(), v.get(), x.get()
    mix_back(q, k, v, mixed_t, lse, grad_mixed, place, length, causal, d_q, d_k, d_v)
    small[0:1] += jnp.sum(d_q[...].astype(F32), axis=0, keepdims=True)
    small[1:2] += jnp.sum(d_v[...].astype(F32), axis=0, keepdims=True)
    small[2:3] += jnp.sum(grad_low[...].astype(F32), axis=0, keepdims=True)
    xl = x[...]
    put(pack.ref, slice(0, 512), dot(xl, d_q[...], TN), later)
    put(pack.ref, slice(512, 1024), dot(xl, d_k[...], TN), later)
    put(pack.ref, slice(1024, 1536), dot(xl, d_v[...], TN), later)
    pack.send()
    proj = proj.get()

    def body(index):
        r = row_block(index)
        rest(r, dot(d_q[r], proj[0], NT) + dot(d_k[r], proj[1], NT) + dot(d_v[r], proj[2], NT))

    loop(x.shape[0] // RB, body)


def begin_small(small, earlier):
    small[...] = jnp.zeros(small.shape, F32) if earlier is None else earlier[...]


def enc_forward_kernel(
    length, x, proj, out_w, w_in, w_out, bias, c_in, c_out, gain, offset,
    memory, shown, q, k, v, mixed_t, lse, normed1, rstd1, act, slope, normed2, rstd2,
):
    x = x.get()
    project(x.shape[0], lambda r: x[r], proj.get(), bias, q, k, v)
    mix_forward(q.ref, k.ref, v.ref, length[0], False, mixed_t.ref, lse)
    mixed_t.send()
    out_w, w_in, w_out = out_w.get(), w_in.get(), w_out.get()

    def body(index):
        r = row_block(index)
        xf = x[r].astype(F32)
        n1, s1 = norm_rows(xf + dot(mixed_t.ref[:, r], out_w[...], TN) + bias[2:3])
        normed1.ref[r] = n1.astype(BF)
        rstd1[r] = s1
        y = n1 * gain[0:1] + offset[0:1]
        f = ffn_rows(y.astype(BF), w_in, c_in, w_out, c_out, act.ref, slope.ref, r)
        n2, s2 = norm_rows(y + f + xf)
        normed2.ref[r] = n2.astype(BF)
        rstd2[r] = s2
        result = n2 * gain[1:2] + offset[1:2]
        memory.ref[r] = result.astype(BF)
        shown.ref[r] = (result * valid_rows(index, length[1])).astype(BF)
        for leaving in (act, slope, memory, shown, normed1, normed2):
            leaving.send(r)

    loop(x.shape[0] // RB, body)


def enc_forward(scalars, picks, x, s, layer, shown):
    proj, out_w, bias, w_in, c_in, w_out, c_out, gain, offset = layer
    count, n, d = x.shape
    f = w_in.shape[1]
    nd = (n, d)
    args = [(x, ("late", s)), (proj, "late"), (out_w, "late"), (w_in, "late"), (w_out, "late")]
    args += [(v, "vmem") for v in (bias, c_in, c_out, gain, offset)]
    outs = [
        (nd, BF, "late"), (nd, BF, ("late", s, shown, count)), (nd, BF, "late"), (nd, BF, "late"), (nd, BF, "late"), ((d, n), BF, "late"),
        ((8, 1, n), F32, "vmem"), (nd, BF, "late"), ((n, 1), F32, "vmem"), ((n, f), BF, "late"), ((n, f), BF, "late"), (nd, BF, "late"), ((n, 1), F32, "vmem"),
    ]
    return call(enc_forward_kernel, "encoder_forward", scalars, picks, args, outs, [], 15e9)


def enc_back_kernel(
    later, length, cot, d_memory, normed2, normed1, w_out, slope, w_in, act, out_w, mixed_t, q, k, v, x, proj,
    lse, rstd1, rstd2, gain, offset, place, *refs,
):
    earlier = refs[0] if later else None
    d_x, pack_a, pack_b, small, last, grad_low, z_low, grad_mixed, d_q, d_k, d_v = refs[later:]
    begin_small(small, earlier)
    cot, d_memory, normed2, normed1 = cot.get(), d_memory.get(), normed2.get(), normed1.get()

    def top(index):
        r = row_block(index)
        n2 = normed2[r].astype(F32)
        g = cot[r].astype(F32) * valid_rows(index, length[1]) + d_memory[r].astype(F32)
        small[9:10] += jnp.sum(g * n2, axis=0, keepdims=True)
        small[11:12] += jnp.sum(g, axis=0, keepdims=True)
        g = norm_rows_back(n2, rstd2[r], gain[1:2], g)
        last[r] = g
        grad_low[r] = g.astype(BF)
        z_low[r] = (normed1[r].astype(F32) * gain[0:1] + offset[0:1]).astype(BF)

    loop(last.shape[0] // RB, top)

    def middle(r, grad):
        n1 = normed1[r].astype(F32)
        g = last[r] + grad
        small[8:9] += jnp.sum(g * n1, axis=0, keepdims=True)
        small[10:11] += jnp.sum(g, axis=0, keepdims=True)
        g = norm_rows_back(n1, rstd1[r], gain[0:1], g)
        last[r] = last[r] + g
        grad_mixed[r] = g.astype(BF)

    def put_rows(start, value):
        if later:
            pack_b.begin.get()
        put(pack_b.ref, slice(start, start + 512), value, later)

    ffn_back(grad_low, act, slope.get(), z_low, w_in.get(), w_out.get(), put_rows, small, middle)
    pack_b.send()
    grad_low[...] = grad_mixed[...]

    def rest(r, grad):
        d_x.ref[r] = last[r] + grad
        d_x.send(r)

    self_back(x, proj, out_w, q, k, v, mixed_t, lse, place, length[0], False, grad_low, grad_mixed, d_q, d_k, d_v, pack_a, later, small, rest)


def enc_back(scalars, picks, x, s, d_memory, cot, layer, place, saved, prev):
    proj, out_w, bias, w_in, c_in, w_out, c_out, gain, offset = layer
    q, k, v, mixed_t, lse, normed1, rstd1, act, slope, normed2, rstd2 = saved
    count, n, d = x.shape
    f = w_in.shape[1]
    nd = (n, d)
    args = [(cot, ("late", s))]
    args += [(a, "late") for a in (d_memory, normed2, normed1, w_out, slope, w_in, act, out_w, mixed_t, q, k, v)]
    args += [(x, ("late", s)), (proj, "late")]
    args += [(a, "vmem") for a in (lse, rstd1, rstd2, gain, offset, place)]
    carry = lambda i: ("from", prev[i]) if prev else "late"
    if prev:
        args.append((prev[3], "vmem"))
    outs = [(nd, F32, ("late", s, prev[0] if prev else None, count)), ((4 * d, d), BF, carry(1)), ((2 * f, d), BF, carry(2)), ((16 + PAIRS, d), F32, "vmem")]
    scratch = [(nd, F32)] + [(nd, BF)] * 6
    return call(functools.partial(enc_back_kernel, bool(prev)), "encoder_back", scalars, picks, args, outs, scratch, 35e9)


def dec_self_kernel(length, x, proj, out_w, pair_table, bias, gain, offset, x_low, q, k, v, mixed_t, lse, normed1, rstd1):
    x = x.get()
    pair_row = pair_table[pl.ds(length[2], 1)]

    def low(r):
        value = (x[r].astype(F32) + pair_row).astype(BF)
        x_low.ref[r] = value
        return value

    project(x.shape[0], low, proj.get(), bias, q, k, v)
    x_low.send()
    mix_forward(q.ref, k.ref, v.ref, length[0], True, mixed_t.ref, lse)
    mixed_t.send()
    out_w = out_w.get()

    def body(index):
        r = row_block(index)
        n1, s1 = norm_rows(x[r].astype(F32) + pair_row + dot(mixed_t.ref[:, r], out_w[...], TN) + bias[2:3])
        normed1.ref[r] = n1.astype(normed1.ref.dtype)
        rstd1[r] = s1
        normed1.send(r)

    loop(x.shape[0] // RB, body)


def dec_self(scalars, picks, x, s, pair_table, layer):
    proj, out_w, bias, w_in, c_in, w_out, c_out, gain, offset = layer
    count, n, d = x.shape
    nd = (n, d)
    args = [(x, ("late", s)), (proj, "late"), (out_w, "late")]
    args += [(v, "vmem") for v in (pair_table, bias, gain, offset)]
    outs = [(nd, BF, "late")] * 4 + [((d, n), BF, "late"), ((8, 1, n), F32, "vmem"), (nd, BF, "late"), ((n, 1), F32, "vmem")]
    return call(dec_self_kernel, "decoder_self", scalars, picks, args, outs, [], 8e9)


def padded(rows, count):
    return -(-rows // (16 * count)) * (16 * count)


def cross_rows(count, d):
    return padded(4 * d, count)


def dec_cross_kernel(
    length, normed1, c_proj, memory, c_bias, vectors,
    q, k, v, mixed_t, lse,
):
    gain, offset = vectors[5:6], vectors[7:8]
    normed1, c_proj = normed1.get(), c_proj.get()

    def queries(index):
        r = row_block(index)
        y = (normed1[r].astype(F32) * gain + offset).astype(BF)
        q.ref[r] = (dot(y, c_proj[0]) + c_bias[0:1]).astype(BF)

    loop(normed1.shape[0] // RB, queries)
    q.send()
    memory = memory.get()

    def keys(index):
        r = row_block(index)
        m = memory[r]
        k.ref[r] = dot(m, c_proj[1]).astype(BF)
        v.ref[r] = (dot(m, c_proj[2]) + c_bias[1:2]).astype(BF)

    loop(memory.shape[0] // RB, keys)
    k.send()
    v.send()
    mix_forward(q.ref, k.ref, v.ref, length[0], False, mixed_t.ref, lse)
    mixed_t.send()


def dec_mid_kernel(
    share_b, share_c, length, normed1, mixed_t, c_out, w_in, w_out, x, cot, q, k, v, c_proj, memory,
    lse, pair_table, c_bias, c_gain, c_offset, vectors, place,
    shown, two, d_memory, pack,
    small, last, top, y_low, z_low, normed2, rstd2, act, slope, grad_low, grad_mixed, d_q, d_k, d_v,
):
    small[...] = jnp.zeros(small.shape, F32)
    grad_last, grad_first = (two.part(i) for i in range(2))
    c_in, c_out_b, gain, offset = vectors[0:4], vectors[4:5], vectors[5:7], vectors[7:9]
    pair_row = pair_table[pl.ds(length[2], 1)]

    def put_part(start, value, share, shift):
        value = value.astype(BF)
        done = 0
        while done < value.shape[0]:
            owner, inner = divmod(start + done, share)
            size = min(share - inner, value.shape[0] - done)
            begin = owner * (share_b + share_c + 16) + shift + inner
            pack.ref[begin : begin + size] = value[done : done + size]
            done += size

    def put_b(start, value):
        put_part(start, value, share_b, 0)

    def put_c(start, value):
        put_part(start, value, share_c, share_b)

    normed1, mixed_t, c_out, w_in, w_out, x, cot = (a.get() for a in (normed1, mixed_t, c_out, w_in, w_out, x, cot))
    count = normed1.shape[0]

    def forward(index):
        r = row_block(index)
        y = normed1[r].astype(F32) * gain[0:1] + offset[0:1]
        y_low[r] = y.astype(BF)
        n2, s2 = norm_rows(y + dot(mixed_t[:, r], c_out[...], TN) + c_bias[2:3])
        normed2[r] = n2.astype(BF)
        rstd2[r] = s2
        z = n2 * c_gain[...] + c_offset[...]
        zl = z.astype(BF)
        z_low[r] = zl
        f = ffn_rows(zl, w_in, c_in, w_out, c_out_b, act, slope, r, True)
        n3, s3 = norm_rows(z + f + x[r].astype(F32) + pair_row)
        valid = valid_rows(index, length[1])
        shown.ref[r] = ((n3 * gain[1:2] + offset[1:2]) * valid).astype(BF)
        shown.send(r)
        g = cot[r].astype(F32) * valid
        small[9:10] += jnp.sum(g * n3, axis=0, keepdims=True)
        small[11:12] += jnp.sum(g, axis=0, keepdims=True)
        g = norm_rows_back(n3, s3, gain[1:2], g)
        last[r] = g
        grad_last.ref[r] = g.astype(BF)

    loop(count // RB, forward)
    grad_last.send()

    def middle(r, grad):
        n2 = normed2[r].astype(F32)
        g = last[r] + grad
        small[8:9] += jnp.sum(g * n2, axis=0, keepdims=True)
        small[10:11] += jnp.sum(g, axis=0, keepdims=True)
        g = norm_rows_back(n2, rstd2[r], c_gain[...], g)
        top[r] = g
        grad_low[r] = g.astype(BF)

    ffn_back(grad_last.ref, act, slope, z_low, w_in, w_out, put_b, small, middle, True)
    grad_mixed[...] = dot(grad_low[...], c_out[...], NT).astype(BF)
    put_c(1536, dot(mixed_t[...], grad_low[...]))
    q, k, v = q.get(), k.get(), v.get()
    mix_back(q, k, v, mixed_t, lse, grad_mixed, place, length[0], False, d_q, d_k, d_v)
    c_proj, memory = c_proj.get(), memory.get()
    span = memory.shape[0]

    def back(index):
        r = row_block(index)
        d_memory.ref[r] = (dot(d_k[r], c_proj[1], NT) + dot(d_v[r], c_proj[2], NT)).astype(BF)
        d_memory.send(r)

    loop(span // RB, back)

    def first(index):
        r = row_block(index)
        grad_first.ref[r] = (top[r] + dot(d_q[r], c_proj[0], NT)).astype(BF)
        grad_first.send(r)

    loop(count // RB, first)
    small[0:1] += jnp.sum(d_q[...].astype(F32), axis=0, keepdims=True)
    small[1:2] += jnp.sum(d_v[...].astype(F32), axis=0, keepdims=True)
    small[2:3] += jnp.sum(grad_low[...].astype(F32), axis=0, keepdims=True)
    m = memory[...]
    put_c(0, dot(y_low[...], d_q[...], TN))
    put_c(512, dot(m, d_k[...], TN))
    put_c(1024, dot(m, d_v[...], TN))
    for owner in range(pack.ref.shape[0] // (share_b + share_c + 16)):
        begin = owner * (share_b + share_c + 16) + share_b + share_c
        pack.ref[begin : begin + 16] = (small[...] if owner == 2 else jnp.zeros((16, 512), F32)).astype(BF)
    pack.send()


def dec_mid(scalars, picks, x, cot, normed1, memory, crossed, pair_table, weights, vectors, cross, place, count):
    c_proj, c_out_w, c_bias, c_gain, c_offset = cross
    q, k, v, mixed_t, lse = crossed
    n, d = normed1[0].shape
    m = memory[0].shape[0]
    f = weights.shape[0] // 2
    nd, md = (n, d), (m, d)
    part = f // count
    share_b, share_c = 2 * f // count, cross_rows(count, d) // count
    either = lambda pair: (pair[0], ("either", None, pair[1], None))
    args = [either(normed1), (mixed_t, "late"), (c_out_w, "late")]
    args += [(weights, ("rows", (f, d), [(2 * part * i + part * j, part * i, part) for i in range(count)])) for j in range(2)]
    args += [(a[0][0], ("either", a[0][1], a[1][0], a[1][1])) for a in (x, cot)]
    args += [(a, "late") for a in (q, k, v, c_proj)] + [either(memory)]
    args += [(a, "vmem") for a in (lse, pair_table, c_bias, c_gain, c_offset, vectors, place)]
    outs = [(nd, BF, "late"), ((2, n, d), BF, "late"), (md, BF, "late"), ((count * (share_b + share_c + 16), d), BF, "late")]
    scratch = [((16, d), F32), (nd, F32), (nd, F32), (nd, BF), (nd, BF)]
    scratch += [(nd, BF), ((n, 1), F32), ((n, f), BF), ((n, f), BF), (nd, BF), (nd, BF), (nd, BF), (md, BF), (md, BF)]
    return call(functools.partial(dec_mid_kernel, share_b, share_c), "decoder_middle", scalars, picks, args, outs, scratch, 45e9)


def dec_cross(scalars, picks, normed1, memory, vectors, cross):
    c_proj, c_out_w, c_bias, c_gain, c_offset = cross
    n, d = normed1[0].shape
    m = memory[0].shape[0]
    either = lambda pair: (pair[0], ("either", None, pair[1], None))
    args = [either(normed1), (c_proj, "late"), either(memory), (c_bias, "vmem"), (vectors, "vmem")]
    outs = [((n, d), BF, "late"), ((m, d), BF, "late"), ((m, d), BF, "late"), ((d, n), BF, "late"), ((8, 1, n), F32, "vmem")]
    return call(dec_cross_kernel, "decoder_cross", scalars, picks, args, outs, [], 11e9)


def dec_self_back_kernel(
    later, length, grad_first, normed1, grad_last, out_w, mixed_t, q, k, v, x_low, proj,
    lse, rstd1, gain, place, *refs,
):
    earlier = refs[0] if later else None
    d_x, pack_a, small, last, grad_low, grad_mixed, d_q, d_k, d_v, column = refs[later:]
    begin_small(small, earlier)
    column[...] = jnp.zeros(column.shape, F32)
    grad_first, normed1, grad_last = grad_first.get(), normed1.get(), grad_last.get()

    def top(index):
        r = row_block(index)
        n1 = normed1[r].astype(F32)
        g = grad_first[r].astype(F32)
        small[8:9] += jnp.sum(g * n1, axis=0, keepdims=True)
        small[10:11] += jnp.sum(g, axis=0, keepdims=True)
        g = norm_rows_back(n1, rstd1[r], gain[0:1], g)
        last[r] = grad_last[r].astype(F32) + g
        grad_low[r] = g.astype(BF)

    loop(last.shape[0] // RB, top)

    def rest(r, grad):
        g = last[r] + grad
        d_x.ref[r] = g
        d_x.send(r)
        column[0:1] += jnp.sum(g, axis=0, keepdims=True)

    self_back(x_low, proj, out_w, q, k, v, mixed_t, lse, place, length[0], True, grad_low, grad_mixed, d_q, d_k, d_v, pack_a, later, small, rest)
    pair_mark = lax.broadcasted_iota(jnp.int32, (PAIRS, 1), 0) == length[2]
    small[16:] += jnp.where(pair_mark, column[0:1], 0.0)


def dec_self_back(scalars, picks, s, count, two, layer, place, saved, prev):
    proj, out_w, bias, w_in, c_in, w_out, c_out, gain, offset = layer
    x_low, q, k, v, mixed_t, lse, normed1, rstd1 = saved
    n, d = x_low.shape
    nd = (n, d)
    args = [(two, ("late", 1)), (normed1, "late"), (two, ("late", 0))]
    args += [(a, "late") for a in (out_w, mixed_t, q, k, v, x_low, proj)]
    args += [(a, "vmem") for a in (lse, rstd1, gain, place)]
    if prev:
        args.append((prev[3], "vmem"))
    outs = [(nd, F32, ("late", s, prev[0] if prev else None, count)), ((4 * d, d), BF, ("from", prev[1]) if prev else "late"), ((16 + PAIRS, d), F32, "vmem")]
    scratch = [(nd, F32)] + [(nd, BF)] * 5 + [((8, d), F32)]
    return call(functools.partial(dec_self_back_kernel, bool(prev)), "decoder_self_back", scalars, picks, args, outs, scratch, 20e9)


def add_rows(target, start, size, sources):
    block = max(b for b in range(16, min(size, 96) + 1, 16) if size % b == 0)

    def body(index):
        here = pl.ds(pl.multiple_of(start + index * block, 16), block)
        value = 0.0
        for ref, begin in sources:
            value = value + ref[pl.ds(pl.multiple_of(begin + index * block, 16), block)].astype(F32)
        target[here] = value.astype(BF)

    loop(size // block, body)


class Ring:
    def __init__(self, count):
        self.m = m = count // 2
        self.me = lax.axis_index("dp")
        self.core = self.me % 2
        chip = self.me // 2
        turn = (chip // 2) * (1 - chip % 2) + (m - 1 - chip // 2) * (chip % 2)
        back = (m - turn) % m
        self.place = turn * (1 - self.core) + back * self.core
        self.place_other = turn * self.core + back * (1 - self.core)
        self.other = self.me + 1 - 2 * self.core
        self.after = self.device(self.place + 1, self.core)
        self.before = self.device(self.place + m - 1, self.core)

    def device(self, place, core):
        m = self.m
        place = place % m
        turn = place * (1 - core) + ((m - place) % m) * core
        odd = turn // (m // 2)
        return 2 * (2 * (turn * (1 - odd) + (m - 1 - turn) * odd) + odd) + core


def rows_of(ref, start, size):
    return ref.at[pl.ds(pl.multiple_of(start, 16), size)]


class Copies:
    def __init__(self, send_sem, recv_sem):
        self.send_sem, self.recv_sem, self.used = send_sem, recv_sem, 0

    def remote(self, src, dst, device):
        index = self.used
        self.used += 1
        return pltpu.make_async_remote_copy(
            src, dst, self.send_sem.at[index], self.recv_sem.at[index], device_id=device, device_id_type=MESH
        )


def halves(size):
    first = size // 32 * 16
    return [(0, first), (first, size - first)] if first else [(0, size)]


def reduce_kernel(count, shares, a, b, own, out, work, inbox, pairbox, load_sem, send_sem, recv_sem):
    ring = Ring(count)
    m, core, place = ring.m, ring.core, ring.place
    section = lax.axis_index("section")
    na, nb, width = a.shape[0], b.shape[0], a.shape[1]
    bases = (0, count * shares[0], count * (shares[0] + shares[1]))
    starts = (0, shares[0], shares[0] + shares[1])
    loads = [
        pltpu.make_async_copy(a, work.at[pl.ds(0, na)], load_sem.at[0]),
        pltpu.make_async_copy(b, work.at[pl.ds(bases[1], nb)], load_sem.at[1]),
    ]
    for copy in loads:
        copy.start()
    barrier = pltpu.get_barrier_semaphore()
    for device in (ring.after, ring.before, ring.other):
        pl.semaphore_signal(barrier, inc=1, device_id={"dp": device}, device_id_type=MESH)
    blank = jnp.zeros((count * shares[2] - own.shape[0], width), F32)
    work[bases[2] : bases[2] + count * shares[2]] = jnp.concatenate([own[16:32], own[0:16], blank]).astype(BF)
    for copy in loads:
        copy.wait()
    pl.semaphore_wait(barrier, 3)
    copies = Copies(send_sem, recv_sem)
    units = [(region, offset, size) for region in range(3) for offset, size in halves(shares[region])]
    boxes, total = [], 0
    for _, _, size in units:
        boxes.append(total)
        total += size

    def where(region, action):
        if region == 1:
            pl.when(section == 0)(action)
        else:
            action()

    near, far = m // 2, m - 1 - m // 2

    def order(place):
        chunks = []
        for s in range(near):
            chunks.append(place + near - s)
            if s < far:
                chunks.append(place + 2 * m - far + s)
        return chunks + [place + m]

    pairs = []
    for t, chunk in enumerate(order(ring.place_other)):
        owner = ring.device(chunk, 1 - core)
        row = []
        for region in range(3):
            size = shares[region]
            row.append(
                copies.remote(
                    rows_of(work, bases[region] + owner * size, size),
                    pairbox.at[pl.ds(t * sum(shares) + starts[region], size)],
                    {"dp": ring.other},
                )
            )
            where(region, row[region].start)
        pairs.append(row)
    slots = [(s, way) for s in range(near) for way in range(2) if way == 0 or s < far]
    box_of = {slot: i for i, slot in enumerate(slots)}
    sends = {}
    for t, chunk in enumerate(order(place)):
        s, way = slots[t] if t < m - 1 else (None, None)
        owner = ring.device(chunk, core)
        for region in range(3):
            where(region, pairs[t][region].wait_recv)
        for u, (region, offset, size) in enumerate(units):
            start = bases[region] + owner * shares[region] + offset
            if s is None:
                before = [(near - 1, 0), (far - 1, 1)] if far else [(near - 1, 0)]
            else:
                before = [(s - 1, way)] if s else []
                target = ring.after if way == 0 else ring.before
                box = box_of[(s, way)] * total + boxes[u]
                sends[(s, way, u)] = copies.remote(rows_of(work, start, size), inbox.at[pl.ds(box, size)], {"dp": target})

            def step(t=t, s=s, way=way, u=u, region=region, offset=offset, size=size, start=start, before=before):
                sources = [(work, start), (pairbox, t * sum(shares) + starts[region] + offset)]
                for slot in before:
                    sends[(*slot, u)].wait_recv()
                    sources.append((inbox, box_of[slot] * total + boxes[u]))
                if s is None:
                    add_rows(out, starts[region] + offset, size, sources)
                else:
                    add_rows(work, start, size, sources)
                    sends[(s, way, u)].start()

            where(region, step)
    for row in pairs:
        for region in range(3):
            where(region, row[region].wait_send)
    for (s, way, u), copy in sends.items():
        where(units[u][0], copy.wait_send)


def reduce_grads(count, shares, a, b, own):
    d = a.shape[1]
    m = count // 2
    width = sum(shares)
    units = sum(len(halves(s)) for s in shares)
    slots = (m - 1) * units + m * 3
    anywhere = pl.BlockSpec(memory_space=pl.ANY)
    inside = pl.BlockSpec(memory_space=pltpu.VMEM)
    return pl.pallas_call(
        functools.partial(reduce_kernel, count, shares),
        name="gradient_reduce",
        out_shape=sds((width, d), BF),
        in_specs=[anywhere] * 2 + [inside],
        out_specs=inside,
        scratch_shapes=[
            vm((count * width, d), BF),
            vm(((m - 1) * width, d), BF),
            vm((m * width, d), BF),
            pltpu.SemaphoreType.DMA((2,)),
            pltpu.SemaphoreType.DMA((slots,)),
            pltpu.SemaphoreType.DMA((slots,)),
        ],
        compiler_params=pltpu.CompilerParams(collective_id=0, has_side_effects=True, vmem_limit_bytes=48 * 2**20),
    )(a, b, own)


def gather_kernel(count, shares, mine, theirs, own, shown, out, shown_far, final, out_sem, send_sem, recv_sem):
    ring = Ring(count)
    m, core, place = ring.m, ring.core, ring.place
    section = lax.axis_index("section")
    decoder = section == 1
    barrier = pltpu.get_barrier_semaphore()
    for device in (ring.after, ring.before, ring.other):
        pl.semaphore_signal(barrier, inc=1, device_id={"dp": device}, device_id_type=MESH)
    pl.semaphore_signal(barrier, inc=1, device_id={"section": 1 - section}, device_id_type=MESH)
    bases = [0]
    for share in shares:
        bases.append(bases[-1] + count * share)
    s0, s1, s2, s3 = shares
    me = ring.me
    split = s2 % 32 == 0
    half = s2 // 2 if split else s2
    near_half = section * half if split else 0
    far_half = half - near_half

    def low(region, place, core):
        return bases[region] + ring.device(place, core) * shares[region]

    def part(region, place, core):
        start = low(region, place, core)
        return (start + near_half, half) if region == 2 else (start, shares[region])

    def here(region):
        return pl.ds(pl.multiple_of(low(region, place, core), 16), shares[region])

    final[here(0)] = own[0:s0]
    final[here(2)] = (mine[s1 : s1 + s2].astype(F32) + theirs[s1 : s1 + s2].astype(F32)).astype(BF)

    @pl.when(decoder)
    def _():
        final[here(1)] = (mine[0:s1].astype(F32) + theirs[0:s1].astype(F32)).astype(BF)

    @pl.when(section == 0)
    def _():
        final[here(1)] = own[s0 : s0 + s1]

    @pl.when(me == 2)
    def _():
        final[here(3)] = (mine[s1 + s2 :].astype(F32) + theirs[s1 + s2 :].astype(F32)).astype(BF)

    @pl.when((me != 2) & ((me != 0) | decoder))
    def _():
        final[here(3)] = own[s0 + s1 :]

    pl.semaphore_wait(barrier, 4)
    copies = Copies(send_sem, recv_sem)
    pair = rows_of(final, low(3, place, core), s3)
    across = copies.remote(pair, pair, {"section": 1 - section})
    pl.when(decoder & (me == 0))(across.start)
    hand = copies.remote(shown, shown_far, {"section": 1 - section})
    pl.when(section == 0)(hand.start)
    near, far = m // 2, m - 1 - m // 2
    passes, shared, arrived, crossed, waiting = {}, [], [], [], []

    def keep(start, size):
        rows = pl.ds(pl.multiple_of(start, 16), size)
        pltpu.make_async_copy(final.at[rows], out.at[rows], out_sem.at[0]).start()

    def give(start, size, far_start):
        block = rows_of(final, start, size)
        shared.append(copies.remote(block, block, {"dp": ring.other}))
        shared[-1].start()
        keep(start, size)
        arrived.append((far_start, size))

    def take_crossed():
        while waiting:
            copy, shift = waiting.pop(0)
            copy.wait_recv()
            give(low(2, place + shift, core) + far_half, half, low(2, ring.place_other + shift, 1 - core) + far_half)

    for s in range(near + 1):
        fresh = []
        for way in range(2):
            if (way == 1 and s > far) or (s == 0 and way == 1 and not far):
                continue
            shift = 2 * m - s if way == 0 else s
            limit, target = (near, ring.after) if way == 0 else (far, ring.before)
            for region in range(4):
                start, size = part(region, place + shift, core)
                block = rows_of(final, start, size)
                if s:
                    passes[(s - 1, way, region)].wait_recv()
                elif region == 3 and way == 0:
                    pl.when((section == 0) & (me == 0))(across.wait_recv)
                if s < limit:
                    passes[(s, way, region)] = copies.remote(block, block, {"dp": target})
                    passes[(s, way, region)].start()
                if s:
                    if region == 2 and split:
                        crossed.append(copies.remote(block, block, {"section": 1 - section}))
                        crossed[-1].start()
                        fresh.append((crossed[-1], shift))
                    give(start, size, part(region, ring.place_other + shift, 1 - core)[0])
                elif way == 0:
                    give(low(region, place, core), shares[region], low(region, ring.place_other, 1 - core))
        take_crossed()
        waiting.extend(fresh)
    take_crossed()
    for copy, (start, size) in zip(shared, arrived):
        copy.wait_recv()
        keep(start, size)
    for copy in [*passes.values(), *shared, *crossed]:
        copy.wait_send()
    pl.when(decoder & (me == 0))(across.wait_send)
    pl.when(section == 0)(hand.wait_send)
    pl.when(decoder)(hand.wait_recv)
    pltpu.make_async_copy(final, out, out_sem.at[0]).wait()


def gather_grads(count, shares, mine, theirs, own, shown):
    d = own.shape[1]
    m = count // 2
    rows = count * sum(shares)
    slots = (2 * m - 1) * 4 + 2 + 2 * (m - 1)
    inside = pl.BlockSpec(memory_space=pltpu.VMEM)
    return pl.pallas_call(
        functools.partial(gather_kernel, count, shares),
        name="gradient_gather",
        out_shape=[sds((rows, d), BF), sds(shown.shape, BF)],
        in_specs=[inside] * 3 + [pl.BlockSpec(memory_space=pl.ANY)],
        out_specs=[pl.BlockSpec(memory_space=pl.ANY)] * 2,
        scratch_shapes=[
            vm((rows, d), BF),
            pltpu.SemaphoreType.DMA((1,)),
            pltpu.SemaphoreType.DMA((slots,)),
            pltpu.SemaphoreType.DMA((slots,)),
        ],
        compiler_params=pltpu.CompilerParams(collective_id=1, has_side_effects=True, vmem_limit_bytes=48 * 2**20),
    )(mine, theirs, own, shown)


def unpack_kernel(
    bases, f, pack_ref, shown_e, shown_t, shown_far,
    proj, out_w, bias, w_in, b_in, w_out, b_out, gain, offset, c_proj, c_out, c_bias, c_gain, c_offset, pair, shown,
    pack, f_proj, f_out, f_in, f_w_out, f_cproj, f_cout, rows_shown, in_sem, out_sem, shown_sem,
):
    d = pack_ref.shape[1]
    own_b, own_c, own_p = bases
    section = lax.axis_index("section")
    leave = pltpu.make_async_copy(rows_shown, shown, shown_sem.at[0])
    far = [
        pltpu.make_async_copy(shown_t, rows_shown.at[0], shown_sem.at[0]),
        pltpu.make_async_copy(shown_far, rows_shown.at[1], shown_sem.at[1]),
    ]
    spans = [(0, own_b), (own_b, own_b + f), (own_b + f, own_c), (own_c, pack.shape[0])]
    loads = []
    for i, (begin, end) in enumerate(spans):
        rows = pl.ds(begin, end - begin)
        loads.append(pltpu.make_async_copy(pack_ref.at[rows], pack.at[rows], in_sem.at[i]))
        loads[-1].start()

    @pl.when(section == 1)
    def _():
        far[0].start()
        far[1].start()

    leaving = []

    def send(held, out):
        leaving.append(pltpu.make_async_copy(held, out, out_sem.at[len(leaving)]))
        leaving[-1].start()

    loads[0].wait()
    f_proj[...] = pack[0 : 3 * d].astype(F32)
    send(f_proj, proj)
    f_out[...] = pack[3 * d : 4 * d].astype(F32)
    send(f_out, out_w)
    loads[1].wait()
    for c in range(f // d):
        f_in[:, c * d : (c + 1) * d] = pack[own_b + c * d : own_b + (c + 1) * d].astype(F32)
    send(f_in, w_in)
    loads[2].wait()
    f_w_out[...] = pack[own_b + f : own_b + 2 * f].astype(F32)
    send(f_w_out, w_out)
    loads[3].wait()

    @pl.when(section == 1)
    def _():
        far[0].wait()
        far[1].wait()
        leave.start()

    f_cproj[...] = pack[own_c : own_c + 3 * d].astype(F32)
    send(f_cproj, c_proj)
    f_cout[...] = pack[own_c + 3 * d : own_c + 4 * d].astype(F32)
    send(f_cout, c_out)
    small = pack[own_p + 16 : own_p + 32].astype(F32)
    middle = pack[own_p + 32 : own_p + 48].astype(F32)
    bias[...] = small[0:3]
    row = lax.broadcasted_iota(jnp.int32, (16, 1), 0)
    moved = (section == 1) & (row >= 3) & (row <= 11) & (row != 8) & (row != 10)
    small = jnp.where(moved, middle, small)
    for c in range(f // d):
        b_in[:, c * d : (c + 1) * d] = small[3 + c : 4 + c]
    b_out[...] = small[7:8]
    gain[...] = small[8:10]
    offset[...] = small[10:12]
    c_bias[...] = middle[0:3]
    c_gain[...] = middle[8:9]
    c_offset[...] = middle[10:11]
    pair[...] = pack[own_p : own_p + 16].astype(F32)[0 : pair.shape[0]]
    for copy in leaving:
        copy.wait()
    pl.when(section == 1)(leave.wait)


def unpack(pack, bases, f, shown_e, shown_t, shown_far):
    d = pack.shape[1]
    inside = pl.BlockSpec(memory_space=pltpu.VMEM)
    anywhere = pl.BlockSpec(memory_space=pl.ANY)
    shapes = [(3 * d, d), (d, d), (3, d), (d, f), (1, f), (f, d), (1, d), (2, d), (2, d), (3 * d, d), (d, d), (3, d), (1, d), (1, d), (PAIRS, d)]
    large = (0, 1, 3, 5, 9, 10)
    return pl.pallas_call(
        functools.partial(unpack_kernel, bases, f),
        name="unpack",
        out_shape=[sds(s, F32) for s in shapes] + [sds(shown_e.shape, BF)],
        in_specs=[anywhere] * 4,
        out_specs=[anywhere if i in large else inside for i in range(len(shapes))] + [anywhere],
        input_output_aliases={1: len(shapes)},
        scratch_shapes=[vm(pack.shape, BF)] + [vm(shapes[i], F32) for i in large]
        + [vm(shown_e.shape, BF), pltpu.SemaphoreType.DMA((4,)), pltpu.SemaphoreType.DMA((6,)), pltpu.SemaphoreType.DMA((2,))],
        compiler_params=pltpu.CompilerParams(vmem_limit_bytes=50 * 2**20),
    )(pack, shown_e, shown_t, shown_far)


def nothing(*refs):
    pass


def blank(*shapes):
    spec = pl.BlockSpec(memory_space=pl.ANY)
    return pl.pallas_call(nothing, name="blank", out_shape=[sds(*s) for s in shapes], out_specs=[spec] * len(shapes))()


def per_device(
    embeds, cotangent, pair_ids, seq_lengths, alive_count,
    self_proj, self_out, self_bias, ffn_in, ffn_in_bias, ffn_out, ffn_out_bias, norm_gain, norm_bias,
    cross_proj, cross_out, cross_bias, cross_norm_gain, cross_norm_bias, pair_embed,
):
    layer = (self_proj[0], self_out[0], self_bias[0], ffn_in[0], ffn_in_bias, ffn_out[0], ffn_out_bias, norm_gain[0], norm_bias[0])
    cross = (cross_proj, cross_out, cross_bias, cross_norm_gain[None], cross_norm_bias[None])
    place = jnp.asarray(place_matrix(), BF)
    section_zero = lax.axis_index("section") == 0
    section_one = lax.axis_index("section") == 1
    devices = lax.axis_size("dp")
    x, cot = embeds[0], cotangent[0]
    count, n, d = x.shape
    f = ffn_in.shape[2]
    live = (jnp.arange(count) < alive_count[0])[None, :]
    numbers = jnp.concatenate([seq_lengths.reshape(-1), jnp.where(live, seq_lengths, 0).reshape(-1), pair_ids])
    src = [(s, 2 * count + s, 4 * count + s) for s in range(count)]
    tgt = [(count + s, 3 * count + s, 4 * count + s) for s in range(count)]
    mid = [(s, 3 * count + s, 4 * count + s) for s in range(count)]
    nd, nf, n1 = (n, d), (n, f), (n, 1)
    ahead, behind, both = [(0, 1)], [(1, 0)], [(0, 1), (1, 0)]

    def move(value, way):
        return lax.ppermute(value, "section", way)

    def pick(received, own):
        return jnp.where(section_zero, received, own)

    part = f // devices
    start = lax.axis_index("dp") * part
    share = jnp.concatenate([
        lax.dynamic_slice_in_dim(ffn_in[0], start, part, 1).T, lax.dynamic_slice_in_dim(ffn_out[0], start, part, 0)
    ])
    share, bias_in = lax.optimization_barrier((share, ffn_in_bias))
    vectors = jnp.concatenate([bias_in[:, i : i + d] for i in range(0, f, d)] + [ffn_out_bias, norm_gain[0], norm_bias[0]])
    x, far_share, far_vectors, x_late, cot_late = lax.optimization_barrier(
        (x, move(share, behind), move(vectors, behind), x[1:], cot[1:])
    )
    far_x = move(x_late, behind)
    weights = lax.all_gather(pick(far_share, share), "dp", axis=0, tiled=True)
    vectors = pick(far_vectors, vectors)

    def first(e, t, shown):
        def enc():
            memory, shown_e, q, k, v, mt, lse, na, ra, act, slope, nb, rb = enc_forward(numbers, src[e], x, e, layer, shown)
            return memory, shown_e, q, k, v, mt, lse, ra, na, act, slope, nb, rb

        def dec():
            low, q, k, v, mt, lse, na, ra = dec_self(numbers, tgt[t], x, t, pair_embed, layer)
            shown_e, act, slope, nb, rb = blank(((count, *nd), BF), (nf, BF), (nf, BF), (nd, BF), (n1, F32))
            return na, shown_e, q, k, v, mt, lse, ra, low, act, slope, nb, rb

        return lax.cond(section_zero, enc, dec) if shown is None else lax.cond(section_one, dec, enc)

    def last(e, t, saved_e, d_memory, grads, saved_t, prev):
        def enc():
            _, _, q, k, v, mt, lse, ra, na, act, slope, nb, rb = saved_e
            return tuple(enc_back(numbers, src[e], x, e, d_memory, cot, layer, place, (q, k, v, mt, lse, na, ra, act, slope, nb, rb), prev))

        def dec():
            na, _, q, k, v, mt, lse, ra, low, _, _, _, _ = saved_t
            d_x, pack_a, small = dec_self_back(
                numbers, tgt[t], t, count, grads, layer, place, (low, q, k, v, mt, lse, na, ra), prev
            )
            return d_x, pack_a, blank(((2 * f, d), BF))[0], small

        return lax.cond(section_one, dec, enc) if prev else lax.cond(section_zero, enc, dec)

    saved = [first(0, 1, None)]
    swapped = move(saved[0][0], both)
    near_first, cot_late = lax.optimization_barrier((saved[0][0], cot_late))
    far_cot = move(cot_late, behind)
    x, far_x = lax.optimization_barrier((x, far_x))
    saved.append(first(1, 0, saved[0][1]))
    normed = (swapped, saved[1][0])
    memory = (saved[1][0], swapped)
    crossed = dec_cross(numbers, (mid[1], mid[0]), normed, memory, vectors, cross)
    shown, two, d_memory, pack = dec_mid(
        numbers, (mid[1], mid[0]), ((far_x, 0), (x, 0)), ((far_cot, 0), (cot, 0)), normed, memory, crossed,
        pair_embed, weights, vectors, cross, place, devices,
    )
    near_d_memory = move(d_memory, behind)
    far_two = move(two, ahead)
    mine = lax.psum_scatter(pack, "dp", scatter_dimension=0, tiled=True)
    grads = last(1, 0, saved[1], d_memory, two, saved[1], ())
    grads = last(0, 1, saved[0], near_d_memory, far_two, saved[0], grads)
    mine, pack_a = lax.optimization_barrier((mine, grads[1]))
    theirs = move(mine, both)
    shares = (padded(4 * d, devices) // devices, 2 * f // devices, cross_rows(devices, d) // devices, 16)
    own = reduce_grads(devices, (shares[0], shares[1], shares[3]), pack_a, grads[2], grads[3])
    pack, far_shown = gather_grads(devices, shares, mine, theirs, own, shown)
    bases = [devices * sum(shares[:i]) for i in (1, 2, 3)]
    proj, out_w, bias, w_in, b_in, w_out, b_out, gain, offset, c_proj, c_out, c_bias, c_gain, c_offset, pair, shown = unpack(pack, bases, f, saved[1][1], shown, far_shown)
    return (
        shown[None], grads[0][None], proj.reshape(1, 3, d, d), out_w[None], bias[None], w_in[None], b_in, w_out[None], b_out, gain[None], offset[None],
        c_proj.reshape(3, d, d), c_out, c_bias, c_gain[0], c_offset[0], pair,
    )


def solution(mesh):
    s, r = "section", P()
    in_specs = (
        P(s, "dp"), P(s, "dp"), P("dp"), P(None, "dp"), P("dp"),
        P(s), P(s), P(s), P(s), P(s), P(s), P(s), P(s), P(s), r, r, r, r, r, r,
    )
    out_specs = (P(s, "dp"), P(s, "dp"), P(s), P(s), P(s), P(s), P(s), P(s), P(s), P(s), P(s), r, r, r, r, r, r)
    return jax.shard_map(per_device, mesh=mesh, in_specs=in_specs, out_specs=out_specs, check_vma=False)
```
